32 devices in a mesh: segment: 4 (over z), dp: 8 (over y, x, core).
Axes of the slice: x: 2, y: 2, z: 4, core: 2. Of those that a mesh axis runs over, the one named last changes fastest.
Arguments:
- tokens: bfloat16 [8192, 512], P(('segment', 'dp')), may hold values from -6 to 6
- lengths: int32 [4, 8], P(None, 'dp'), may hold values from 1 to 256, as said below
- cotangent: bfloat16 [8192, 512], P(('segment', 'dp')), may hold values from -6 to 6
- main_weight: bfloat16 [4, 512, 2048], P('segment')
- side_weight: bfloat16 [4, 512, 1024], P('segment'), may hold values from -0.1875 to 0.1875
- in_bias: bfloat16 [4, 1536], P('segment'), may hold values from -1.5 to 1.5
- out_bias: bfloat16 [4, 512], P('segment'), may hold values from -1.5 to 1.5
- norm_gain: bfloat16 [4, 512], P('segment'), may hold values from 0.5 to 1.5
- norm_shift: bfloat16 [4, 512], P('segment'), may hold values from -1.5 to 1.5
Outputs:
- outputs: bfloat16 [8192, 512], P(('segment', 'dp'))
- input_grad: bfloat16 [8192, 512], P(('segment', 'dp'))
- main_grad: float32 [4, 512, 2048], P('segment')
- side_grad: float32 [4, 512, 1024], P('segment')
- in_bias_grad: float32 [4, 1536], P('segment')
- out_bias_grad: float32 [4, 512], P('segment')
- gain_grad: float32 [4, 512], P('segment')
- shift_grad: float32 [4, 512], P('segment')
- stats: float32 [4, 2], P('segment')
The draws below stay inside these ranges and needn't reach their ends.
Inputs may be any that keep to these rules, and one draw needn't show every extreme that they name: `lengths`: both 1 and 256 occur.
All inputs are finite; a program needn't handle non-finite values.
Results may differ from the reference program's by a relative error of at most 0.03.
Values may be sent and summed in bfloat16 or wider, within the bound.
No kernel may reach another device: no remote copies, remote signals or barrier semaphores. Data moves between devices by JAX's collectives and lax.ppermute only.
A program may use at most 256 MiB of HBM per device.

```python
import jax
import jax.numpy as jnp
from jax import lax

D = 512
FF = 2048
HEADS = 8
SEQ = 256
SEQ_DEV = 1
SEGMENTS = 4
SHARDS = 8
TOKENS = 8192


def draw_lengths(key, part):
    key = jax.random.fold_in(key, 5)
    key_len, key_row, key_col = jax.random.split(key, 3)
    column = jnp.arange(SHARDS * SEQ_DEV) // SEQ_DEV
    ceiling = SEQ * (SHARDS - 1 + 2 * column) // (3 * (SHARDS - 1))
    spread = jax.random.randint(key_len, (SEGMENTS, SHARDS * SEQ_DEV), 0, 1 << 20)
    length_draw = ceiling[None, :] - spread % (ceiling[None, :] // 2 + 1)
    row_pick = jax.random.randint(key_row, (), 0, SEGMENTS)
    col_pick = jax.random.randint(key_col, (), 0, SHARDS * SEQ_DEV)
    length_draw = length_draw.at[row_pick, col_pick].set(SEQ)
    length_draw = length_draw.at[(row_pick + 1) % SEGMENTS, col_pick].set(1)
    return length_draw.astype(jnp.int32)


def draw_main_weight(key, part):
    key = jax.random.fold_in(key, 9)
    column = jnp.arange(FF)[None, None, :]
    is_attend = (jnp.arange(SEGMENTS) % 2 == 0)[:, None, None]
    factor = jnp.where(is_attend & (column < 2 * D), 1.25, 1.0)
    factor = jnp.where(is_attend & (column >= 3 * D), 32.0 ** 0.5, factor)
    normal_draw = jax.random.normal(key, (SEGMENTS, D, FF), jnp.float32)
    return (normal_draw * factor * D ** (-0.5)).astype(jnp.bfloat16)


def levels(own_key, dims, pieces, smallest, high):
    def one(position, shards_of):
        draws = jax.random.uniform(jax.random.fold_in(jax.random.fold_in(own_key, 6), position), (shards_of,), jnp.float32, smallest / len(pieces), high / len(pieces))
        return jnp.repeat(jnp.exp(draws), dims[position] // shards_of).reshape((-1,) + (1,) * (len(dims) - position - 1))

    gain = one(*pieces[0])
    for cut in pieces[1:]:
        gain = gain * one(*cut)
    return gain


def gaussian(rng, shape, width, bound, pieces=(), held_as=jnp.bfloat16):
    values = width * jax.random.normal(rng, shape, jnp.float32)
    if pieces:
        values = values * levels(rng, shape, pieces, -0.22, 0.18)
    return jnp.clip(values, -bound, bound).astype(held_as)


def setup_inputs(seed: int = 0) -> dict:
    streams_of = jax.random.split(jax.random.key(seed), 10)
    return {
        "tokens": gaussian(streams_of[0], (TOKENS, D), 1.0, 6.0, ((0, 32),)),
        "lengths": draw_lengths(jax.random.fold_in(streams_of[9], 71), 0),
        "cotangent": gaussian(streams_of[2], (TOKENS, D), 1.0, 6.0, ((0, 32),)),
        "main_weight": draw_main_weight(jax.random.fold_in(streams_of[9], 71), 0),
        "side_weight": gaussian(streams_of[4], (SEGMENTS, D, FF // 2), (FF // 2) ** -0.5, 0.1875, ((0, 4),)),
        "in_bias": gaussian(streams_of[5], (SEGMENTS, 3 * D), 0.3, 1.5, ((0, 4),)),
        "out_bias": gaussian(streams_of[6], (SEGMENTS, D), 0.3, 1.5, ((0, 4),)),
        "norm_gain": jnp.clip(1.0 + 0.1 * jax.random.normal(streams_of[7], (SEGMENTS, D), jnp.float32), 0.5, 1.5).astype(jnp.bfloat16),
        "norm_shift": gaussian(streams_of[8], (SEGMENTS, D), 0.3, 1.5, ((0, 4),)),
    }


@jax.custom_vjp
def low(v):
    return lax.optimization_barrier(v.astype(jnp.bfloat16)).astype(jnp.float32)

@jax.custom_vjp
def low_back(v):
    return v

def low_keep(v):
    return (low(v), None)

def low_pass(kept, grad):
    return (grad,)

def back_keep(v):
    return (v, None)

def back_low(kept, grad):
    return (low(grad),)
low.defvjp(low_keep, low_pass)
low_back.defvjp(back_keep, back_low)
eps = 1e-05

def matmul(left, right):
    return jnp.dot(left, right, precision=lax.Precision.HIGHEST)

def post_norm(residual, gain_vec, shift_vec):
    row_mean = lax.optimization_barrier(jnp.mean(residual, axis=-1, keepdims=True))
    centred = residual - row_mean
    row_var = lax.optimization_barrier(jnp.mean(centred * centred, axis=-1, keepdims=True))
    return centred * lax.rsqrt(row_var + eps) * gain_vec + shift_vec

def attend(flat_rows, seq_lens, main_mat, bias_in, bias_out):
    seq_count = seq_lens.shape[0]
    seq_len = flat_rows.shape[0] // seq_count
    model_width = flat_rows.shape[1]
    head_size = model_width // HEADS
    projected = matmul(flat_rows, main_mat[:, :3 * model_width])
    queries = low_back(low(projected[:, :model_width] + bias_in[:model_width]))
    key_rows = low_back(low(projected[:, model_width:2 * model_width]))
    values = low_back(low(projected[:, 2 * model_width:] + bias_in[model_width:2 * model_width]))
    shape_heads = (seq_count, seq_len, HEADS, head_size)
    scores = jnp.einsum('bqhe,bkhe->bhqk', queries.reshape(shape_heads), key_rows.reshape(shape_heads), precision=lax.Precision.HIGHEST) * head_size ** (-0.5)
    key_live = jnp.arange(seq_len)[None, None, None, :] < seq_lens[:, None, None, None]
    scores = low_back(jnp.where(key_live, scores, -1e+30))
    row_max = lax.optimization_barrier(jnp.max(scores, axis=-1, keepdims=True))
    exponent = jnp.exp(scores - row_max)
    probability = exponent / lax.optimization_barrier(jnp.sum(exponent, axis=-1, keepdims=True))
    context = jnp.einsum('bhqk,bkhe->bqhe', low(probability), values.reshape(shape_heads), precision=lax.Precision.HIGHEST)
    context = low_back(low(context.reshape(seq_count * seq_len, model_width)))
    return low_back(matmul(context, main_mat[:, 3 * model_width:]) + bias_out)

def feed_forward(flat_rows, main_mat, down_t, bias_in, bias_out):
    pre_act = low_back(matmul(flat_rows, main_mat) + bias_in)
    hidden = low(jax.nn.gelu(pre_act, approximate=True))
    projected = lax.dot_general(hidden, down_t, (((1,), (1,)), ((), ())), precision=lax.Precision.HIGHEST)
    return low_back(projected + bias_out)

def group_pass(param_set, flat_rows, seq_lens):
    main_all, side_all, bias_ins, bias_outs, gains_all, shifts_all = param_set
    model_width = flat_rows.shape[1]
    seq_len = flat_rows.shape[0] // seq_lens.shape[0]
    row_live = (jnp.arange(seq_len)[None, :] < seq_lens[:, None]).reshape(-1, 1).astype(flat_rows.dtype)
    activation = flat_rows
    square_list = []
    for segment_at in range(4):
        if segment_at % 2 == 0:
            branch = attend(activation, seq_lens, main_all[segment_at], bias_ins[segment_at], bias_outs[segment_at])
        else:
            down_t = jnp.concatenate([side_all[segment_at - 1], side_all[segment_at]], axis=1)
            bias_first = jnp.concatenate([bias_ins[segment_at - 1][2 * model_width:], bias_ins[segment_at]])
            branch = feed_forward(activation, main_all[segment_at], down_t, bias_first, bias_outs[segment_at])
        residual = activation + branch
        square_list.append(jnp.stack([jnp.sum(row_live * residual * residual), jnp.sum(row_live * branch * branch)]))
        normed_out = post_norm(residual, gains_all[segment_at], shifts_all[segment_at])
        activation = low_back(low(normed_out)) if segment_at < 3 else low(normed_out)
    return (activation, jnp.stack(square_list))

def reference(tokens, lengths, cotangent, main_weight, side_weight, in_bias, out_bias, norm_gain, norm_shift):
    params = (main_weight.astype(jnp.float32), side_weight.astype(jnp.float32), in_bias.astype(jnp.float32), out_bias.astype(jnp.float32), norm_gain.astype(jnp.float32), norm_shift.astype(jnp.float32))
    group_seqs = SEQ_DEV * SEGMENTS
    seq_groups = lengths.reshape(-1, group_seqs)

    def forward(param_set, token_rows):
        grouped = low_back(token_rows).reshape(-1, group_seqs * SEQ, D)

        def one_group(group_item):
            return group_pass(param_set, group_item[0], group_item[1])
        outs_grouped, squares = lax.map(jax.checkpoint(one_group), (grouped, seq_groups))
        return (outs_grouped.reshape(-1, D), lax.optimization_barrier(jnp.sum(squares, axis=0)))
    outputs, pull_back, square_sums = jax.vjp(forward, params, tokens.astype(jnp.float32), has_aux=True)
    param_grads, input_grad = pull_back(cotangent.astype(jnp.float32))
    token_total = jnp.sum(lengths).astype(jnp.float32)
    stats = jnp.sqrt(square_sums / (token_total * D))
    return (outputs.astype(jnp.bfloat16), input_grad.astype(jnp.bfloat16), param_grads[0], param_grads[1], param_grads[2], param_grads[3], param_grads[4], param_grads[5], stats)
```

```python
import jax
import jax.numpy as jnp
from jax import lax
from jax.experimental import pallas as pl
from jax.experimental.pallas import tpu as pltpu
from jax.sharding import PartitionSpec as P

HEADS = 8
EPS = 1e-05
VMEM_LIMIT = 48 * 1024 * 1024
F32 = jnp.float32
BF16 = jnp.bfloat16
GELU_IN = 0.7978845608028654
GELU_CUBE = 0.044715 * GELU_IN


def dot_nn(left, right):
    return jnp.dot(left, right, preferred_element_type=F32)


def dot_nt(left, right):
    return lax.dot_general(left, right, (((1,), (1,)), ((), ())), preferred_element_type=F32)


def kernel_call(body, where, meta, order, ins, outs, scratch, copies):
    n_in, n_out = len(ins), len(outs)

    def kernel(meta_ref, *refs):
        in_refs = refs[:n_in]
        out_refs = refs[n_in + 1 : n_in + 1 + n_out]
        rest = refs[n_in + 2 + n_out :]
        sems = rest[-1]

        def run():
            body(meta_ref, in_refs, out_refs, rest[:-1], sems)

        if where is None:
            run()
        else:
            here = meta_ref[0] == where[0]
            for other in where[1:]:
                here = here | (meta_ref[0] == other)
            pl.when(here)(run)

    anywhere = pl.BlockSpec(memory_space=pl.ANY)
    results = pl.pallas_call(
        kernel,
        out_shape=[jax.ShapeDtypeStruct(s, t) for s, t in outs]
        + [jax.ShapeDtypeStruct(order.shape, order.dtype)],
        in_specs=[pl.BlockSpec(memory_space=pltpu.SMEM)] + [anywhere] * (n_in + 1),
        out_specs=[anywhere] * (n_out + 1),
        scratch_shapes=[pltpu.VMEM(s, t) for s, t in scratch]
        + [pltpu.SemaphoreType.DMA((copies,))],
        input_output_aliases={1 + n_in: n_out},
        compiler_params=pltpu.CompilerParams(vmem_limit_bytes=VMEM_LIMIT),
        cost_estimate=pl.CostEstimate(flops=0, bytes_accessed=0, transcendentals=0),
    )(meta, *ins, order)
    return tuple(results[:n_out]), results[n_out]


class Copies:
    def __init__(self, sems):
        self.sems, self.used, self.open = sems, 0, []

    def start(self, src, dst):
        copy = pltpu.make_async_copy(src, dst, self.sems.at[self.used])
        self.used += 1
        copy.start()
        return copy

    def out(self, src, dst):
        self.open.append(self.start(src, dst))

    def finish(self):
        for copy in self.open:
            copy.wait()


def norm_forward(inputs, branch, seq_len, gain, shift):
    resid = inputs.astype(F32) + branch
    mean = jnp.mean(resid, axis=-1, keepdims=True)
    centred = resid - mean
    var = jnp.mean(centred * centred, axis=-1, keepdims=True)
    inv_std = lax.rsqrt(var + EPS)
    xhat = centred * inv_std
    row = lax.broadcasted_iota(jnp.int32, resid.shape, 0)
    live = row < seq_len
    squares = jnp.concatenate(
        [
            jnp.sum(jnp.where(live, resid * resid, 0.0), axis=0, keepdims=True),
            jnp.sum(jnp.where(live, branch * branch, 0.0), axis=0, keepdims=True),
            jnp.zeros((6, resid.shape[1]), F32),
        ],
        axis=0,
    )
    return (xhat * gain + shift).astype(BF16), xhat, inv_std, squares


def norm_backward(grad, xhat, inv_std, gain):
    grad = grad.astype(F32)
    gy = grad * gain
    first = jnp.mean(gy, axis=-1, keepdims=True)
    second = jnp.mean(gy * xhat, axis=-1, keepdims=True)
    dresid = (gy - first - xhat * second) * inv_std
    sums = jnp.concatenate(
        [
            jnp.sum(grad * xhat, axis=0, keepdims=True),
            jnp.sum(grad, axis=0, keepdims=True),
            jnp.zeros((6, grad.shape[1]), F32),
        ],
        axis=0,
    )
    return dresid, sums


def attend_forward(slot):
    def body(meta, ins, outs, scratch, sems):
        a_h, w_h, p_h = ins
        y_h, qkv_h, ctx_h, pt_h, xh_h, rs_h, sq_h = outs
        a_v, w_v, p_v, y_v, qkv_v, ctx_v, ctxt_v, vt_v, pt_v, xh_v, rs_v, sq_v = scratch
        rows, width = a_v.shape
        size = width // HEADS
        cp = Copies(sems)
        w_in = [cp.start(a_h, a_v), cp.start(p_h, p_v)]
        w_parts = [
            cp.start(w_h.at[:, i * width : (i + 1) * width], w_v.at[:, i * width : (i + 1) * width])
            for i in range(4)
        ]
        for c in w_in:
            c.wait()
        inputs = a_v[...]
        seq_len = meta[2 + slot]
        w_parts[0].wait()
        q = (dot_nn(inputs, w_v[:, :width]) + p_v[0:1, :]).astype(BF16)
        qkv_v[:, :width] = q * jnp.asarray(size**-0.5, BF16)
        w_parts[1].wait()
        qkv_v[:, width : 2 * width] = dot_nn(inputs, w_v[:, width : 2 * width]).astype(BF16)
        w_parts[2].wait()
        v = (dot_nn(inputs, w_v[:, 2 * width : 3 * width]) + p_v[2:3, :]).astype(BF16)
        qkv_v[:, 2 * width :] = v
        vt_v[...] = v.T
        cp.out(qkv_v, qkv_h)
        key_live = lax.broadcasted_iota(jnp.int32, (rows, rows), 0) < seq_len
        lane = lax.broadcasted_iota(jnp.int32, (rows, 2 * size), 1)
        for pair in range(HEADS // 2):
            cols = slice(2 * size * pair, 2 * size * (pair + 1))
            qp = qkv_v[:, cols]
            kp = qkv_v[:, width + cols.start : width + cols.stop]
            for half in range(2):
                head = 2 * pair + half
                mine = (lane >= size) if half else (lane < size)
                scores = dot_nt(jnp.where(mine, kp, jnp.zeros_like(kp)), qp)
                scores = jnp.where(key_live, scores, -1e30)
                top = jnp.max(scores, axis=0, keepdims=True)
                expo = jnp.exp(scores - top)
                total = jnp.sum(expo, axis=0, keepdims=True)
                probs = (expo * (1.0 / total)).astype(BF16)
                pt_v[head] = probs
                ctxt_v[head * size : (head + 1) * size, :] = dot_nn(
                    vt_v[head * size : (head + 1) * size, :], probs
                ).astype(BF16)
        cp.out(pt_v, pt_h)
        ctx = ctxt_v[...].T
        ctx_v[...] = ctx
        cp.out(ctx_v, ctx_h)
        w_parts[3].wait()
        branch = dot_nn(ctx, w_v[:, 3 * width :]) + p_v[4:5, :]
        y, xhat, inv_std, squares = norm_forward(
            inputs, branch, seq_len, p_v[5:6, :], p_v[6:7, :]
        )
        y_v[...] = y
        cp.out(y_v, y_h)
        xh_v[...] = xhat
        cp.out(xh_v, xh_h)
        rs_v[...] = jnp.broadcast_to(inv_std, rs_v.shape)
        cp.out(rs_v, rs_h)
        sq_v[...] = squares
        cp.out(sq_v, sq_h)
        cp.finish()

    return body


def feed_hidden(inputs, w_v, v_v, p_v, keep_hidden, keep_slope):
    width = inputs.shape[1]
    branch = None
    for c in range(w_v.shape[1] // width):
        cols = slice(c * width, (c + 1) * width)
        x = dot_nn(inputs, w_v[:, cols]) + p_v[c : c + 1, :]
        square = x * x
        t = jnp.tanh(x * (GELU_IN + GELU_CUBE * square))
        s = 0.5 + 0.5 * t
        act = x * s
        slope = s + act * (1.0 - t) * (GELU_IN + (3.0 * GELU_CUBE) * square)
        hidden = act.astype(BF16)
        keep_hidden[:, cols] = hidden
        keep_slope[:, cols] = slope.astype(BF16)
        part = dot_nt(hidden, v_v[:, cols])
        branch = part if branch is None else branch + part
    return branch + p_v[4:5, :]


def feed_forward(slot):
    def body(meta, ins, outs, scratch, sems):
        a_h, w_h, v_h, p_h = ins
        y_h, hid_h, slope_h, xh_h, rs_h, sq_h = outs
        a_v, w_v, v_v, p_v, y_v, hid_v, slope_v, xh_v, rs_v, sq_v = scratch
        cp = Copies(sems)
        for c in [
            cp.start(a_h, a_v),
            cp.start(p_h, p_v),
            cp.start(w_h, w_v),
            cp.start(v_h, v_v),
        ]:
            c.wait()
        inputs = a_v[...]
        branch = feed_hidden(inputs, w_v, v_v, p_v, hid_v, slope_v)
        cp.out(hid_v, hid_h)
        cp.out(slope_v, slope_h)
        y, xhat, inv_std, squares = norm_forward(
            inputs, branch, meta[2 + slot], p_v[5:6, :], p_v[6:7, :]
        )
        y_v[...] = y
        cp.out(y_v, y_h)
        xh_v[...] = xhat
        cp.out(xh_v, xh_h)
        rs_v[...] = jnp.broadcast_to(inv_std, rs_v.shape)
        cp.out(rs_v, rs_h)
        sq_v[...] = squares
        cp.out(sq_v, sq_h)
        cp.finish()

    return body


def feed_backward_values(dresid, w_v, v_v, slope_v, dpre_v):
    width = dresid.shape[1]
    dbranch = dresid.astype(BF16)
    total = dresid
    for c in range(w_v.shape[1] // width):
        cols = slice(c * width, (c + 1) * width)
        dhidden = dot_nn(dbranch, v_v[:, cols])
        dpre = (dhidden * slope_v[:, cols].astype(F32)).astype(BF16)
        dpre_v[:, cols] = dpre
        total = total + dot_nt(dpre, w_v[:, cols])
    return dbranch, total.astype(BF16)


def feed_backward():
    def body(meta, ins, outs, scratch, sems):
        g_h, xh_h, rs_h, slope_h, w_h, v_h, p_h = ins
        dx_h, dpre_h, db_h, sums_h = outs
        g_v, xh_v, rs_v, slope_v, w_v, v_v, p_v, dx_v, dpre_v, db_v, sums_v = scratch
        cp = Copies(sems)
        for c in [
            cp.start(s, d)
            for s, d in zip(ins, (g_v, xh_v, rs_v, slope_v, w_v, v_v, p_v), strict=True)
        ]:
            c.wait()
        dresid, sums = norm_backward(g_v[...], xh_v[...], rs_v[:, 0:1], p_v[5:6, :])
        dbranch, dx = feed_backward_values(dresid, w_v, v_v, slope_v, dpre_v)
        dx_v[...] = dx
        cp.out(dx_v, dx_h)
        db_v[...] = dbranch
        cp.out(db_v, db_h)
        cp.out(dpre_v, dpre_h)
        sums_v[...] = sums
        cp.out(sums_v, sums_h)
        cp.finish()

    return body


def feed_both(slot):
    def body(meta, ins, outs, scratch, sems):
        a_h, g_h, w_h, v_h, p_h = ins
        y_h, dx_h, hid_h, dpre_h, db_h, sq_h, sums_h = outs
        a_v, g_v, w_v, v_v, p_v, y_v, dx_v, hid_v, slope_v, dpre_v, db_v, sq_v, sums_v = scratch
        cp = Copies(sems)
        for c in [
            cp.start(s, d) for s, d in zip(ins, (a_v, g_v, w_v, v_v, p_v), strict=True)
        ]:
            c.wait()
        inputs = a_v[...]
        branch = feed_hidden(inputs, w_v, v_v, p_v, hid_v, slope_v)
        cp.out(hid_v, hid_h)
        y, xhat, inv_std, squares = norm_forward(
            inputs, branch, meta[2 + slot], p_v[5:6, :], p_v[6:7, :]
        )
        y_v[...] = y
        cp.out(y_v, y_h)
        dresid, sums = norm_backward(g_v[...], xhat, inv_std, p_v[5:6, :])
        dbranch, dx = feed_backward_values(dresid, w_v, v_v, slope_v, dpre_v)
        dx_v[...] = dx
        cp.out(dx_v, dx_h)
        db_v[...] = dbranch
        cp.out(db_v, db_h)
        cp.out(dpre_v, dpre_h)
        sq_v[...] = squares
        cp.out(sq_v, sq_h)
        sums_v[...] = sums
        cp.out(sums_v, sums_h)
        cp.finish()

    return body


def attend_backward():
    def body(meta, ins, outs, scratch, sems):
        dx_h, dqkv_h, db_h, sums_h = outs
        g_v, xh_v, rs_v, qkv_v, pt_v, w_v, p_v, dx_v, dqkv_v, db_v, sums_v, dc_v, kt_v, dqt_v = scratch
        rows, width = g_v.shape
        size = width // HEADS
        cp = Copies(sems)
        for c in [
            cp.start(s, d)
            for s, d in zip(ins, (g_v, xh_v, rs_v, qkv_v, pt_v, w_v, p_v), strict=True)
        ]:
            c.wait()
        dresid, sums = norm_backward(g_v[...], xh_v[...], rs_v[:, 0:1], p_v[5:6, :])
        dbranch = dresid.astype(BF16)
        db_v[...] = dbranch
        cp.out(db_v, db_h)
        sums_v[...] = sums
        cp.out(sums_v, sums_h)
        dc_v[...] = dot_nt(dbranch, w_v[:, 3 * width :]).astype(BF16)
        kt_v[...] = (qkv_v[:, width : 2 * width] * jnp.asarray(size**-0.5, BF16)).T
        lane = lax.broadcasted_iota(jnp.int32, (rows, 2 * size), 1)
        for pair in range(HEADS // 2):
            cols = slice(2 * size * pair, 2 * size * (pair + 1))
            qp = qkv_v[:, cols]
            vp = qkv_v[:, 2 * width + cols.start : 2 * width + cols.stop]
            dcp = dc_v[:, cols]
            none = jnp.zeros_like(qp)
            dk = dv = None
            for half in range(2):
                head = 2 * pair + half
                mine = (lane >= size) if half else (lane < size)
                probs_low = pt_v[head]
                probs = probs_low.astype(F32)
                dprobs = dot_nt(jnp.where(mine, vp, none), dcp)
                inner = jnp.sum(probs * dprobs, axis=0, keepdims=True)
                dscores = (probs * (dprobs - inner)).astype(BF16)
                dv_part = dot_nn(probs_low, jnp.where(mine, dcp, none))
                dk_part = dot_nn(dscores, jnp.where(mine, qp, none))
                dqt_v[head * size : (head + 1) * size, :] = dot_nn(
                    kt_v[head * size : (head + 1) * size, :], dscores
                ).astype(BF16)
                dv = dv_part if dv is None else dv + dv_part
                dk = dk_part if dk is None else dk + dk_part
            dqkv_v[:, width + cols.start : width + cols.stop] = dk.astype(BF16)
            dqkv_v[:, 2 * width + cols.start : 2 * width + cols.stop] = dv.astype(BF16)
        dqkv_v[:, :width] = dqt_v[...].T
        cp.out(dqkv_v, dqkv_h)
        dx_v[...] = (dresid + dot_nt(dqkv_v[...], w_v[:, : 3 * width])).astype(BF16)
        cp.out(dx_v, dx_h)
        cp.finish()

    return body


def core_rows(meta, own):
    bit = lax.rem(meta[1], 2)
    return bit if own else 1 - bit


def weight_sums(feed):
    def body(meta, ins, outs, scratch, sems):
        cp = Copies(sems)
        if feed:
            keep_m, send_m, keep_v, send_v, small_h = outs
        else:
            keep_m, send_m, small_h = outs
        a_v, wide_v, b_v, other_v, sq_v, sums_v, main_v, side_v, at_v, small_v = scratch
        count = sq_v.shape[0]
        rows, width = a_v.shape[0] // count, a_v.shape[1]
        half = width // 2
        a_h, wide_h, b_h, other_h, sq_h, sums_h = (
            ins[i * count : (i + 1) * count] for i in range(6)
        )
        loads = []
        for j in range(count):
            part = pl.ds(j * rows, rows)
            loads += [
                cp.start(a_h[j], a_v.at[part]),
                cp.start(wide_h[j], wide_v.at[part]),
                cp.start(b_h[j], b_v.at[part]),
                cp.start(other_h[j], other_v.at[part]),
                cp.start(sq_h[j], sq_v.at[j]),
                cp.start(sums_h[j], sums_v.at[j]),
            ]
        for c in loads:
            c.wait()
        at_v[:width, :] = a_v[...].T
        at_v[width:, :] = jnp.ones((at_v.shape[0] - width, a_v.shape[0]), BF16)
        small_v[...] = jnp.zeros_like(small_v)
        wide = wide_v.shape[1]
        for c in range(wide // width):
            cols = slice(c * width, (c + 1) * width)
            grad = dot_nn(at_v[...], wide_v[:, cols])
            main_v[:, cols] = grad[:width].astype(BF16)
            place = (3, 0, 1, 2)[c] if feed else (0, 2, 1)[c]
            small_v[place : place + 1, :] = grad[width : width + 1]
        if feed:
            small_v[4:5, :] = jnp.sum(b_v[...].astype(F32), axis=0, keepdims=True)
            at_v[:width, :] = b_v[...].T
            for c in range(wide // width):
                cols = slice(c * width, (c + 1) * width)
                side_v[:, cols] = dot_nn(at_v[:width, :], other_v[:, cols]).astype(BF16)
        else:
            at_v[:width, :] = other_v[...].T
            grad = dot_nn(at_v[...], b_v[...])
            main_v[:, 3 * width :] = grad[:width].astype(BF16)
            small_v[4:5, :] = grad[width : width + 1]
            small_v[2:3, :] = jnp.zeros((1, width), F32)
        sq = sq_v[0]
        sm = sums_v[0]
        for j in range(1, count):
            sq, sm = sq + sq_v[j], sm + sums_v[j]
        small_v[5:7, :] = sm[0:2]
        small_v[7:9, :] = sq[0:2]
        tokens = meta[2]
        for j in range(1, count):
            tokens = tokens + meta[2 + j]
        small_v[9:10, :] = jnp.full((1, width), tokens, jnp.int32).astype(F32)
        own = pl.multiple_of(core_rows(meta, True) * half, half)
        far = pl.multiple_of(core_rows(meta, False) * half, half)
        cp.out(main_v.at[pl.ds(far, half)], send_m)
        if feed:
            cp.out(side_v.at[pl.ds(far, half)], send_v)
        cp.out(small_v, small_h)
        cp.out(main_v.at[pl.ds(own, half)], keep_m)
        if feed:
            cp.out(side_v.at[pl.ds(own, half)], keep_v)
        cp.finish()

    return body


def core_add(masks, with_small):
    def body(meta, ins, outs, scratch, sems):
        keep_h, got_h = ins[:2]
        keep_v, got_v, sum_v, small_v = scratch
        cp = Copies(sems)
        loads = [cp.start(keep_h, keep_v), cp.start(got_h, got_v)]
        if with_small:
            loads += [cp.start(ins[2], small_v.at[0]), cp.start(ins[3], small_v.at[1])]
        for c in loads:
            c.wait()
        sum_v[...] = (keep_v[...].astype(F32) + got_v[...].astype(F32)).astype(BF16)
        chip = lax.div(meta[1], 2)
        size = outs[0].shape[0]
        for mask, out in zip(masks, outs):
            at = pl.multiple_of(jnp.bitwise_xor(chip, mask // 2) * size, size)
            cp.out(sum_v.at[pl.ds(at, size)], out)
        if with_small:
            small_v[0] = small_v[0] + small_v[1]
            cp.out(small_v.at[0], outs[len(masks)])
        cp.finish()

    return body


def chip_add(count, split, with_small):
    def body(meta, ins, outs, scratch, sems):
        got_v, sum_v, small_v = scratch
        cp = Copies(sems)
        loads = [cp.start(ins[i], got_v.at[i]) for i in range(count)]
        if with_small:
            loads += [cp.start(ins[count + i], small_v.at[i]) for i in range(count)]
        for c in loads:
            c.wait()
        total = got_v[0].astype(F32)
        for i in range(1, count):
            total = total + got_v[i].astype(F32)
        sum_v[...] = total.astype(BF16)
        if split:
            half = sum_v.shape[1] // 2
            cp.out(sum_v.at[:, :half], outs[0])
            cp.out(sum_v.at[:, half:], outs[1])
        else:
            cp.out(sum_v, outs[0])
        if with_small:
            total = small_v[0]
            for i in range(1, count):
                total = total + small_v[i]
            small_v[0] = total
            cp.out(small_v.at[0], outs[-1])
        cp.finish()

    return body


def assemble(masks):
    def body(meta, ins, outs, scratch, sems):
        (out_h,) = outs
        (all_v,) = scratch
        blocks, own_h = ins[:-1], ins[-1]
        width, half = own_h.shape
        size = blocks[0].shape[0]
        cp = Copies(sems)
        chip, core = lax.div(meta[1], 2), lax.rem(meta[1], 2)
        loads = [cp.start(own_h, all_v.at[:, half:])]
        for mask, block in zip(masks, blocks, strict=True):
            side = jnp.bitwise_xor(core, mask % 2)
            at = side * (width // 2) + jnp.bitwise_xor(chip, mask // 2) * size
            at = pl.multiple_of(at, size)
            loads.append(cp.start(block, all_v.at[pl.ds(at, size), :half]))
        for c in loads:
            c.wait()
        cp.out(all_v, out_h)
        cp.finish()

    return body


def widen(masks):
    def body(meta, ins, outs, scratch, sems):
        main_h, side_h = outs
        low_m, low_s, full_m, full_s = scratch
        width = main_h.shape[1]
        count = len(masks)
        size = ins[0].shape[0]
        cp = Copies(sems)
        chip, core = lax.div(meta[1], 2), lax.rem(meta[1], 2)
        loads = []
        for i in range(count):
            loads.append(
                (cp.start(ins[i], low_m.at[i]), cp.start(ins[count + i], low_s.at[i]))
            )
        for i, mask in enumerate(masks):
            for c in loads[i]:
                c.wait()
            full_m[i] = low_m[i].astype(F32)
            full_s[i] = low_s[i].astype(F32)
            side = jnp.bitwise_xor(core, mask % 2)
            at = side * (width // 2) + jnp.bitwise_xor(chip, mask // 2) * size
            at = pl.multiple_of(at, size)
            cp.out(full_m.at[i], main_h.at[0, pl.ds(at, size)])
            cp.out(full_s.at[i], side_h.at[0, pl.ds(at, size)])
        cp.finish()

    return body


def on_device(
    tokens, lengths, cotangent, main_weight, side_weight, in_bias, out_bias, norm_gain, norm_shift
):
    segments, shards = lax.axis_size("segment"), lax.axis_size("dp")
    z, d = lax.axis_index("segment"), lax.axis_index("dp")
    rows, width = tokens.shape
    main_mat, side_mat = main_weight[0], side_weight[0]
    hidden = main_mat.shape[1]
    half_width = side_mat.shape[1]
    block = width // shards
    last = segments - 1
    feeds = tuple(range(1, segments, 2))
    chip_masks = tuple(range(0, shards, 2))
    masks = chip_masks + tuple(m + 1 for m in chip_masks)
    meta = jnp.concatenate(
        [jnp.stack([z, d]).astype(jnp.int32), lengths[:, 0].astype(jnp.int32)]
    )
    order = jnp.zeros((8, 128), F32)

    def hop(value, *pairs):
        return lax.ppermute(value, "segment", list(pairs))

    def swap(value, mask, where=None):
        if where is None:
            return lax.ppermute(value, "dp", [(i, i ^ mask) for i in range(shards)])
        pairs = [(s * shards + i, s * shards + (i ^ mask)) for s in where for i in range(shards)]
        return lax.ppermute(value, ("segment", "dp"), pairs)

    row0 = jnp.mod(d, 2) * (width // 2) + (d // 2) * block
    share = lax.dynamic_slice(side_mat, (row0, 0), (block, half_width))
    up = [(s - 1, s) for s in feeds]
    share = hop(share, *up)
    low_bias = hop(in_bias[0, 2 * width :].reshape(1, width), *up)

    bias = in_bias[0].astype(F32).reshape(3, width)
    is_feed = jnp.mod(z, 2) == 1
    params = jnp.concatenate(
        [
            jnp.where(
                is_feed,
                jnp.concatenate([low_bias.astype(F32), bias]),
                jnp.concatenate(
                    [bias[0:1], jnp.zeros((1, width), F32), bias[1:2], jnp.zeros((1, width), F32)]
                ),
            ),
            out_bias.astype(F32),
            norm_gain.astype(F32),
            norm_shift.astype(F32),
            jnp.zeros((9, width), F32),
        ]
    )

    first_in = [tokens] + [hop(tokens, (j, 0)) for j in range(1, segments)]
    last_in = [hop(cotangent, (j, last)) for j in range(last)] + [cotangent]

    got = [share] + [swap(share, m, feeds) for m in chip_masks[1:]]
    got += [swap(b, 1, feeds) for b in got]

    narrow = ((rows, width), BF16)
    wide = ((rows, hidden), BF16)
    full = ((rows, width), F32)
    std = ((rows, 128), F32)
    small = ((8, width), F32)
    pset = ((16, width), F32)
    wmat = ((width, hidden), BF16)
    qkv = ((rows, 3 * width), BF16)
    probs = ((HEADS, rows, rows), BF16)

    (down,), order = kernel_call(
        assemble(masks), feeds, meta, order, got + [side_mat], [wmat], [wmat], len(masks) + 2
    )

    acts = {}
    keep = {}
    inputs = first_in
    for s in range(last):
        outs_here = []
        for j in range(segments):
            if s % 2 == 0:
                res, order = kernel_call(
                    attend_forward(j), (s,), meta, order, [inputs[j], main_mat, params],
                    [narrow, qkv, narrow, probs, full, std, small],
                    [narrow, wmat, pset, narrow, qkv, narrow, ((width, rows), BF16),
                     ((width, rows), BF16), probs, full, std, small],
                    16,
                )
                keep[s, j] = dict(zip(("y", "qkv", "ctx", "pt", "xh", "rs", "sq"), res))
            else:
                res, order = kernel_call(
                    feed_forward(j), (s,), meta, order, [inputs[j], main_mat, down, params],
                    [narrow, wide, wide, full, std, small],
                    [narrow, wmat, wmat, pset, narrow, wide, wide, full, std, small],
                    16,
                )
                keep[s, j] = dict(zip(("y", "hid", "slope", "xh", "rs", "sq"), res))
            acts[s, j] = inputs[j]
            outs_here.append(hop(res[0], (s, s + 1)))
        inputs = outs_here

    finals, grads = [], []
    for j in range(segments):
        res, order = kernel_call(
            feed_both(j), (last,), meta, order, [inputs[j], last_in[j], main_mat, down, params],
            [narrow, narrow, wide, wide, narrow, small, small],
            [narrow, narrow, wmat, wmat, pset, narrow, narrow, wide, wide, wide, narrow, small, small],
            16,
        )
        keep[last, j] = dict(zip(("y", "dx", "hid", "dpre", "db", "sq", "sums"), res))
        acts[last, j] = inputs[j]
        finals.append(res[0])
        grads.append(hop(res[1], (last, last - 1)))

    returned = []
    for s in range(last - 1, -1, -1):
        outs_here = []
        for j in range(segments):
            k = keep[s, j]
            if s % 2 == 0:
                res, order = kernel_call(
                    attend_backward(), (s,), meta, order,
                    [grads[j], k["xh"], k["rs"], k["qkv"], k["pt"], main_mat, params],
                    [narrow, qkv, narrow, small],
                    [narrow, full, std, qkv, probs, wmat, pset, narrow, qkv, narrow, small,
                     narrow, ((width, rows), BF16), ((width, rows), BF16)],
                    16,
                )
                k.update(zip(("dx", "dqkv", "db", "sums"), res))
            else:
                res, order = kernel_call(
                    feed_backward(), (s,), meta, order,
                    [grads[j], k["xh"], k["rs"], k["slope"], main_mat, down, params],
                    [narrow, wide, narrow, small],
                    [narrow, full, std, wide, wmat, wmat, pset, narrow, wide, narrow, small],
                    16,
                )
                k.update(zip(("dx", "dpre", "db", "sums"), res))
            outs_here.append(hop(res[0], (s, s - 1)) if s else res[0])
        grads = outs_here

    homeward = [hop(finals[j], (last, j)) for j in range(last)] + [finals[last]]
    outputs = lax.select_n(z, *homeward)
    homeward = [grads[0]] + [hop(grads[j], (0, j)) for j in range(1, segments)]
    input_grad = lax.select_n(z, *homeward)

    half = (width // 2, hidden)
    smalls = (16, width)

    def stacked(names_even, s):
        return [keep[s, j][n] if n != "a" else acts[s, j] for n in names_even for j in range(segments)]

    def picked(name_attend, name_feed):
        return name_attend, name_feed

    all_rows = segments * rows
    results = {}
    for s in range(last, -1, -1):
        feed = s % 2 == 1
        names = ("a", "dpre", "db", "hid", "sq", "sums") if feed else ("a", "dqkv", "db", "ctx", "sq", "sums")
        wide_cols = hidden if feed else 3 * width
        other_cols = hidden if feed else width
        outs_s = [(half, BF16), (half, BF16)] + ([(half, BF16), (half, BF16)] if feed else []) + [(smalls, F32)]
        res, order = kernel_call(
            weight_sums(feed), (s,), meta, order, stacked(names, s), outs_s,
            [((all_rows, width), BF16), ((all_rows, wide_cols), BF16), ((all_rows, width), BF16),
             ((all_rows, other_cols), BF16), ((segments, 8, width), F32), ((segments, 8, width), F32),
             wmat, wmat, ((width + 16, all_rows), BF16), (smalls, F32)],
            6 * segments + 8,
        )
        results[s] = res
    parts = [lax.select_n(z, *[results[s][i] for s in range(segments)]) for i in range(2)]
    small_own = lax.select_n(z, *[results[s][-1] for s in range(segments)])
    v_keep = lax.select_n((z == last).astype(jnp.int32), *[results[s][2] for s in feeds])
    v_send = lax.select_n((z == last).astype(jnp.int32), *[results[s][3] for s in feeds])

    n_chip = len(chip_masks)
    blk = ((block, hidden), BF16)
    side_blk = ((block, half_width), BF16)
    halfs = (half, BF16)
    sm = (smalls, F32)
    m_blocks, order = kernel_call(
        core_add(chip_masks, True), None, meta, order,
        [parts[0], swap(parts[1], 1), small_own, swap(small_own, 1)],
        [blk] * n_chip + [sm], [halfs, halfs, halfs, ((2,) + smalls, F32)], n_chip + 8,
    )
    v_blocks, order = kernel_call(
        core_add(chip_masks, False), feeds, meta, order, [v_keep, swap(v_send, 1, feeds)],
        [blk] * n_chip, [halfs, halfs, halfs, ((2,) + smalls, F32)], n_chip + 8,
    )
    small_chip = m_blocks[-1]
    m_blocks = [m_blocks[0]] + [swap(m_blocks[i], chip_masks[i]) for i in range(1, n_chip)]
    s_blocks = [small_chip] + [swap(small_chip, m) for m in chip_masks[1:]]
    v_blocks = [v_blocks[0]] + [swap(v_blocks[i], chip_masks[i], feeds) for i in range(1, n_chip)]
    (main_own, small_all), order = kernel_call(
        chip_add(n_chip, False, True), None, meta, order, m_blocks + s_blocks, [blk, sm],
        [((n_chip,) + blk[0], BF16), blk, ((n_chip,) + smalls, F32)], 2 * n_chip + 4,
    )
    (low_own, high_own), order = kernel_call(
        chip_add(n_chip, True, False), feeds, meta, order, v_blocks, [side_blk, side_blk],
        [((n_chip,) + blk[0], BF16), blk, ((n_chip,) + smalls, F32)], 2 * n_chip + 4,
    )
    down_pairs = [(s, s - 1) for s in feeds]
    low_got = hop(low_own, *down_pairs)
    side_own = jnp.where(is_feed, high_own, low_got)
    bias_got = hop(small_all[3:4], *down_pairs)

    main_got = [main_own] + [swap(main_own, m) for m in chip_masks[1:]]
    main_got += [swap(b, 1) for b in main_got]
    side_got = [side_own] + [swap(side_own, m) for m in chip_masks[1:]]
    side_got += [swap(b, 1) for b in side_got]
    (main_grad, side_grad), order = kernel_call(
        widen(masks), None, meta, order, main_got + side_got,
        [((1, width, hidden), F32), ((1, width, half_width), F32)],
        [((shards,) + blk[0], BF16), ((shards,) + side_blk[0], BF16),
         ((shards,) + blk[0], F32), ((shards,) + side_blk[0], F32)],
        4 * shards + 2,
    )

    in_bias_grad = jnp.concatenate(
        [small_all[0], small_all[1], jnp.where(is_feed, small_all[2], bias_got[0])]
    )
    tokens_all = small_all[9, 0]
    square_sums = jnp.sum(small_all[7:9], axis=1)
    stats = jnp.sqrt(square_sums / (tokens_all * width))
    return (
        outputs,
        input_grad,
        main_grad,
        side_grad,
        in_bias_grad[None],
        small_all[4:5],
        small_all[5:6],
        small_all[6:7],
        stats[None],
    )


def solution(mesh):
    over = P(("segment", "dp"), None)
    by_segment = [P("segment", None, None)] * 2 + [P("segment", None)] * 4
    in_specs = (over, P(None, "dp"), over, *by_segment)
    out_specs = (over, over, *by_segment, P("segment", None))
    return jax.shard_map(
        on_device, mesh=mesh, in_specs=in_specs, out_specs=out_specs, check_vma=False
    )
```

```python
import jax
import jax.numpy as jnp
from jax import lax
from jax.experimental import pallas as pl
from jax.experimental.pallas import tpu as pltpu
from jax.sharding import PartitionSpec as P

HEADS = 8
EPS = 1e-05
LANES = 128
VMEM_LIMIT = 22 * 1024 * 1024
F32 = jnp.float32
BF16 = jnp.bfloat16
GELU_IN = 0.7978845608028654
GELU_CUBE = 0.044715 * GELU_IN

BIAS, OUT_BIAS, GAIN, SHIFT, RESID_SQ, BRANCH_SQ, COUNT, SMALLS = 0, 4, 5, 6, 7, 8, 9, 16


def dot_nn(left, right):
    return jnp.dot(left, right, preferred_element_type=F32)


def dot_nt(left, right):
    return lax.dot_general(left, right, (((1,), (1,)), ((), ())), preferred_element_type=F32)


def kernel_call(body, meta, ins, outs, scratch=(), kept=(), copies=0, hbm_ins=(), hbm_outs=()):
    n_in, n_kept, n_out = len(ins), len(kept), len(outs)

    def kernel(z_ref, d_ref, *refs):
        at = 0
        groups = []
        for n in (n_in, n_kept, n_out, n_kept):
            groups.append(refs[at : at + n])
            at += n
        body((z_ref[0], d_ref[0]), groups[0], groups[2], groups[3], refs[at:])

    vmem = pl.BlockSpec(memory_space=pltpu.VMEM)
    hbm = pl.BlockSpec(memory_space=pltpu.HBM)

    def held(x, space=pltpu.VMEM):
        return pltpu.with_memory_space_constraint(x, space)

    results = pl.pallas_call(
        kernel,
        out_shape=[
            jax.ShapeDtypeStruct(*o) if i in hbm_outs else pltpu.VMEM(*o) for i, o in enumerate(outs)
        ]
        + [pltpu.VMEM(k.shape, k.dtype) for k in kept],
        in_specs=[pl.BlockSpec(memory_space=pltpu.SMEM)] * 2
        + [hbm if i in hbm_ins else vmem for i in range(n_in)]
        + [vmem] * n_kept,
        out_specs=[hbm if i in hbm_outs else vmem for i in range(n_out)] + [vmem] * n_kept,
        scratch_shapes=[pltpu.VMEM(*s) for s in scratch]
        + ([pltpu.SemaphoreType.DMA((copies,))] if copies else []),
        input_output_aliases={2 + n_in + i: n_out + i for i in range(n_kept)},
        compiler_params=pltpu.CompilerParams(vmem_limit_bytes=VMEM_LIMIT),
        cost_estimate=pl.CostEstimate(flops=1, bytes_accessed=1, transcendentals=1),
    )(
        *meta,
        *[held(x, pltpu.HBM if i in hbm_ins else pltpu.VMEM) for i, x in enumerate(ins)],
        *[held(k) for k in kept],
    )
    return tuple(results[:n_out]), tuple(results[n_out:])


def norm_forward(inputs, branch, seq_len, gain, shift):
    resid = inputs.astype(F32) + branch
    mean = jnp.mean(resid, axis=-1, keepdims=True)
    centred = resid - mean
    var = jnp.mean(centred * centred, axis=-1, keepdims=True)
    inv_std = lax.rsqrt(var + EPS)
    xhat = centred * inv_std
    row = lax.broadcasted_iota(jnp.int32, resid.shape, 0)
    live = row < seq_len
    resid_sq = jnp.sum(jnp.where(live, resid * resid, 0.0), axis=0, keepdims=True)
    branch_sq = jnp.sum(jnp.where(live, branch * branch, 0.0), axis=0, keepdims=True)
    return (xhat * gain + shift).astype(BF16), xhat, inv_std, resid_sq, branch_sq


def norm_backward(grad, xhat, inv_std, gain):
    grad = grad.astype(F32)
    gy = grad * gain
    first = jnp.mean(gy, axis=-1, keepdims=True)
    second = jnp.mean(gy * xhat, axis=-1, keepdims=True)
    dresid = (gy - first - xhat * second) * inv_std
    gain_sum = jnp.sum(grad * xhat, axis=0, keepdims=True)
    shift_sum = jnp.sum(grad, axis=0, keepdims=True)
    return dresid, gain_sum, shift_sum


class Vectors:
    def __init__(self, in_bias, out_bias, gain, shift, low_bias=None):
        self.refs = (in_bias, out_bias, gain, shift, low_bias)

    def in_bias(self, i, width):
        return self.refs[0][0:1, i * width : (i + 1) * width].astype(F32)

    def first_bias(self, i, width):
        return self.refs[4][0:1, :width].astype(F32) if i == 0 else self.in_bias(i - 1, width)

    out_bias = property(lambda self: self.refs[1][...].astype(F32))
    gain = property(lambda self: self.refs[2][...].astype(F32))
    shift = property(lambda self: self.refs[3][...].astype(F32))


class Store:
    def __init__(self, kept, j):
        acts, wide, aux, xhat, inv_std, grad_wide, grad_branch, sums = kept[:8]
        self.x, self.wide, self.aux, self.xhat, self.inv_std, self.gwide, self.db = (
            a.at[j] for a in (acts, wide, aux, xhat, inv_std, grad_wide, grad_branch)
        )
        self.sums, self.first = sums, j == 0

    def add(self, row, value):
        if self.first:
            self.sums[row : row + 1, :] = value
        else:
            self.sums[row : row + 1, :] = self.sums[row : row + 1, :] + value


def attend_forward(inputs, w, vec, seq_len, st, send, scratch):
    vt, ctxt = scratch[:2]
    rows, width = inputs.shape
    size = width // HEADS
    st.x[...] = inputs
    q = (dot_nn(inputs, w[:, :width]) + vec.in_bias(0, width)).astype(BF16)
    st.wide[:, :width] = q * jnp.asarray(size**-0.5, BF16)
    st.wide[:, width : 2 * width] = dot_nn(inputs, w[:, width : 2 * width]).astype(BF16)
    v = (dot_nn(inputs, w[:, 2 * width : 3 * width]) + vec.in_bias(1, width)).astype(BF16)
    st.wide[:, 2 * width : 3 * width] = v
    vt[...] = v.T
    key_live = lax.broadcasted_iota(jnp.int32, (rows, rows), 0) < seq_len
    lane = lax.broadcasted_iota(jnp.int32, (rows, 2 * size), 1)
    for pair in range(HEADS // 2):
        cols = slice(2 * size * pair, 2 * size * (pair + 1))
        qp = st.wide[:, cols]
        kp = st.wide[:, width + cols.start : width + cols.stop]
        for half in range(2):
            head = 2 * pair + half
            mine = (lane >= size) if half else (lane < size)
            scores = dot_nt(jnp.where(mine, kp, jnp.zeros_like(kp)), qp)
            scores = jnp.where(key_live, scores, -1e30)
            top = jnp.max(scores, axis=0, keepdims=True)
            expo = jnp.exp(scores - top)
            total = jnp.sum(expo, axis=0, keepdims=True)
            probs = (expo * (1.0 / total)).astype(BF16)
            st.aux[:, head * rows : (head + 1) * rows] = probs
            ctxt[head * size : (head + 1) * size, :] = dot_nn(
                vt[head * size : (head + 1) * size, :], probs
            ).astype(BF16)
    ctx = ctxt[...].T
    st.wide[:, 3 * width :] = ctx
    branch = dot_nn(ctx, w[:, 3 * width :]) + vec.out_bias
    y, xhat, inv_std, resid_sq, branch_sq = norm_forward(inputs, branch, seq_len, vec.gain, vec.shift)
    send[...] = y
    st.xhat[...] = xhat
    st.inv_std[...] = jnp.broadcast_to(inv_std, st.inv_std.shape)
    st.add(RESID_SQ, resid_sq)
    st.add(BRANCH_SQ, branch_sq)


def feed_branch(inputs, w, down, vec, st):
    width = inputs.shape[1]
    st.x[...] = inputs
    branch = None
    for c in range(w.shape[1] // width):
        cols = slice(c * width, (c + 1) * width)
        x = dot_nn(inputs, w[:, cols]) + vec.first_bias(c, width)
        square = x * x
        t = jnp.tanh(x * (GELU_IN + GELU_CUBE * square))
        s = 0.5 + 0.5 * t
        act = x * s
        slope = s + act * (1.0 - t) * (GELU_IN + (3.0 * GELU_CUBE) * square)
        hidden = act.astype(BF16)
        st.wide[:, cols] = hidden
        st.aux[:, cols] = slope.astype(BF16)
        part = dot_nt(hidden, down[:, cols])
        branch = part if branch is None else branch + part
    return branch + vec.out_bias


def feed_forward(inputs, w, down, vec, seq_len, st, send):
    branch = feed_branch(inputs, w, down, vec, st)
    y, xhat, inv_std, resid_sq, branch_sq = norm_forward(inputs, branch, seq_len, vec.gain, vec.shift)
    send[...] = y
    st.xhat[...] = xhat
    st.inv_std[...] = jnp.broadcast_to(inv_std, st.inv_std.shape)
    st.add(RESID_SQ, resid_sq)
    st.add(BRANCH_SQ, branch_sq)


def feed_grads(dresid, w, down, st, send):
    width = dresid.shape[1]
    dbranch = dresid.astype(BF16)
    st.db[...] = dbranch
    total = dresid
    for c in range(w.shape[1] // width):
        cols = slice(c * width, (c + 1) * width)
        dhidden = dot_nn(dbranch, down[:, cols])
        dpre = (dhidden * st.aux[:, cols].astype(F32)).astype(BF16)
        st.gwide[:, cols] = dpre
        total = total + dot_nt(dpre, w[:, cols])
    send[...] = total.astype(BF16)


def feed_backward(grad, w, down, vec, st, send):
    dresid, gain_sum, shift_sum = norm_backward(grad, st.xhat[...], st.inv_std[:, 0:1], vec.gain)
    st.add(GAIN, gain_sum)
    st.add(SHIFT, shift_sum)
    feed_grads(dresid, w, down, st, send)


def feed_both(inputs, grad, w, down, vec, seq_len, st, y_out, send):
    branch = feed_branch(inputs, w, down, vec, st)
    y, xhat, inv_std, resid_sq, branch_sq = norm_forward(inputs, branch, seq_len, vec.gain, vec.shift)
    y_out[...] = y
    dresid, gain_sum, shift_sum = norm_backward(grad, xhat, inv_std, vec.gain)
    st.add(RESID_SQ, resid_sq)
    st.add(BRANCH_SQ, branch_sq)
    st.add(GAIN, gain_sum)
    st.add(SHIFT, shift_sum)
    feed_grads(dresid, w, down, st, send)


def attend_backward(grad, w, vec, st, send, scratch):
    kt, dqt, dc = scratch[:3]
    rows, width = grad.shape
    size = width // HEADS
    dresid, gain_sum, shift_sum = norm_backward(grad, st.xhat[...], st.inv_std[:, 0:1], vec.gain)
    st.add(GAIN, gain_sum)
    st.add(SHIFT, shift_sum)
    dbranch = dresid.astype(BF16)
    st.gwide[:, 3 * width :] = dbranch
    dc[...] = dot_nt(dbranch, w[:, 3 * width :]).astype(BF16)
    kt[...] = (st.wide[:, width : 2 * width] * jnp.asarray(size**-0.5, BF16)).T
    lane = lax.broadcasted_iota(jnp.int32, (rows, 2 * size), 1)
    for pair in range(HEADS // 2):
        cols = slice(2 * size * pair, 2 * size * (pair + 1))
        qp = st.wide[:, cols]
        vp = st.wide[:, 2 * width + cols.start : 2 * width + cols.stop]
        dcp = dc[:, cols]
        none = jnp.zeros_like(qp)
        dk = dv = None
        for half in range(2):
            head = 2 * pair + half
            mine = (lane >= size) if half else (lane < size)
            probs_low = st.aux[:, head * rows : (head + 1) * rows]
            probs = probs_low.astype(F32)
            dprobs = dot_nt(jnp.where(mine, vp, none), dcp)
            inner = jnp.sum(probs * dprobs, axis=0, keepdims=True)
            dscores = (probs * (dprobs - inner)).astype(BF16)
            dv_part = dot_nn(probs_low, jnp.where(mine, dcp, none))
            dk_part = dot_nn(dscores, jnp.where(mine, qp, none))
            dqt[head * size : (head + 1) * size, :] = dot_nn(
                kt[head * size : (head + 1) * size, :], dscores
            ).astype(BF16)
            dv = dv_part if dv is None else dv + dv_part
            dk = dk_part if dk is None else dk + dk_part
        st.gwide[:, width + cols.start : width + cols.stop] = dk.astype(BF16)
        st.gwide[:, 2 * width + cols.start : 2 * width + cols.stop] = dv.astype(BF16)
    st.gwide[:, :width] = dqt[...].T
    send[...] = (dresid + dot_nt(st.gwide[:, : 3 * width], w[:, : 3 * width])).astype(BF16)


def roles_of(slot, segments):
    last = segments - 1
    found = []
    for z in range(segments):
        j = slot - 2 * z
        if 0 <= j < segments:
            found.append((z, "both" if z == last else "forward", j))
        j = slot - (4 * last - 2 * z)
        if z < last and 0 <= j < segments:
            found.append((z, "backward", j))
    return found


def half_rows(meta, own, width):
    bit = lax.rem(meta[1], 2)
    bit = bit if own else 1 - bit
    return pl.multiple_of(bit * (width // 2), width // 2)


def weight_half(own, where):
    def body(meta, ins, outs, kept, scratch):
        acts, wide, _, _, _, grad_wide, grad_branch, sums, *rest = kept
        main_out, side_out = rest if rest else outs
        (lengths,) = ins
        at, sm = scratch
        count, rows, width = acts.shape
        half = width // 2
        full = wide.shape[2]
        total = count * rows
        start = half_rows(meta, own, width)
        mine = pl.ds(start, half)
        feeds = [s for s in where if s % 2]
        attends = [s for s in where if s % 2 == 0]

        def put_small():
            tokens = jnp.sum(lengths[...].astype(F32), axis=0, keepdims=True)
            sm[COUNT : COUNT + 1, :] = jnp.broadcast_to(tokens, (1, width))
            main_out[:, full:] = sm[:, mine].T.astype(BF16)

        def load(source, lanes):
            for j in range(count):
                at[:half, j * rows : (j + 1) * rows] = source[j, :, lanes].T

        def begin():
            sm[...] = jnp.zeros_like(sm)
            sm[:SMALLS, :] = sums[...]
            at[half:, :] = jnp.ones((at.shape[0] - half, total), BF16)
            load(acts, mine)

        def feed():
            begin()
            grads = grad_wide[...].reshape(total, full)
            for c in range(full // width):
                cols = slice(c * width, (c + 1) * width)
                grad = dot_nn(at[...], grads[:, cols])
                main_out[:, cols] = grad[:half].astype(BF16)
                place = BIAS + (3, 0, 1, 2)[c]
                sm[place : place + 1, :] = grad[half : half + 1]
            branch_sum = jnp.sum(grad_branch[...].reshape(total, width).astype(F32), axis=0, keepdims=True)
            sm[OUT_BIAS : OUT_BIAS + 1, :] = branch_sum
            put_small()
            side_out[:, full // 2 : full // 2 + LANES] = jnp.broadcast_to(
                sm[BIAS + 3 : BIAS + 4, mine], (LANES, half)
            ).T.astype(BF16)
            load(grad_branch, mine)
            hid = wide[...].reshape(total, full)
            for c in range(full // width):
                cols = slice(c * width, (c + 1) * width)
                grad = dot_nn(at[:half, :], hid[:, cols]).astype(BF16)
                put = c * width + (LANES if c * width >= full // 2 else 0)
                side_out[:, put : put + width] = grad

        def attend():
            begin()
            grads = grad_wide[...].reshape(total, full)
            for c in range(3):
                cols = slice(c * width, (c + 1) * width)
                grad = dot_nn(at[...], grads[:, cols])
                main_out[:, cols] = grad[:half].astype(BF16)
                if c != 1:
                    place = BIAS + c // 2
                    sm[place : place + 1, :] = grad[half : half + 1]
            load(wide, pl.ds(pl.multiple_of(3 * width + start, half), half))
            grad = dot_nn(at[...], grads[:, 3 * width :])
            main_out[:, 3 * width : full] = grad[:half].astype(BF16)
            sm[OUT_BIAS : OUT_BIAS + 1, :] = grad[half : half + 1]
            put_small()

        for segments_here, run in ((feeds, feed), (attends, attend)):
            if segments_here:
                here = meta[0] == segments_here[0]
                for other in segments_here[1:]:
                    here = here | (meta[0] == other)
                pl.when(here)(run)

    return body


def core_add(masks, feeds_only):
    def body(meta, ins, outs, kept, scratch):
        keep, got = ins
        size = outs[0].shape[0]
        chip = lax.div(meta[1], 2)

        def run():
            for mask, out in zip(masks, outs, strict=True):
                at = pl.multiple_of(jnp.bitwise_xor(chip, mask // 2) * size, size)
                rows = pl.ds(at, size)
                out[...] = (keep[rows, :].astype(F32) + got[rows, :].astype(F32)).astype(BF16)

        if feeds_only:
            pl.when(lax.rem(meta[0], 2) == 1)(run)
        else:
            run()

    return body


def summed(refs, cols):
    total = refs[0][:, cols].astype(F32)
    for r in refs[1:]:
        total = total + r[:, cols].astype(F32)
    return total.astype(BF16)


def side_sum(meta, ins, outs, kept, scratch):
    @pl.when(lax.rem(meta[0], 2) == 1)
    def _():
        low = outs[0].shape[1]
        outs[0][...] = summed(ins, slice(0, low))
        outs[1][...] = summed(ins, slice(low, None))


def payload(meta, ins, outs, kept, scratch):
    *blocks, high, low_got = ins
    (out,) = outs
    main = blocks[0].shape[1]
    out[:, : main - LANES] = summed(blocks, slice(0, main - LANES))
    small = summed(blocks, slice(main - LANES, None))
    half = high.shape[1]

    @pl.when(lax.rem(meta[0], 2) == 1)
    def _():
        out[:, main - LANES : main] = small
        out[:, main:] = high[...]

    @pl.when(lax.rem(meta[0], 2) == 0)
    def _():
        lane = lax.broadcasted_iota(jnp.int32, small.shape, 1)
        out[:, main - LANES : main] = jnp.where(lane == BIAS + 2, low_got[:, half:], small)
        out[:, main:] = low_got[:, :half]


def block_row(meta, mask, width, size):
    chip, core = lax.div(meta[1], 2), lax.rem(meta[1], 2)
    side = jnp.bitwise_xor(core, mask % 2)
    at = side * (width // 2) + jnp.bitwise_xor(chip, mask // 2) * size
    return pl.multiple_of(at, size)


def begin(meta, ins, outs, kept, scratch):
    share, zero_sums = outs[0], outs[1]
    sems = scratch[-1]
    side = ins[0]
    in_bias = ins[1]
    width = side.shape[0]
    block = share.shape[0] - 16
    copies = [
        pltpu.make_async_copy(
            side.at[pl.ds(block_row(meta, 0, width, block), block)], share.at[:block], sems.at[0]
        )
    ]
    for i, (src, dst) in enumerate(zip(ins[1:], outs[2:])):
        copies.append(pltpu.make_async_copy(src, dst, sems.at[1 + i]))
    for c in copies:
        c.start()
    zero_sums[...] = jnp.zeros_like(zero_sums)
    share[block:, width:] = jnp.zeros((16, share.shape[1] - width), BF16)
    copies[1].wait()
    share[block:, :width] = jnp.broadcast_to(outs[2][:, 2 * width :], (16, width))
    for i, c in enumerate(copies):
        if i != 1:
            c.wait()


def join_chips(masks):
    def body(meta, ins, outs, kept, scratch):
        @pl.when(lax.rem(meta[0], 2) == 1)
        def _():
            (out,) = outs
            block = ins[0].shape[0] - 16
            chip = lax.div(meta[1], 2)
            for mask, share in zip(masks, ins, strict=True):
                at = pl.multiple_of(jnp.bitwise_xor(chip, mask // 2) * block, block)
                out[pl.ds(at, block), :] = share[:block, :]

    return body


def join_cores(meta, ins, outs, kept, scratch):
    @pl.when(lax.rem(meta[0], 2) == 1)
    def _():
        own, other, side, share = ins
        down, low_bias = outs
        width, half = side.shape
        copy = pltpu.make_async_copy(side, down.at[:, half:], scratch[-1].at[0])
        copy.start()
        down[pl.ds(half_rows(meta, True, width), width // 2), :half] = own[...]
        down[pl.ds(half_rows(meta, False, width), width // 2), :half] = other[...]
        low_bias[...] = share[share.shape[0] - 16 :, :width]
        copy.wait()


def widen(masks, segments):
    def body(meta, ins, outs, kept, scratch):
        n = len(masks)
        blocks, finals, backs = ins[:n], ins[n : n + segments], ins[n + segments :]
        out_y, out_g, main_h, side_h, in_b, out_b, gain_h, shift_h, stats_h = outs
        full_m, full_s, cols, vecs, stat, sems = scratch
        used = [0]
        copies = []

        def out(src, dst):
            copy = pltpu.make_async_copy(src, dst, sems.at[used[0]])
            used[0] += 1
            copy.start()
            copies.append(copy)

        def picked(refs, dst):
            at = used[0]
            used[0] += 1
            for j, r in enumerate(refs):

                @pl.when(meta[0] == j)
                def _(r=r):
                    pltpu.make_async_copy(r, dst, sems.at[at]).start()

            copies.append(pltpu.make_async_copy(refs[0], dst, sems.at[at]))

        picked(finals, out_y)
        picked(backs, out_g)
        width, main = main_h.shape[1], main_h.shape[2]
        half = side_h.shape[2]
        size = blocks[0].shape[0]
        for i, mask in enumerate(masks):
            at = block_row(meta, mask, width, size)
            cols[pl.ds(at, size), :] = blocks[i][:, main : main + LANES]
        small = cols[...].T.astype(F32)
        vecs[0:1, :width] = small[BIAS : BIAS + 1]
        vecs[0:1, width : 2 * width] = small[BIAS + 1 : BIAS + 2]
        vecs[0:1, 2 * width :] = small[BIAS + 2 : BIAS + 3]
        vecs[1:2, :width] = small[OUT_BIAS : OUT_BIAS + 1]
        vecs[2:3, :width] = small[GAIN : GAIN + 1]
        vecs[3:4, :width] = small[SHIFT : SHIFT + 1]
        squares = jnp.sum(small[RESID_SQ : BRANCH_SQ + 1], axis=1, keepdims=True)
        values = jnp.sqrt(squares / (small[COUNT : COUNT + 1, 0:1] * width))
        lane = lax.broadcasted_iota(jnp.int32, (1, LANES), 1)
        stat[...] = jnp.where(lane == 0, values[0:1], values[1:2])
        out(vecs.at[0:1], in_b)
        out(vecs.at[1:2, :width], out_b)
        out(vecs.at[2:3, :width], gain_h)
        out(vecs.at[3:4, :width], shift_h)
        out(stat, stats_h)
        for i, mask in enumerate(masks):
            at = block_row(meta, mask, width, size)
            full_m[i] = blocks[i][:, :main].astype(F32)
            out(full_m.at[i], main_h.at[0, pl.ds(at, size)])
            full_s[i] = blocks[i][:, main + LANES : main + LANES + half].astype(F32)
            out(full_s.at[i], side_h.at[0, pl.ds(at, size)])
        for c in copies:
            c.wait()

    return body


def on_device(
    tokens, lengths, cotangent, main_weight, side_weight, in_bias, out_bias, norm_gain, norm_shift
):
    segments, shards = lax.axis_size("segment"), lax.axis_size("dp")
    z, d = lax.axis_index("segment"), lax.axis_index("dp")
    rows, width = tokens.shape
    main_mat, side_mat = main_weight[0], side_weight[0]
    hidden = main_mat.shape[1]
    half_width = side_mat.shape[1]
    block = width // shards
    last = segments - 1
    feeds = tuple(range(1, segments, 2))
    chip_masks = tuple(range(0, shards, 2))
    masks = chip_masks + tuple(m + 1 for m in chip_masks)
    meta = (z.reshape(1), d.reshape(1))

    def hop(value, *pairs):
        return lax.ppermute(value, "segment", list(pairs))

    def swap(value, mask, where=None):
        if where is None:
            return lax.ppermute(value, "dp", [(i, i ^ mask) for i in range(shards)])
        pairs = [(s * shards + i, s * shards + (i ^ mask)) for s in where for i in range(shards)]
        return lax.ppermute(value, ("segment", "dp"), pairs)

    first_in = [None] + [hop(tokens, (j, 0)) for j in range(1, segments)]
    last_in = [hop(cotangent, (j, last)) for j in range(last)]

    kept_shapes = [
        ((segments, rows, width), BF16),
        ((segments, rows, hidden), BF16),
        ((segments, rows, hidden), BF16),
        ((segments, rows, width), F32),
        ((segments, rows, LANES), F32),
        ((segments, rows, hidden), BF16),
        ((segments, rows, width), BF16),
    ]
    loads = [in_bias, out_bias, norm_gain, norm_shift, lengths, main_mat, tokens, cotangent]
    loaded, _ = kernel_call(
        begin, meta, [side_mat, *loads],
        [((block + 16, half_width), BF16), ((SMALLS, width), F32)]
        + [(x.shape, x.dtype) for x in loads]
        + kept_shapes,
        copies=1 + len(loads), hbm_ins=tuple(range(1 + len(loads))),
    )
    share, sums = loaded[:2]
    bias_v, out_bias_v, gain_v, shift_v, lengths_v, main_v, tokens_v, cotangent_v = loaded[2 : 2 + len(loads)]
    kept = (*loaded[2 + len(loads) :], sums)
    first_in[0] = tokens_v
    last_in.append(cotangent_v)

    def lend(share):
        share = hop(share, *[(s - 1, s) for s in feeds])
        got = [share] + [swap(share, m, feeds) for m in chip_masks[1:]]
        (own_half,), _ = kernel_call(join_chips(chip_masks), meta, got, [((width // 2, half_width), BF16)])
        other_half = swap(own_half, 1, feeds)
        (down, low_bias), _ = kernel_call(
            join_cores, meta, [own_half, other_half, side_mat, share],
            [((width, hidden), BF16), ((16, width), BF16)], hbm_ins=(2,), copies=1,
        )
        return down, low_bias

    narrow = ((rows, width), BF16)
    turned = ((width, rows), BF16)
    ext = hidden + LANES
    halfs = ((width // 2, ext), BF16)
    at_shape = ((width // 2 + 16, segments * rows), BF16)
    weight_scratch = [at_shape, ((LANES, width), F32)]
    slots = 4 * last + segments
    waves, sent, finals = {}, {}, []
    homeward = {slots - segments - 2 + 2 * i: last - 1 - i for i in range(last - 1)}
    weights_at = slots - segments + 1
    for slot in range(slots):
        roles = roles_of(slot, segments)
        uses = [r[1] for r in roles]
        attends = any(r[0] % 2 == 0 for r in roles)
        feed_roles = any(r[0] % 2 == 1 for r in roles)
        names, ins = [], []

        def give(name, value):
            names.append(name)
            ins.append(value)

        for name, value in zip(
            ("main", "in_bias", "out_bias", "gain", "shift", "lengths"),
            (main_v, bias_v, out_bias_v, gain_v, shift_v, lengths_v),
        ):
            give(name, value)
        if feed_roles:
            give("down", down)
            give("low_bias", low_bias)
        if slot < segments:
            give("first", first_in[slot])
        if slot == last:
            for value in last_in[:last]:
                give("early", value)
        if slot - 2 in waves:
            give("wave", waves[slot - 2])
        if "both" in uses:
            give("last", last_in[slot - 2 * last])
        if slot in homeward:
            give("home", finals[homeward[slot]])
        outs = [narrow] + ([narrow] if "both" in uses else [])

        def body(meta, in_refs, out_refs, kept_refs, scratch, roles=roles, names=tuple(names)):
            ref = dict(zip(names, in_refs))
            vec = Vectors(
                ref["in_bias"], ref["out_bias"], ref["gain"], ref["shift"], ref.get("low_bias")
            )
            for z_role, what, j in roles:

                @pl.when(meta[0] == z_role)
                def _(z_role=z_role, what=what, j=j):
                    st = Store(kept_refs, j)
                    seq_len = ref["lengths"][j : j + 1, :]
                    w, send = ref["main"], out_refs[0]
                    if what == "backward":
                        if z_role % 2:
                            feed_backward(ref["wave"][...], w, ref["down"], vec, st, send)
                        else:
                            attend_backward(ref["wave"][...], w, vec, st, send, scratch)
                        return
                    inputs = ref["first" if z_role == 0 else "wave"][...]
                    if what == "both":
                        feed_both(
                            inputs, ref["last"][...], w, ref["down"], vec, seq_len, st, out_refs[1], send
                        )
                    elif z_role % 2:
                        feed_forward(inputs, w, ref["down"], vec, seq_len, st, send)
                    else:
                        attend_forward(inputs, w, vec, seq_len, st, send, scratch)

            if "home" in ref:

                @pl.when(meta[0] == last)
                def _():
                    out_refs[0][...] = ref["home"][...]

        scratch = [turned, turned, narrow] if attends else []
        lent = (share,) if slot == 0 else ()
        res, kept = kernel_call(body, meta, ins, outs, scratch, (*kept, *lent))
        if lent:
            kept, share = kept[:-1], kept[-1]
            down, low_bias = lend(share)
        sent[slot] = res[0]
        if "both" in uses:
            finals.append(res[1])
        pairs = []
        for z_role, what, j in roles:
            if what == "forward":
                pairs.append((z_role, z_role + 1))
            elif z_role > 0:
                pairs.append((z_role, z_role - 1))
            elif j > 0:
                pairs.append((z_role, j))
        if slot in homeward:
            pairs.append((last, homeward[slot]))
        if pairs:
            waves[slot] = hop(res[0], *pairs)
        if slot == weights_at:
            upper = tuple(range(1, segments))
            send_out, kept = kernel_call(
                weight_half(False, upper), meta, [lengths_v], [halfs, halfs], weight_scratch, kept
            )
            keep_out, kept = kernel_call(
                weight_half(True, upper), meta, [lengths_v], [halfs, halfs], weight_scratch, kept
            )

    first_home = hop(finals[0], (last, 0))
    outputs_at = [first_home] + [
        waves[next(k for k, v in homeward.items() if v == s)] for s in range(1, last)
    ] + [finals[last]]
    start = slots - segments
    grads_at = [sent[start]] + [waves[start + s] for s in range(1, segments)]

    n_chip = len(chip_masks)
    blk = ((block, ext), BF16)
    low_ext = half_width + LANES
    _, kept = kernel_call(
        weight_half(False, (0,)), meta, [lengths_v], [], weight_scratch, (*kept, *send_out)
    )
    kept, send_out = kept[:-2], kept[-2:]
    _, kept = kernel_call(
        weight_half(True, (0,)), meta, [lengths_v], [], weight_scratch, (*kept, *keep_out)
    )
    kept, keep_out = kept[:-2], kept[-2:]
    main_got = swap(send_out[0], 1)
    side_got = swap(send_out[1], 1, feeds)
    m_blocks, _ = kernel_call(core_add(chip_masks, False), meta, [keep_out[0], main_got], [blk] * n_chip)
    s_blocks, _ = kernel_call(core_add(chip_masks, True), meta, [keep_out[1], side_got], [blk] * n_chip)
    m_blocks = [m_blocks[0]] + [swap(m_blocks[i], chip_masks[i]) for i in range(1, n_chip)]
    s_blocks = [s_blocks[0]] + [swap(s_blocks[i], chip_masks[i], feeds) for i in range(1, n_chip)]
    (low_own, high_own), _ = kernel_call(
        side_sum, meta, s_blocks, [((block, low_ext), BF16), ((block, half_width), BF16)]
    )
    low_got = hop(low_own, *[(s, s - 1) for s in feeds])
    (mine,), _ = kernel_call(
        payload, meta, [*m_blocks, high_own, low_got], [((block, ext + half_width), BF16)]
    )
    gathered = [mine] + [swap(mine, m) for m in chip_masks[1:]]
    gathered += [swap(b, 1) for b in gathered]

    results, _ = kernel_call(
        widen(masks, segments), meta, [*gathered, *outputs_at, *grads_at],
        [
            narrow, narrow,
            ((1, width, hidden), F32), ((1, width, half_width), F32), ((1, 3 * width), F32),
            ((1, width), F32), ((1, width), F32), ((1, width), F32), ((1, LANES), F32),
        ],
        [
            ((shards, block, hidden), F32), ((shards, block, half_width), F32),
            ((width, LANES), BF16), ((8, 3 * width), F32), ((1, LANES), F32),
        ],
        copies=2 * shards + 8,
        hbm_outs=tuple(range(9)),
    )
    return (*results[:8], results[8][:, :2])


def solution(mesh):
    over = P(("segment", "dp"), None)
    by_segment = [P("segment", None, None)] * 2 + [P("segment", None)] * 4
    in_specs = (over, P(None, "dp"), over, *by_segment)
    out_specs = (over, over, *by_segment, P("segment", None))
    return jax.shard_map(
        on_device, mesh=mesh, in_specs=in_specs, out_specs=out_specs, check_vma=False
    )
```

```python
import functools

import jax
import jax.numpy as jnp
from jax import lax
from jax.experimental import pallas as pl
from jax.experimental.pallas import tpu as pltpu
from jax.sharding import PartitionSpec as P

HEADS = 8
EPS = 1e-05
LANES = 128
VMEM_LIMIT = 22 * 1024 * 1024
SLOT_FLOPS = 8 * 10**9
F32 = jnp.float32
BF16 = jnp.bfloat16
GELU_IN = 0.7978845608028654
GELU_CUBE = 0.044715 * GELU_IN

BIAS, OUT_BIAS, GAIN, SHIFT, RESID_SQ, BRANCH_SQ, COUNT, SMALLS = 0, 4, 5, 6, 7, 8, 9, 16


def dot_nn(left, right):
    return jnp.dot(left, right, preferred_element_type=F32)


def dot_nt(left, right):
    return lax.dot_general(left, right, (((1,), (1,)), ((), ())), preferred_element_type=F32)


def kernel_call(
    body, meta, ins, outs, scratch=(), kept=(), copies=0, hbm_ins=(), smem_ins=(), hbm_outs=(), where=None,
    after=(), flops=1,
):
    ins = [*ins, *after]
    n_in, n_kept, n_out = len(ins), len(kept), len(outs)

    def kernel(z_ref, d_ref, *refs):
        at = 0
        groups = []
        for n in (n_in, n_kept, n_out, n_kept):
            groups.append(refs[at : at + n])
            at += n

        def run():
            body((z_ref[0], d_ref[0]), groups[0][: n_in - len(after)], groups[2], groups[3], refs[at:])

        if where is None:
            run()
        else:
            here = z_ref[0] == where[0]
            for other in where[1:]:
                here = here | (z_ref[0] == other)
            pl.when(here)(run)

    smem = pl.BlockSpec(memory_space=pltpu.SMEM)
    vmem = pl.BlockSpec(memory_space=pltpu.VMEM)
    hbm = pl.BlockSpec(memory_space=pltpu.HBM)

    def held(x, space=pltpu.VMEM):
        return pltpu.with_memory_space_constraint(x, space)

    results = pl.pallas_call(
        kernel,
        out_shape=[
            jax.ShapeDtypeStruct(*o) if i in hbm_outs else pltpu.VMEM(*o) for i, o in enumerate(outs)
        ]
        + [pltpu.VMEM(k.shape, k.dtype) for k in kept],
        in_specs=[smem] * 2
        + [smem if i in smem_ins else hbm if i in hbm_ins else vmem for i in range(n_in)]
        + [vmem] * n_kept,
        out_specs=[hbm if i in hbm_outs else vmem for i in range(n_out)] + [vmem] * n_kept,
        scratch_shapes=[pltpu.VMEM(*s) for s in scratch]
        + ([pltpu.SemaphoreType.DMA((copies,))] if copies else []),
        input_output_aliases={2 + n_in + i: n_out + i for i in range(n_kept)},
        compiler_params=pltpu.CompilerParams(vmem_limit_bytes=VMEM_LIMIT),
        cost_estimate=pl.CostEstimate(flops=flops, bytes_accessed=1, transcendentals=1),
    )(
        *meta,
        *[
            x if i in smem_ins else held(x, pltpu.HBM if i in hbm_ins else pltpu.VMEM)
            for i, x in enumerate(ins)
        ],
        *[held(k) for k in kept],
    )
    return tuple(results[:n_out]), tuple(results[n_out:])


def norm_forward(inputs, branch, seq_len, gain, shift):
    resid = inputs.astype(F32) + branch
    mean = jnp.mean(resid, axis=-1, keepdims=True)
    centred = resid - mean
    var = jnp.mean(centred * centred, axis=-1, keepdims=True)
    inv_std = lax.rsqrt(var + EPS)
    xhat = centred * inv_std
    row = lax.broadcasted_iota(jnp.int32, resid.shape, 0)
    live = row < seq_len
    resid_sq = jnp.sum(jnp.where(live, resid * resid, 0.0), axis=0, keepdims=True)
    branch_sq = jnp.sum(jnp.where(live, branch * branch, 0.0), axis=0, keepdims=True)
    return (xhat * gain + shift).astype(BF16), xhat, inv_std, resid_sq, branch_sq


def norm_backward(grad, xhat, inv_std, gain):
    grad = grad.astype(F32)
    gy = grad * gain
    first = jnp.mean(gy, axis=-1, keepdims=True)
    second = jnp.mean(gy * xhat, axis=-1, keepdims=True)
    dresid = (gy - first - xhat * second) * inv_std
    gain_sum = jnp.sum(grad * xhat, axis=0, keepdims=True)
    shift_sum = jnp.sum(grad, axis=0, keepdims=True)
    return dresid, gain_sum, shift_sum


class Vectors:
    def __init__(self, in_bias, out_bias, gain, shift, low_bias=None):
        self.refs = (in_bias, out_bias, gain, shift, low_bias)

    def in_bias(self, i, width):
        return self.refs[0][0:1, i * width : (i + 1) * width].astype(F32)

    def first_bias(self, i, width):
        return self.refs[4][0:1, :width].astype(F32) if i == 0 else self.in_bias(i - 1, width)

    out_bias = property(lambda self: self.refs[1][...].astype(F32))
    gain = property(lambda self: self.refs[2][...].astype(F32))
    shift = property(lambda self: self.refs[3][...].astype(F32))


class Store:
    def __init__(self, kept, j):
        acts, wide, aux, xhat, inv_std, grad_wide, grad_branch, sums = kept[:8]
        self.x, self.wide, self.aux, self.xhat, self.inv_std, self.gwide, self.db = (
            a.at[j] for a in (acts, wide, aux, xhat, inv_std, grad_wide, grad_branch)
        )
        self.sums, self.first = sums, j == 0

    def add(self, row, value):
        if self.first:
            self.sums[row : row + 1, :] = value
        else:
            self.sums[row : row + 1, :] = self.sums[row : row + 1, :] + value


def attend_forward(inputs, w, vec, seq_len, st, send, scratch):
    vt, ctxt = scratch[:2]
    rows, width = inputs.shape
    size = width // HEADS
    st.x[...] = inputs
    q = (dot_nn(inputs, w[:, :width]) + vec.in_bias(0, width)).astype(BF16)
    st.wide[:, :width] = q * jnp.asarray(size**-0.5, BF16)
    st.wide[:, width : 2 * width] = dot_nn(inputs, w[:, width : 2 * width]).astype(BF16)
    v = (dot_nn(inputs, w[:, 2 * width : 3 * width]) + vec.in_bias(1, width)).astype(BF16)
    st.wide[:, 2 * width : 3 * width] = v
    vt[...] = v.T
    key_live = lax.broadcasted_iota(jnp.int32, (rows, rows), 0) < seq_len
    lane = lax.broadcasted_iota(jnp.int32, (rows, 2 * size), 1)
    for pair in range(HEADS // 2):
        cols = slice(2 * size * pair, 2 * size * (pair + 1))
        qp = st.wide[:, cols]
        kp = st.wide[:, width + cols.start : width + cols.stop]
        for half in range(2):
            head = 2 * pair + half
            mine = (lane >= size) if half else (lane < size)
            scores = dot_nt(jnp.where(mine, kp, jnp.zeros_like(kp)), qp)
            scores = jnp.where(key_live, scores, -1e30)
            top = jnp.max(scores, axis=0, keepdims=True)
            expo = jnp.exp(scores - top)
            total = jnp.sum(expo, axis=0, keepdims=True)
            probs = (expo * (1.0 / total)).astype(BF16)
            st.aux[:, head * rows : (head + 1) * rows] = probs
            ctxt[head * size : (head + 1) * size, :] = dot_nn(
                vt[head * size : (head + 1) * size, :], probs
            ).astype(BF16)
    ctx = ctxt[...].T
    st.wide[:, 3 * width :] = ctx
    branch = dot_nn(ctx, w[:, 3 * width :]) + vec.out_bias
    y, xhat, inv_std, resid_sq, branch_sq = norm_forward(inputs, branch, seq_len, vec.gain, vec.shift)
    send[...] = y
    st.xhat[...] = xhat
    st.inv_std[...] = jnp.broadcast_to(inv_std, st.inv_std.shape)
    st.add(RESID_SQ, resid_sq)
    st.add(BRANCH_SQ, branch_sq)


def feed_branch(inputs, w, down, vec, st):
    width = inputs.shape[1]
    st.x[...] = inputs
    branch = None
    for c in range(w.shape[1] // width):
        cols = slice(c * width, (c + 1) * width)
        x = dot_nn(inputs, w[:, cols]) + vec.first_bias(c, width)
        square = x * x
        t = jnp.tanh(x * (GELU_IN + GELU_CUBE * square))
        s = 0.5 + 0.5 * t
        act = x * s
        slope = s + act * (1.0 - t) * (GELU_IN + (3.0 * GELU_CUBE) * square)
        hidden = act.astype(BF16)
        st.wide[:, cols] = hidden
        st.aux[:, cols] = slope.astype(BF16)
        part = dot_nt(hidden, down[:, cols])
        branch = part if branch is None else branch + part
    return branch + vec.out_bias


def feed_forward(inputs, w, down, vec, seq_len, st, send):
    branch = feed_branch(inputs, w, down, vec, st)
    y, xhat, inv_std, resid_sq, branch_sq = norm_forward(inputs, branch, seq_len, vec.gain, vec.shift)
    send[...] = y
    st.xhat[...] = xhat
    st.inv_std[...] = jnp.broadcast_to(inv_std, st.inv_std.shape)
    st.add(RESID_SQ, resid_sq)
    st.add(BRANCH_SQ, branch_sq)


def feed_grads(dresid, w, down, st, send):
    width = dresid.shape[1]
    dbranch = dresid.astype(BF16)
    st.db[...] = dbranch
    total = dresid
    for c in range(w.shape[1] // width):
        cols = slice(c * width, (c + 1) * width)
        dhidden = dot_nn(dbranch, down[:, cols])
        dpre = (dhidden * st.aux[:, cols].astype(F32)).astype(BF16)
        st.gwide[:, cols] = dpre
        total = total + dot_nt(dpre, w[:, cols])
    send[...] = total.astype(BF16)


def feed_backward(grad, w, down, vec, st, send):
    dresid, gain_sum, shift_sum = norm_backward(grad, st.xhat[...], st.inv_std[:, 0:1], vec.gain)
    st.add(GAIN, gain_sum)
    st.add(SHIFT, shift_sum)
    feed_grads(dresid, w, down, st, send)


def feed_both(inputs, grad, w, down, vec, seq_len, st, y_out, send):
    branch = feed_branch(inputs, w, down, vec, st)
    y, xhat, inv_std, resid_sq, branch_sq = norm_forward(inputs, branch, seq_len, vec.gain, vec.shift)
    y_out[...] = y
    dresid, gain_sum, shift_sum = norm_backward(grad, xhat, inv_std, vec.gain)
    st.add(RESID_SQ, resid_sq)
    st.add(BRANCH_SQ, branch_sq)
    st.add(GAIN, gain_sum)
    st.add(SHIFT, shift_sum)
    feed_grads(dresid, w, down, st, send)


def attend_backward(grad, w, vec, st, send, scratch):
    kt, dqt, dc = scratch[:3]
    rows, width = grad.shape
    size = width // HEADS
    dresid, gain_sum, shift_sum = norm_backward(grad, st.xhat[...], st.inv_std[:, 0:1], vec.gain)
    st.add(GAIN, gain_sum)
    st.add(SHIFT, shift_sum)
    dbranch = dresid.astype(BF16)
    st.gwide[:, 3 * width :] = dbranch
    dc[...] = dot_nt(dbranch, w[:, 3 * width :]).astype(BF16)
    kt[...] = (st.wide[:, width : 2 * width] * jnp.asarray(size**-0.5, BF16)).T
    lane = lax.broadcasted_iota(jnp.int32, (rows, 2 * size), 1)
    for pair in range(HEADS // 2):
        cols = slice(2 * size * pair, 2 * size * (pair + 1))
        qp = st.wide[:, cols]
        vp = st.wide[:, 2 * width + cols.start : 2 * width + cols.stop]
        dcp = dc[:, cols]
        none = jnp.zeros_like(qp)
        dk = dv = None
        for half in range(2):
            head = 2 * pair + half
            mine = (lane >= size) if half else (lane < size)
            probs_low = st.aux[:, head * rows : (head + 1) * rows]
            probs = probs_low.astype(F32)
            dprobs = dot_nt(jnp.where(mine, vp, none), dcp)
            inner = jnp.sum(probs * dprobs, axis=0, keepdims=True)
            dscores = (probs * (dprobs - inner)).astype(BF16)
            dv_part = dot_nn(probs_low, jnp.where(mine, dcp, none))
            dk_part = dot_nn(dscores, jnp.where(mine, qp, none))
            dqt[head * size : (head + 1) * size, :] = dot_nn(
                kt[head * size : (head + 1) * size, :], dscores
            ).astype(BF16)
            dv = dv_part if dv is None else dv + dv_part
            dk = dk_part if dk is None else dk + dk_part
        st.gwide[:, width + cols.start : width + cols.stop] = dk.astype(BF16)
        st.gwide[:, 2 * width + cols.start : 2 * width + cols.stop] = dv.astype(BF16)
    st.gwide[:, :width] = dqt[...].T
    send[...] = (dresid + dot_nt(st.gwide[:, : 3 * width], w[:, : 3 * width])).astype(BF16)


def roles_of(slot, segments):
    last = segments - 1
    found = []
    for z in range(segments):
        j = slot - 2 * z
        if 0 <= j < segments:
            found.append((z, "both" if z == last else "forward", j))
        j = slot - (4 * last - 2 * z)
        if z < last and 0 <= j < segments:
            found.append((z, "backward", j))
    return found


def half_rows(meta, own, width):
    bit = lax.rem(meta[1], 2)
    bit = bit if own else 1 - bit
    return pl.multiple_of(bit * (width // 2), width // 2)


def load_turned(at, source, lanes):
    for j in range(source.shape[0]):
        rows = source.shape[1]
        at[: lanes.size, j * rows : (j + 1) * rows] = source[j, :, lanes].T


def weight_refs(lengths, kept):
    acts, wide, _, _, _, grad_wide, grad_branch, sums = kept[:8]
    return [lengths, acts, wide, grad_wide, grad_branch, sums]


def main_half(own, feed):
    def body(meta, ins, outs, kept, scratch):
        lengths, acts, wide, grad_wide, grad_branch, sums = ins
        (out,) = kept or outs
        at, sm = scratch
        count, rows, width = acts.shape
        half, full, total = width // 2, wide.shape[2], count * rows
        start = half_rows(meta, own, width)
        mine = pl.ds(start, half)
        sm[...] = jnp.zeros_like(sm)
        sm[:SMALLS, :] = sums[...]
        tokens = jnp.sum(lengths[:, 0:1].astype(F32), axis=0, keepdims=True)
        sm[COUNT : COUNT + 1, :] = jnp.broadcast_to(tokens, (1, width))
        at[half:, :] = jnp.ones((at.shape[0] - half, total), BF16)
        load_turned(at, acts, mine)
        grads = grad_wide[...].reshape(total, full)
        for c in range(full // width):
            cols = slice(c * width, (c + 1) * width)
            if c == 3 and not feed:
                load_turned(at, wide, pl.ds(pl.multiple_of(3 * width + start, half), half))
            grad = dot_nn(at[...], grads[:, cols])
            out[:, cols] = grad[:half].astype(BF16)
            place = BIAS + (3, 0, 1, 2)[c] if feed else (BIAS, None, BIAS + 1, OUT_BIAS)[c]
            if place is not None:
                sm[place : place + 1, :] = grad[half : half + 1]
        if feed:
            sm[OUT_BIAS : OUT_BIAS + 1, :] = jnp.sum(
                grad_branch[...].reshape(total, width).astype(F32), axis=0, keepdims=True
            )
        out[:, full:] = sm[:, mine].T.astype(BF16)

    return body


def side_half(own):
    def body(meta, ins, outs, kept, scratch):
        wide, grad_wide, grad_branch = ins[:3]
        (out,) = kept or outs
        at, sm = scratch
        count, rows, width = grad_branch.shape
        half, full, total = width // 2, wide.shape[2], count * rows
        mine = pl.ds(half_rows(meta, own, width), half)
        sm[...] = jnp.broadcast_to(
            jnp.sum(
                grad_wide[:, :, :width].reshape(total, width).astype(F32), axis=0, keepdims=True
            ),
            sm.shape,
        )
        out[:, full // 2 : full // 2 + LANES] = sm[:, mine].T.astype(BF16)
        load_turned(at, grad_branch, mine)
        hid = wide[...].reshape(total, full)
        for c in range(full // width):
            cols = slice(c * width, (c + 1) * width)
            grad = dot_nn(at[:half, :], hid[:, cols]).astype(BF16)
            put = c * width + (LANES if c * width >= full // 2 else 0)
            out[:, put : put + width] = grad

    return body


def core_add(masks):
    def body(meta, ins, outs, kept, scratch):
        size = outs[0].shape[0]
        chip = lax.div(meta[1], 2)
        for mask, out in zip(masks, outs, strict=True):
            rows = pl.ds(pl.multiple_of(jnp.bitwise_xor(chip, mask // 2) * size, size), size)
            at = 0
            for keep, got in zip(ins[0::2], ins[1::2], strict=True):
                cols = slice(at, at + keep.shape[1])
                at += keep.shape[1]
                out[:, cols] = (keep[rows, :].astype(F32) + got[rows, :].astype(F32)).astype(BF16)

    return body


def summed(refs, cols):
    total = refs[0][:, cols].astype(F32)
    for r in refs[1:]:
        total = total + r[:, cols].astype(F32)
    return total.astype(BF16)


def chip_sum(meta, ins, outs, kept, scratch):
    at = 0
    for out in outs:
        out[...] = summed(ins, slice(at, at + out.shape[1]))
        at += out.shape[1]


def payload(meta, ins, outs, kept, scratch):
    total, high, low_got = ins
    (out,) = outs
    main = total.shape[1]
    half = high.shape[1]
    out[:, : main - LANES] = total[:, : main - LANES]
    small = total[:, main - LANES :]

    @pl.when(lax.rem(meta[0], 2) == 1)
    def _():
        out[:, main - LANES : main] = small
        out[:, main:] = high[...]

    @pl.when(lax.rem(meta[0], 2) == 0)
    def _():
        lane = lax.broadcasted_iota(jnp.int32, small.shape, 1)
        out[:, main - LANES : main] = jnp.where(lane == BIAS + 2, low_got[:, half:], small)
        out[:, main:] = low_got[:, :half]


def block_row(meta, mask, width, size):
    chip, core = lax.div(meta[1], 2), lax.rem(meta[1], 2)
    side = jnp.bitwise_xor(core, mask % 2)
    at = side * (width // 2) + jnp.bitwise_xor(chip, mask // 2) * size
    return pl.multiple_of(at, size)


def begin(meta, ins, outs, kept, scratch):
    lens, side, in_bias, *rest = ins
    share, zero_sums, lens_v, bias_v, *outs = outs
    sems = scratch[-1]
    width, block = side.shape[0], share.shape[0] - 16
    rows = pl.ds(half_rows(meta, True, width), block)
    pairs = [(in_bias, bias_v), (side.at[rows], share.at[:block])]
    pairs += list(zip(rest, outs[: len(rest)], strict=True))
    copies = [pltpu.make_async_copy(src, dst, sems.at[i]) for i, (src, dst) in enumerate(pairs)]
    for c in copies:
        c.start()
    zero_sums[...] = jnp.zeros_like(zero_sums)
    for j in range(lens_v.shape[0]):
        lens_v[j : j + 1, :] = jnp.full((1, LANES), lens[j], jnp.int32)
    share[block:, width:] = jnp.zeros((16, share.shape[1] - width), BF16)
    copies[0].wait()
    share[block:, :width] = jnp.broadcast_to(bias_v[:, 2 * width :], (16, width))
    for c in copies[1:]:
        c.wait()


def join_down(meta, ins, outs, kept, scratch):
    lent, other, side = ins
    down, low_bias = outs
    width, half = side.shape
    block = width // 2
    copy = pltpu.make_async_copy(side, down.at[:, half:], scratch[-1].at[0])
    copy.start()
    down[pl.ds(half_rows(meta, True, width), block), :half] = lent[:block]
    down[pl.ds(half_rows(meta, False, width), block), :half] = other[:block]
    low_bias[...] = lent[block:, :width]
    copy.wait()


def widen(masks, segments):
    def body(meta, ins, outs, kept, scratch):
        n = len(masks)
        blocks, finals, backs = ins[:n], ins[n : n + segments], ins[n + segments :]
        out_y, out_g, main_h, side_h, in_b, out_b, gain_h, shift_h, stats_h = outs
        full_m, full_s, cols, vecs, stat, sems = scratch
        used = [0]
        copies = []

        def out(src, dst):
            copy = pltpu.make_async_copy(src, dst, sems.at[used[0]])
            used[0] += 1
            copy.start()
            copies.append(copy)

        def picked(refs, dst):
            at = used[0]
            used[0] += 1
            for j, r in enumerate(refs):

                @pl.when(meta[0] == j)
                def _(r=r):
                    pltpu.make_async_copy(r, dst, sems.at[at]).start()

            copies.append(pltpu.make_async_copy(refs[0], dst, sems.at[at]))

        picked(finals, out_y)
        picked(backs, out_g)
        width, main = main_h.shape[1], main_h.shape[2]
        half = side_h.shape[2]
        size = blocks[0].shape[0]
        for i, mask in enumerate(masks):
            at = block_row(meta, mask, width, size)
            cols[pl.ds(at, size), :] = blocks[i][:, main : main + LANES]
        small = cols[...].T.astype(F32)
        vecs[0:1, :width] = small[BIAS : BIAS + 1]
        vecs[0:1, width : 2 * width] = small[BIAS + 1 : BIAS + 2]
        vecs[0:1, 2 * width :] = small[BIAS + 2 : BIAS + 3]
        vecs[1:2, :width] = small[OUT_BIAS : OUT_BIAS + 1]
        vecs[2:3, :width] = small[GAIN : GAIN + 1]
        vecs[3:4, :width] = small[SHIFT : SHIFT + 1]
        squares = jnp.sum(small[RESID_SQ : BRANCH_SQ + 1], axis=1, keepdims=True)
        values = jnp.sqrt(squares / (small[COUNT : COUNT + 1, 0:1] * width))
        lane = lax.broadcasted_iota(jnp.int32, (1, LANES), 1)
        stat[...] = jnp.where(lane == 0, values[0:1], values[1:2])
        out(vecs.at[0:1], in_b)
        out(vecs.at[1:2, :width], out_b)
        out(vecs.at[2:3, :width], gain_h)
        out(vecs.at[3:4, :width], shift_h)
        out(stat, stats_h)
        for i, mask in enumerate(masks):
            at = block_row(meta, mask, width, size)
            full_m[i] = blocks[i][:, :main].astype(F32)
            out(full_m.at[i], main_h.at[0, pl.ds(at, size)])
            full_s[i] = blocks[i][:, main + LANES : main + LANES + half].astype(F32)
            out(full_s.at[i], side_h.at[0, pl.ds(at, size)])
        for c in copies:
            c.wait()

    return body


def on_device(
    tokens, lengths, cotangent, main_weight, side_weight, in_bias, out_bias, norm_gain, norm_shift
):
    segments, shards = lax.axis_size("segment"), lax.axis_size("dp")
    z, d = lax.axis_index("segment"), lax.axis_index("dp")
    rows, width = tokens.shape
    main_mat, side_mat = main_weight[0], side_weight[0]
    hidden = main_mat.shape[1]
    half_width = side_mat.shape[1]
    block = width // shards
    last = segments - 1
    feeds = tuple(range(1, segments, 2))
    chip_masks = tuple(range(0, shards, 2))
    masks = chip_masks + tuple(m + 1 for m in chip_masks)
    meta = (z.reshape(1), d.reshape(1))

    def hop(value, *pairs):
        return lax.ppermute(value, "segment", list(pairs))

    def swap(value, mask, where=None):
        if where is None:
            return lax.ppermute(value, "dp", [(i, i ^ mask) for i in range(shards)])
        pairs = [(s * shards + i, s * shards + (i ^ mask)) for s in where for i in range(shards)]
        return lax.ppermute(value, ("segment", "dp"), pairs)

    ext = hidden + LANES
    low_ext = half_width + LANES
    kept_shapes = [
        ((segments, rows, width), BF16),
        ((segments, rows, hidden), BF16),
        ((segments, rows, hidden), BF16),
        ((segments, rows, width), F32),
        ((segments, rows, LANES), F32),
        ((segments, rows, hidden), BF16),
        ((segments, rows, width), BF16),
    ]
    lent = ((width // 2 + 16, half_width), BF16)
    narrow = ((rows, width), BF16)
    loads = [out_bias, norm_gain, norm_shift, main_mat, tokens, cotangent]
    loaded, _ = kernel_call(
        begin, meta, [lengths.reshape(segments), side_mat, in_bias, *loads],
        [lent, ((SMALLS, width), F32), ((segments, LANES), jnp.int32), (in_bias.shape, BF16)]
        + [(x.shape, x.dtype) for x in loads]
        + kept_shapes,
        copies=2 + len(loads), smem_ins=(0,), hbm_ins=tuple(range(1, 3 + len(loads))),
    )
    share, sums, lengths_v, bias_v, out_bias_v, gain_v, shift_v, main_v, tokens_v, cotangent_v, *kept = loaded
    kept = (*kept, sums)

    turns = (0, *range(last, 0, -1))
    share = hop(share, *[(s - 1, s) for s in feeds])
    first_in = [tokens_v, hop(tokens_v, (turns[1], 0))]
    riders = {
        0: [(turns[2], 0, "tokens"), (turns[3], last, "cotangent")],
        1: [(turns[3], 0, "tokens"), (turns[2], last, "cotangent")],
    }

    turned = ((width, rows), BF16)
    n_chip = len(chip_masks)
    weight_scratch = [((width // 2 + 16, segments * rows), BF16), ((LANES, width), F32)]

    slots = 4 * last + segments
    waves, sent, finals = {}, {}, []
    after, last_in = {}, []
    main, side = [], []
    half_out = ((width // 2, ext), BF16)

    def hops_after(slot):
        pairs = []
        for z_role, what, j in roles_of(slot, segments):
            if what == "forward":
                pairs.append((z_role, z_role + 1))
            elif z_role > 0:
                pairs.append((z_role, z_role - 1))
            elif turns[j] > 0:
                pairs.append((z_role, turns[j]))
        return pairs + [(source, to) for source, to, _ in riders.get(slot, ())]

    homeward = {}
    for slot in range(2 * last + segments, slots):
        taken = [to for _, to in hops_after(slot)]
        free = [home for home in range(1, last) if home not in taken and home not in homeward.values()]
        if free:
            homeward[slot] = free[-1]
    for slot in range(slots):
        roles = roles_of(slot, segments)
        uses = [r[1] for r in roles]
        attends = any(r[0] % 2 == 0 for r in roles)
        feed_roles = any(r[0] % 2 == 1 for r in roles)
        names, ins = [], []

        def give(name, value):
            names.append(name)
            ins.append(value)

        for name, value in zip(
            ("main", "in_bias", "out_bias", "gain", "shift", "lengths"),
            (main_v, bias_v, out_bias_v, gain_v, shift_v, lengths_v),
        ):
            give(name, value)
        if feed_roles:
            give("down", down)
            give("low_bias", low_bias)
        if slot < 2:
            give("first", first_in[slot])
            give("tokens", tokens_v)
            give("cotangent", cotangent_v)
        if slot - 2 in waves:
            give("wave", waves[slot - 2])
        if "both" in uses:
            give("last", last_in[slot - 2 * last])
        if slot in homeward:
            give("home", finals[turns.index(homeward[slot])])
        outs = [narrow] + ([narrow] if "both" in uses else [])
        weighing = slots - 2 <= slot
        if weighing:
            outs += [half_out, half_out]

        def body(meta, in_refs, out_refs, kept_refs, scratch, roles=roles, names=tuple(names)):
            ref = dict(zip(names, in_refs))
            vec = Vectors(
                ref["in_bias"], ref["out_bias"], ref["gain"], ref["shift"], ref.get("low_bias")
            )
            for z_role, what, j in roles:

                @pl.when(meta[0] == z_role)
                def _(z_role=z_role, what=what, j=j):
                    st = Store(kept_refs, j)
                    seq_len = ref["lengths"][turns[j] : turns[j] + 1, 0:1]
                    w, send = ref["main"], out_refs[0]
                    if what == "backward":
                        if z_role % 2:
                            feed_backward(ref["wave"][...], w, ref["down"], vec, st, send)
                        else:
                            attend_backward(ref["wave"][...], w, vec, st, send, scratch)
                        return
                    inputs = ref.get("first", ref.get("wave"))[...]
                    if what == "both":
                        feed_both(
                            inputs, ref["last"][...], w, ref["down"], vec, seq_len, st, out_refs[1], send
                        )
                    elif z_role % 2:
                        feed_forward(inputs, w, ref["down"], vec, seq_len, st, send)
                    else:
                        attend_forward(inputs, w, vec, seq_len, st, send, scratch)

            for source, _, what in riders.get(slot, ()):

                @pl.when(meta[0] == source)
                def _(what=what):
                    out_refs[0][...] = ref[what][...]

            if "home" in ref:

                @pl.when(meta[0] == last)
                def _():
                    out_refs[0][...] = ref["home"][...]

            if weighing:
                own = slot == slots - 2
                feed_here = lax.rem(meta[0], 2) == 1
                main_out, side_out = out_refs[-2:]
                sums = weight_refs(ref["lengths"], kept_refs)

                @pl.when(feed_here)
                def _():
                    side_half(own)(meta, sums[2:], [side_out], (), scratch[-2:])
                    main_half(own, True)(meta, sums, [main_out], (), scratch[-2:])

                @pl.when(jnp.logical_not(feed_here) & (meta[0] > 0))
                def _():
                    main_half(own, False)(meta, sums, [main_out], (), scratch[-2:])

        scratch = [turned, turned, narrow] if attends else []
        if weighing:
            scratch = scratch + weight_scratch
        extra = (finals[0],) if slot == slots - 1 else (cotangent_v,) if slot == last else ()
        res, kept = kernel_call(
            body, meta, ins, outs, scratch, (*kept, *extra), after=after.get(slot, ()), flops=SLOT_FLOPS
        )
        if slot == last:
            kept, cotangent_v = kept[:-1], kept[-1]
            last_in = [hop(cotangent_v, (0, last)), cotangent_v, waves[1], waves[0]]
        if slot == slots - 1:
            kept, first_final = kept[:-1], kept[-1]
        if slot == 0:
            _, kept = kernel_call(lambda *_: None, meta, [], [], kept=kept, after=[first_in[1]])
            (down, low_bias), _ = kernel_call(
                join_down, meta, [share, swap(share, 1, feeds), side_mat],
                [((width, hidden), BF16), ((16, width), BF16)], hbm_ins=(2,), copies=1, where=feeds,
            )
        sent[slot] = res[0]
        if weighing:
            main.insert(0, res[-2])
            side.insert(0, res[-1])
        if "both" in uses:
            finals.append(res[1])
        pairs = hops_after(slot)
        if slot in homeward:
            pairs.append((last, homeward[slot]))
        if pairs:
            waves[slot] = hop(res[0], *pairs)
    first_home = hop(first_final, (last, 0))
    outputs_at = [first_home] + [
        waves[next(k for k, v in homeward.items() if v == s)] for s in range(1, last)
    ]
    outputs_at.append(finals[turns.index(last)])
    start = slots - segments
    grads_at = [sent[start]] + [waves[start + turns.index(s)] for s in range(1, segments)]

    def weigh(own, after):
        _, (main[own],) = kernel_call(
            main_half(bool(own), False), meta, weight_refs(lengths_v, kept), [], weight_scratch,
            (main[own],), where=(0,), after=after,
        )

    def add_cores(keep, got, segs, after=()):
        return kernel_call(
            core_add(chip_masks), meta, [keep, got], [((block, ext), BF16)] * n_chip, where=segs, after=after
        )[0]

    def to_chips(blocks, segs):
        return [blocks[0]] + [swap(b, m, segs) for b, m in zip(blocks[1:], chip_masks[1:])]

    waves_home = [waves[slots - 2], waves[slots - 1]]
    side_got = swap(side[0], 1, feeds)
    weigh(0, [side_got])
    main_got = swap(main[0], 1)
    side_blocks = add_cores(side[1], side_got, feeds, [main[0]])
    weigh(1, [side_blocks[0]])
    main_blocks = add_cores(main[1], main_got, None)
    (low_own, high_own), _ = kernel_call(
        chip_sum, meta, to_chips(side_blocks, feeds), [((block, low_ext), BF16), ((block, half_width), BF16)],
        where=feeds,
    )
    (total,), _ = kernel_call(
        chip_sum, meta, to_chips(main_blocks, None), [((block, ext), BF16)], after=waves_home
    )
    low_got = hop(low_own, *[(s, s - 1) for s in feeds])
    (mine,), _ = kernel_call(
        payload, meta, [total, high_own, low_got], [((block, ext + half_width), BF16)],
        after=[first_home],
    )

    gathered = [mine] + [swap(mine, m) for m in chip_masks[1:]]
    gathered += [swap(b, 1) for b in gathered]

    results, _ = kernel_call(
        widen(masks, segments), meta, [*gathered, *outputs_at, *grads_at],
        [
            narrow, narrow,
            ((1, width, hidden), F32), ((1, width, half_width), F32), ((1, 3 * width), F32),
            ((1, width), F32), ((1, width), F32), ((1, width), F32), ((1, LANES), F32),
        ],
        [
            ((shards, block, hidden), F32), ((shards, block, half_width), F32),
            ((width, LANES), BF16), ((8, 3 * width), F32), ((1, LANES), F32),
        ],
        copies=2 * shards + 8,
        hbm_outs=tuple(range(9)),
    )
    return (*results[:8], results[8][:, :2])


def solution(mesh):
    over = P(("segment", "dp"), None)
    by_segment = [P("segment", None, None)] * 2 + [P("segment", None)] * 4
    in_specs = (over, P(None, "dp"), over, *by_segment)
    out_specs = (over, over, *by_segment, P("segment", None))
    return jax.shard_map(
        on_device, mesh=mesh, in_specs=in_specs, out_specs=out_specs, check_vma=False
    )
```

```python
import functools

import jax
import jax.numpy as jnp
from jax import lax
from jax.experimental import pallas as pl
from jax.experimental.pallas import tpu as pltpu
from jax.sharding import PartitionSpec as P

HEADS = 8
EPS = 1e-05
LANES = 128
VMEM_LIMIT = 22 * 1024 * 1024
SLOT_FLOPS = 40 * 10**9
F32 = jnp.float32
BF16 = jnp.bfloat16
GELU_IN = 0.7978845608028654
GELU_CUBE = 0.044715 * GELU_IN

BIAS, OUT_BIAS, GAIN, SHIFT, RESID_SQ, BRANCH_SQ, COUNT, SMALLS = 0, 4, 5, 6, 7, 8, 9, 16


def dot_nn(left, right):
    return jnp.dot(left, right, preferred_element_type=F32)


def dot_nt(left, right):
    return lax.dot_general(left, right, (((1,), (1,)), ((), ())), preferred_element_type=F32)


def kernel_call(
    body, meta, ins, outs, scratch=(), kept=(), copies=0, hbm_ins=(), smem_ins=(), hbm_outs=(), where=None,
    after=(), flops=1,
):
    ins = [*ins, *after]
    n_in, n_kept, n_out = len(ins), len(kept), len(outs)

    def kernel(z_ref, d_ref, *refs):
        at = 0
        groups = []
        for n in (n_in, n_kept, n_out, n_kept):
            groups.append(refs[at : at + n])
            at += n

        def run():
            body((z_ref[0], d_ref[0]), groups[0][: n_in - len(after)], groups[2], groups[3], refs[at:])

        if where is None:
            run()
        else:
            here = z_ref[0] == where[0]
            for other in where[1:]:
                here = here | (z_ref[0] == other)
            pl.when(here)(run)

    smem = pl.BlockSpec(memory_space=pltpu.SMEM)
    vmem = pl.BlockSpec(memory_space=pltpu.VMEM)
    hbm = pl.BlockSpec(memory_space=pltpu.HBM)

    def held(x, space=pltpu.VMEM):
        return pltpu.with_memory_space_constraint(x, space)

    results = pl.pallas_call(
        kernel,
        out_shape=[
            jax.ShapeDtypeStruct(*o) if i in hbm_outs else pltpu.VMEM(*o) for i, o in enumerate(outs)
        ]
        + [pltpu.VMEM(k.shape, k.dtype) for k in kept],
        in_specs=[smem] * 2
        + [smem if i in smem_ins else hbm if i in hbm_ins else vmem for i in range(n_in)]
        + [vmem] * n_kept,
        out_specs=[hbm if i in hbm_outs else vmem for i in range(n_out)] + [vmem] * n_kept,
        scratch_shapes=[pltpu.VMEM(*s) for s in scratch]
        + ([pltpu.SemaphoreType.DMA((copies,))] if copies else []),
        input_output_aliases={2 + n_in + i: n_out + i for i in range(n_kept)},
        compiler_params=pltpu.CompilerParams(vmem_limit_bytes=VMEM_LIMIT),
        cost_estimate=pl.CostEstimate(flops=flops, bytes_accessed=1, transcendentals=1),
    )(
        *meta,
        *[
            x if i in smem_ins else held(x, pltpu.HBM if i in hbm_ins else pltpu.VMEM)
            for i, x in enumerate(ins)
        ],
        *[held(k) for k in kept],
    )
    return tuple(results[:n_out]), tuple(results[n_out:])


def norm_forward(inputs, branch, seq_len, gain, shift):
    resid = inputs.astype(F32) + branch
    mean = jnp.mean(resid, axis=-1, keepdims=True)
    centred = resid - mean
    var = jnp.mean(centred * centred, axis=-1, keepdims=True)
    inv_std = lax.rsqrt(var + EPS)
    xhat = centred * inv_std
    row = lax.broadcasted_iota(jnp.int32, resid.shape, 0)
    live = row < seq_len
    resid_sq = jnp.sum(jnp.where(live, resid * resid, 0.0), axis=0, keepdims=True)
    branch_sq = jnp.sum(jnp.where(live, branch * branch, 0.0), axis=0, keepdims=True)
    return (xhat * gain + shift).astype(BF16), xhat, inv_std, resid_sq, branch_sq


def norm_backward(grad, xhat, inv_std, gain):
    grad = grad.astype(F32)
    gy = grad * gain
    first = jnp.mean(gy, axis=-1, keepdims=True)
    second = jnp.mean(gy * xhat, axis=-1, keepdims=True)
    dresid = (gy - first - xhat * second) * inv_std
    gain_sum = jnp.sum(grad * xhat, axis=0, keepdims=True)
    shift_sum = jnp.sum(grad, axis=0, keepdims=True)
    return dresid, gain_sum, shift_sum


class Vectors:
    def __init__(self, in_bias, out_bias, gain, shift, low_bias=None):
        self.refs = (in_bias, out_bias, gain, shift, low_bias)

    def in_bias(self, i, width):
        return self.refs[0][0:1, i * width : (i + 1) * width].astype(F32)

    def first_bias(self, i, width):
        return self.refs[4][0:1, :width].astype(F32) if i == 0 else self.in_bias(i - 1, width)

    out_bias = property(lambda self: self.refs[1][...].astype(F32))
    gain = property(lambda self: self.refs[2][...].astype(F32))
    shift = property(lambda self: self.refs[3][...].astype(F32))


class Store:
    def __init__(self, kept, j):
        acts, wide, aux, xhat, inv_std, grad_wide, grad_branch, sums = kept[:8]
        self.x, self.wide, self.aux, self.xhat, self.inv_std, self.gwide, self.db = (
            a.at[j] for a in (acts, wide, aux, xhat, inv_std, grad_wide, grad_branch)
        )
        self.sums, self.first = sums, j == 0

    def add(self, row, value):
        if self.first:
            self.sums[row : row + 1, :] = value
        else:
            self.sums[row : row + 1, :] = self.sums[row : row + 1, :] + value


def attend_forward(inputs, w, vec, seq_len, st, send, scratch):
    vt, ctxt = scratch[:2]
    rows, width = inputs.shape
    size = width // HEADS
    st.x[...] = inputs
    q = (dot_nn(inputs, w[:, :width]) + vec.in_bias(0, width)).astype(BF16)
    st.wide[:, :width] = q * jnp.asarray(size**-0.5, BF16)
    st.wide[:, width : 2 * width] = dot_nn(inputs, w[:, width : 2 * width]).astype(BF16)
    v = (dot_nn(inputs, w[:, 2 * width : 3 * width]) + vec.in_bias(1, width)).astype(BF16)
    st.wide[:, 2 * width : 3 * width] = v
    vt[...] = v.T
    key_live = lax.broadcasted_iota(jnp.int32, (rows, rows), 0) < seq_len
    lane = lax.broadcasted_iota(jnp.int32, (rows, 2 * size), 1)
    for pair in range(HEADS // 2):
        cols = slice(2 * size * pair, 2 * size * (pair + 1))
        qp = st.wide[:, cols]
        kp = st.wide[:, width + cols.start : width + cols.stop]
        for half in range(2):
            head = 2 * pair + half
            mine = (lane >= size) if half else (lane < size)
            scores = dot_nt(jnp.where(mine, kp, jnp.zeros_like(kp)), qp)
            scores = jnp.where(key_live, scores, -1e30)
            top = jnp.max(scores, axis=0, keepdims=True)
            expo = jnp.exp(scores - top)
            total = jnp.sum(expo, axis=0, keepdims=True)
            probs = (expo * (1.0 / total)).astype(BF16)
            st.aux[:, head * rows : (head + 1) * rows] = probs
            ctxt[head * size : (head + 1) * size, :] = dot_nn(
                vt[head * size : (head + 1) * size, :], probs
            ).astype(BF16)
    ctx = ctxt[...].T
    st.wide[:, 3 * width :] = ctx
    branch = dot_nn(ctx, w[:, 3 * width :]) + vec.out_bias
    y, xhat, inv_std, resid_sq, branch_sq = norm_forward(inputs, branch, seq_len, vec.gain, vec.shift)
    send[...] = y
    st.xhat[...] = xhat
    st.inv_std[...] = jnp.broadcast_to(inv_std, st.inv_std.shape)
    st.add(RESID_SQ, resid_sq)
    st.add(BRANCH_SQ, branch_sq)


def feed_branch(inputs, w, down, vec, st):
    width = inputs.shape[1]
    st.x[...] = inputs
    branch = None
    for c in range(w.shape[1] // width):
        cols = slice(c * width, (c + 1) * width)
        x = dot_nn(inputs, w[:, cols]) + vec.first_bias(c, width)
        square = x * x
        t = jnp.tanh(x * (GELU_IN + GELU_CUBE * square))
        s = 0.5 + 0.5 * t
        act = x * s
        slope = s + act * (1.0 - t) * (GELU_IN + (3.0 * GELU_CUBE) * square)
        hidden = act.astype(BF16)
        st.wide[:, cols] = hidden
        st.aux[:, cols] = slope.astype(BF16)
        part = dot_nt(hidden, down[:, cols])
        branch = part if branch is None else branch + part
    return branch + vec.out_bias


def feed_forward(inputs, w, down, vec, seq_len, st, send):
    branch = feed_branch(inputs, w, down, vec, st)
    y, xhat, inv_std, resid_sq, branch_sq = norm_forward(inputs, branch, seq_len, vec.gain, vec.shift)
    send[...] = y
    st.xhat[...] = xhat
    st.inv_std[...] = jnp.broadcast_to(inv_std, st.inv_std.shape)
    st.add(RESID_SQ, resid_sq)
    st.add(BRANCH_SQ, branch_sq)


def feed_grads(dresid, w, down, st, send):
    width = dresid.shape[1]
    dbranch = dresid.astype(BF16)
    st.db[...] = dbranch
    total = dresid
    for c in range(w.shape[1] // width):
        cols = slice(c * width, (c + 1) * width)
        dhidden = dot_nn(dbranch, down[:, cols])
        dpre = (dhidden * st.aux[:, cols].astype(F32)).astype(BF16)
        st.gwide[:, cols] = dpre
        total = total + dot_nt(dpre, w[:, cols])
    send[...] = total.astype(BF16)


def feed_backward(grad, w, down, vec, st, send):
    dresid, gain_sum, shift_sum = norm_backward(grad, st.xhat[...], st.inv_std[:, 0:1], vec.gain)
    st.add(GAIN, gain_sum)
    st.add(SHIFT, shift_sum)
    feed_grads(dresid, w, down, st, send)


def feed_both(inputs, grad, w, down, vec, seq_len, st, y_out, send):
    branch = feed_branch(inputs, w, down, vec, st)
    y, xhat, inv_std, resid_sq, branch_sq = norm_forward(inputs, branch, seq_len, vec.gain, vec.shift)
    y_out[...] = y
    dresid, gain_sum, shift_sum = norm_backward(grad, xhat, inv_std, vec.gain)
    st.add(RESID_SQ, resid_sq)
    st.add(BRANCH_SQ, branch_sq)
    st.add(GAIN, gain_sum)
    st.add(SHIFT, shift_sum)
    feed_grads(dresid, w, down, st, send)


def attend_backward(grad, w, vec, st, send, scratch):
    kt, dqt, dc = scratch[:3]
    rows, width = grad.shape
    size = width // HEADS
    dresid, gain_sum, shift_sum = norm_backward(grad, st.xhat[...], st.inv_std[:, 0:1], vec.gain)
    st.add(GAIN, gain_sum)
    st.add(SHIFT, shift_sum)
    dbranch = dresid.astype(BF16)
    st.gwide[:, 3 * width :] = dbranch
    dc[...] = dot_nt(dbranch, w[:, 3 * width :]).astype(BF16)
    kt[...] = (st.wide[:, width : 2 * width] * jnp.asarray(size**-0.5, BF16)).T
    lane = lax.broadcasted_iota(jnp.int32, (rows, 2 * size), 1)
    for pair in range(HEADS // 2):
        cols = slice(2 * size * pair, 2 * size * (pair + 1))
        qp = st.wide[:, cols]
        vp = st.wide[:, 2 * width + cols.start : 2 * width + cols.stop]
        dcp = dc[:, cols]
        none = jnp.zeros_like(qp)
        dk = dv = None
        for half in range(2):
            head = 2 * pair + half
            mine = (lane >= size) if half else (lane < size)
            probs_low = st.aux[:, head * rows : (head + 1) * rows]
            probs = probs_low.astype(F32)
            dprobs = dot_nt(jnp.where(mine, vp, none), dcp)
            inner = jnp.sum(probs * dprobs, axis=0, keepdims=True)
            dscores = (probs * (dprobs - inner)).astype(BF16)
            dv_part = dot_nn(probs_low, jnp.where(mine, dcp, none))
            dk_part = dot_nn(dscores, jnp.where(mine, qp, none))
            dqt[head * size : (head + 1) * size, :] = dot_nn(
                kt[head * size : (head + 1) * size, :], dscores
            ).astype(BF16)
            dv = dv_part if dv is None else dv + dv_part
            dk = dk_part if dk is None else dk + dk_part
        st.gwide[:, width + cols.start : width + cols.stop] = dk.astype(BF16)
        st.gwide[:, 2 * width + cols.start : 2 * width + cols.stop] = dv.astype(BF16)
    st.gwide[:, :width] = dqt[...].T
    send[...] = (dresid + dot_nt(st.gwide[:, : 3 * width], w[:, : 3 * width])).astype(BF16)


def roles_of(slot, segments):
    last = segments - 1
    found = []
    for z in range(segments):
        j = slot - 2 * z
        if 0 <= j < segments:
            found.append((z, "both" if z == last else "forward", j))
        j = slot - (4 * last - 2 * z)
        if z < last and 0 <= j < segments:
            found.append((z, "backward", j))
    return found


def half_rows(meta, own, width):
    bit = lax.rem(meta[1], 2)
    bit = bit if own else 1 - bit
    return pl.multiple_of(bit * (width // 2), width // 2)


def load_turned(at, source, lanes):
    for j in range(source.shape[0]):
        rows = source.shape[1]
        at[: lanes.size, j * rows : (j + 1) * rows] = source[j, :, lanes].T


def weight_refs(lengths, kept):
    acts, wide, _, _, _, grad_wide, grad_branch, sums = kept[:8]
    return [lengths, acts, wide, grad_wide, grad_branch, sums]


def main_half(own, feed):
    def body(meta, ins, outs, kept, scratch):
        lengths, acts, wide, grad_wide, grad_branch, sums = ins
        (out,) = kept or outs
        at, sm = scratch
        count, rows, width = acts.shape
        half, full, total = width // 2, wide.shape[2], count * rows
        start = half_rows(meta, own, width)
        mine = pl.ds(start, half)
        sm[...] = jnp.zeros_like(sm)
        sm[:SMALLS, :] = sums[...]
        tokens = jnp.sum(lengths[:, 0:1].astype(F32), axis=0, keepdims=True)
        sm[COUNT : COUNT + 1, :] = jnp.broadcast_to(tokens, (1, width))
        at[half:, :] = jnp.ones((at.shape[0] - half, total), BF16)
        load_turned(at, acts, mine)
        grads = grad_wide[...].reshape(total, full)
        for c in range(full // width):
            cols = slice(c * width, (c + 1) * width)
            if c == 3 and not feed:
                load_turned(at, wide, pl.ds(pl.multiple_of(3 * width + start, half), half))
            grad = dot_nn(at[...], grads[:, cols])
            out[:, cols] = grad[:half].astype(BF16)
            place = BIAS + (3, 0, 1, 2)[c] if feed else (BIAS, None, BIAS + 1, OUT_BIAS)[c]
            if place is not None:
                sm[place : place + 1, :] = grad[half : half + 1]
        if feed:
            sm[OUT_BIAS : OUT_BIAS + 1, :] = jnp.sum(
                grad_branch[...].reshape(total, width).astype(F32), axis=0, keepdims=True
            )
        out[:, full:] = sm[:, mine].T.astype(BF16)

    return body


def side_half(own):
    def body(meta, ins, outs, kept, scratch):
        wide, grad_wide, grad_branch = ins[:3]
        (out,) = kept or outs
        at, sm = scratch
        count, rows, width = grad_branch.shape
        half, full, total = width // 2, wide.shape[2], count * rows
        mine = pl.ds(half_rows(meta, own, width), half)
        sm[...] = jnp.broadcast_to(
            jnp.sum(
                grad_wide[:, :, :width].reshape(total, width).astype(F32), axis=0, keepdims=True
            ),
            sm.shape,
        )
        out[:, full // 2 : full // 2 + LANES] = sm[:, mine].T.astype(BF16)
        load_turned(at, grad_branch, mine)
        hid = wide[...].reshape(total, full)
        for c in range(full // width):
            cols = slice(c * width, (c + 1) * width)
            grad = dot_nn(at[:half, :], hid[:, cols]).astype(BF16)
            put = c * width + (LANES if c * width >= full // 2 else 0)
            out[:, put : put + width] = grad

    return body


def core_add(masks):
    def body(meta, ins, outs, kept, scratch):
        size = outs[0].shape[0]
        chip = lax.div(meta[1], 2)
        for mask, out in zip(masks, outs, strict=True):
            rows = pl.ds(pl.multiple_of(jnp.bitwise_xor(chip, mask // 2) * size, size), size)
            at = 0
            for keep, got in zip(ins[0::2], ins[1::2], strict=True):
                cols = slice(at, at + keep.shape[1])
                at += keep.shape[1]
                out[:, cols] = (keep[rows, :].astype(F32) + got[rows, :].astype(F32)).astype(BF16)

    return body


def summed(refs, cols):
    total = refs[0][:, cols].astype(F32)
    for r in refs[1:]:
        total = total + r[:, cols].astype(F32)
    return total.astype(BF16)


def chip_sum(meta, ins, outs, kept, scratch):
    at = 0
    for out in outs or kept:
        out[...] = summed(ins, slice(at, at + out.shape[1]))
        at += out.shape[1]


def payload(meta, ins, outs, kept, scratch):
    total, high, low_got = ins
    main = total.shape[1]
    half = high.shape[1]
    small = total[:, main - LANES :]

    @pl.when(lax.rem(meta[0], 2) == 1)
    def _():
        for out in outs:
            out[:, : main - LANES] = total[:, : main - LANES]
            out[:, main - LANES : main] = small
            out[:, main:] = high[...]

    @pl.when(lax.rem(meta[0], 2) == 0)
    def _():
        lane = lax.broadcasted_iota(jnp.int32, small.shape, 1)
        for out in outs:
            out[:, : main - LANES] = total[:, : main - LANES]
            out[:, main - LANES : main] = jnp.where(lane == BIAS + 2, low_got[:, half:], small)
            out[:, main:] = low_got[:, :half]


def block_row(meta, mask, width, size):
    chip, core = lax.div(meta[1], 2), lax.rem(meta[1], 2)
    side = jnp.bitwise_xor(core, mask % 2)
    at = side * (width // 2) + jnp.bitwise_xor(chip, mask // 2) * size
    return pl.multiple_of(at, size)


def begin(meta, ins, outs, kept, scratch):
    lens, side, in_bias, *rest = ins
    share, again, zero_sums, lens_v, bias_v, *outs = outs
    sems = scratch[-1]
    width, block = side.shape[0], share.shape[0] - 16
    rows = pl.ds(half_rows(meta, True, width), block)
    pairs = [(in_bias, bias_v), (side.at[rows], share.at[:block]), (side.at[rows], again.at[:block])]
    pairs += list(zip(rest, outs[: len(rest)], strict=True))
    copies = [pltpu.make_async_copy(src, dst, sems.at[i]) for i, (src, dst) in enumerate(pairs)]
    for c in copies:
        c.start()
    zero_sums[...] = jnp.zeros_like(zero_sums)
    for j in range(lens_v.shape[0]):
        lens_v[j : j + 1, :] = jnp.full((1, LANES), lens[j], jnp.int32)
    copies[0].wait()
    for ref in (share, again):
        ref[block:, width:] = jnp.zeros((16, share.shape[1] - width), BF16)
        ref[block:, :width] = jnp.broadcast_to(bias_v[:, 2 * width :], (16, width))
    for c in copies[1:]:
        c.wait()


def join_down(meta, ins, outs, kept, scratch):
    lent, other, side = ins
    down, low_bias = kept
    width, half = side.shape
    block = width // 2
    copy = pltpu.make_async_copy(side, down.at[:, half:], scratch[-1].at[0])
    copy.start()
    down[pl.ds(half_rows(meta, True, width), block), :half] = lent[:block]
    down[pl.ds(half_rows(meta, False, width), block), :half] = other[:block]
    low_bias[...] = lent[block:, :width]
    copy.wait()


def widen(masks, segments):
    def body(meta, ins, outs, kept, scratch):
        n = len(masks)
        blocks, finals, backs = ins[:n], ins[n : n + segments], ins[n + segments :]
        out_y, out_g, main_h, side_h, in_b, out_b, gain_h, shift_h, stats_h = outs
        full_m, full_s, cols, vecs, stat, sems = scratch
        used = [0]
        copies = []

        def out(src, dst):
            copy = pltpu.make_async_copy(src, dst, sems.at[used[0]])
            used[0] += 1
            copy.start()
            copies.append(copy)

        def picked(refs, dst):
            at = used[0]
            used[0] += 1
            for j, r in enumerate(refs):

                @pl.when(meta[0] == j)
                def _(r=r):
                    pltpu.make_async_copy(r, dst, sems.at[at]).start()

            copies.append(pltpu.make_async_copy(refs[0], dst, sems.at[at]))

        picked(finals, out_y)
        picked(backs, out_g)
        width, main = main_h.shape[1], main_h.shape[2]
        half = side_h.shape[2]
        size = blocks[0].shape[0]
        for i, mask in enumerate(masks):
            at = block_row(meta, mask, width, size)
            cols[pl.ds(at, size), :] = blocks[i][:, main : main + LANES]
        small = cols[...].T.astype(F32)
        vecs[0:1, :width] = small[BIAS : BIAS + 1]
        vecs[0:1, width : 2 * width] = small[BIAS + 1 : BIAS + 2]
        vecs[0:1, 2 * width :] = small[BIAS + 2 : BIAS + 3]
        vecs[1:2, :width] = small[OUT_BIAS : OUT_BIAS + 1]
        vecs[2:3, :width] = small[GAIN : GAIN + 1]
        vecs[3:4, :width] = small[SHIFT : SHIFT + 1]
        squares = jnp.sum(small[RESID_SQ : BRANCH_SQ + 1], axis=1, keepdims=True)
        values = jnp.sqrt(squares / (small[COUNT : COUNT + 1, 0:1] * width))
        lane = lax.broadcasted_iota(jnp.int32, (1, LANES), 1)
        stat[...] = jnp.where(lane == 0, values[0:1], values[1:2])
        out(vecs.at[0:1], in_b)
        out(vecs.at[1:2, :width], out_b)
        out(vecs.at[2:3, :width], gain_h)
        out(vecs.at[3:4, :width], shift_h)
        out(stat, stats_h)
        for i, mask in enumerate(masks):
            at = block_row(meta, mask, width, size)
            full_m[i] = blocks[i][:, :main].astype(F32)
            out(full_m.at[i], main_h.at[0, pl.ds(at, size)])
            full_s[i] = blocks[i][:, main + LANES : main + LANES + half].astype(F32)
            out(full_s.at[i], side_h.at[0, pl.ds(at, size)])
        for c in copies:
            c.wait()

    return body


def on_device(
    tokens, lengths, cotangent, main_weight, side_weight, in_bias, out_bias, norm_gain, norm_shift
):
    segments, shards = lax.axis_size("segment"), lax.axis_size("dp")
    z, d = lax.axis_index("segment"), lax.axis_index("dp")
    rows, width = tokens.shape
    main_mat, side_mat = main_weight[0], side_weight[0]
    hidden = main_mat.shape[1]
    half_width = side_mat.shape[1]
    block = width // shards
    last = segments - 1
    feeds = tuple(range(1, segments, 2))
    chip_masks = tuple(range(0, shards, 2))
    masks = chip_masks + tuple(m + 1 for m in chip_masks)
    meta = (z.reshape(1), d.reshape(1))

    def hop(value, *pairs):
        return lax.ppermute(value, "segment", list(pairs))

    def swap(value, mask, where=None):
        if where is None:
            return lax.ppermute(value, "dp", [(i, i ^ mask) for i in range(shards)])
        pairs = [(s * shards + i, s * shards + (i ^ mask)) for s in where for i in range(shards)]
        return lax.ppermute(value, ("segment", "dp"), pairs)

    ext = hidden + LANES
    low_ext = half_width + LANES
    kept_shapes = [
        ((segments, rows, width), BF16),
        ((segments, rows, hidden), BF16),
        ((segments, rows, hidden), BF16),
        ((segments, rows, width), F32),
        ((segments, rows, LANES), F32),
        ((segments, rows, hidden), BF16),
        ((segments, rows, width), BF16),
    ]
    lent = ((width // 2 + 16, half_width), BF16)
    borrowed_shapes = [((width, hidden), BF16), ((16, width), BF16)]
    narrow = ((rows, width), BF16)
    loads = [out_bias, norm_gain, norm_shift, main_mat, tokens, cotangent, cotangent]
    loaded, _ = kernel_call(
        begin, meta, [lengths.reshape(segments), side_mat, in_bias, *loads],
        [lent, lent, ((SMALLS, width), F32), ((segments, LANES), jnp.int32), (in_bias.shape, BF16)]
        + [(x.shape, x.dtype) for x in loads]
        + kept_shapes + borrowed_shapes,
        copies=3 + len(loads), smem_ins=(0,), hbm_ins=tuple(range(1, 3 + len(loads))),
    )
    share, later_share, sums, lengths_v, bias_v, *loaded = loaded
    out_bias_v, gain_v, shift_v, main_v, tokens_v, cotangent_v, later_cotangent, *kept = loaded
    kept, borrowed = (*kept[:-2], sums), tuple(kept[-2:])

    turns = tuple(range(last, -1, -1))
    first_share = hop(share, (0, 1))
    first_in = [hop(tokens_v, (home, 0)) for home in turns[:2]]
    riders = {
        0: [(turns[2], 0, "tokens"), (turns[1], last, "cotangent")],
        1: [(turns[2], last, "cotangent")],
    }

    def join(s, share, other, blank):
        return kernel_call(
            join_down, meta, [share, other, side_mat], [], kept=blank, hbm_ins=(2,), copies=1, where=(s,)
        )[1]

    turned = ((width, rows), BF16)
    n_chip = len(chip_masks)
    weight_scratch = [((width // 2 + 16, segments * rows), BF16), ((LANES, width), F32)]

    slots = 4 * last + segments
    waves, sent, finals = {}, {}, []
    after, last_in = {}, []
    side, main = [], []
    half_out = ((width // 2, ext), BF16)

    def hops_after(slot):
        pairs = []
        for z_role, what, j in roles_of(slot, segments):
            if what == "forward":
                pairs.append((z_role, z_role + 1))
            elif z_role > 0:
                pairs.append((z_role, z_role - 1))
            elif turns[j] > 0:
                pairs.append((z_role, turns[j]))
        return pairs + [(source, to) for source, to, _ in riders.get(slot, ())]

    homeward = {}
    for slot in range(2 * last + segments, slots):
        taken = [to for _, to in hops_after(slot)]
        free = [home for home in range(last) if home not in taken and home not in homeward.values()]
        if free:
            homeward[slot] = free[-1]
    for slot in range(slots):
        roles = roles_of(slot, segments)
        uses = [r[1] for r in roles]
        attends = any(r[0] % 2 == 0 for r in roles)
        feed_roles = any(r[0] % 2 == 1 for r in roles)
        names, ins = [], []

        def give(name, value):
            names.append(name)
            ins.append(value)

        for name, value in zip(
            ("main", "in_bias", "out_bias", "gain", "shift", "lengths"),
            (main_v, bias_v, out_bias_v, gain_v, shift_v, lengths_v),
        ):
            give(name, value)
        if feed_roles and slot != last + 2:
            give("down", down)
            give("low_bias", low_bias)
        if slot < 2:
            give("first", first_in[slot])
            give("cotangent", cotangent_v)
        if slot in (0, last):
            give("tokens", tokens_v)
        if slot - 2 in waves:
            give("wave", waves[slot - 2])
        if "both" in uses:
            give("last", last_in[slot - 2 * last])
        if slot in homeward:
            give("home", finals[turns.index(homeward[slot])])
        outs = [narrow] + ([narrow] if "both" in uses else [])
        weighing = slots - 2 <= slot
        if weighing:
            outs += [half_out] * (4 if slot == slots - 2 else 0)

        def body(
            meta, in_refs, out_refs, kept_refs, scratch, slot=slot, roles=roles, names=tuple(names)
        ):
            ref = dict(zip(names, in_refs))
            if slot == last + 2:
                ref["down"], ref["low_bias"] = kept_refs[-2:]
            vec = Vectors(
                ref["in_bias"], ref["out_bias"], ref["gain"], ref["shift"], ref.get("low_bias")
            )
            for z_role, what, j in roles:

                @pl.when(meta[0] == z_role)
                def _(z_role=z_role, what=what, j=j):
                    st = Store(kept_refs, j)
                    seq_len = ref["lengths"][turns[j] : turns[j] + 1, 0:1]
                    w, send = ref["main"], out_refs[0]
                    if what == "backward":
                        if z_role % 2:
                            feed_backward(ref["wave"][...], w, ref["down"], vec, st, send)
                        else:
                            attend_backward(ref["wave"][...], w, vec, st, send, scratch)
                        return
                    own = slot == last and z_role == 0
                    inputs = ref["tokens" if own else "first" if "first" in ref else "wave"][...]
                    if what == "both":
                        feed_both(
                            inputs, ref["last"][...], w, ref["down"], vec, seq_len, st, out_refs[1], send
                        )
                    elif z_role % 2:
                        feed_forward(inputs, w, ref["down"], vec, seq_len, st, send)
                    else:
                        attend_forward(inputs, w, vec, seq_len, st, send, scratch)

            for source, _, what in riders.get(slot, ()):

                @pl.when(meta[0] == source)
                def _(what=what):
                    out_refs[0][...] = ref[what][...]

            if "home" in ref:

                @pl.when(meta[0] == last)
                def _():
                    out_refs[0][...] = ref["home"][...]

            if weighing:
                sums = weight_refs(ref["lengths"], kept_refs)
                first = slot == slots - 2
                sides, mains = (out_refs[-4:-2], out_refs[-2:]) if first else ((), kept_refs[-2:])
                feed_here = lax.rem(meta[0], 2) == 1

                @pl.when(feed_here)
                def _():
                    for own in range(2):
                        if first:
                            side_half(bool(own))(meta, sums[2:], [sides[own]], (), scratch[-2:])
                        else:
                            main_half(bool(own), True)(meta, sums, [mains[own]], (), scratch[-2:])

                if first:

                    @pl.when(jnp.logical_not(feed_here) & (meta[0] > 0))
                    def _():
                        for own in range(2):
                            main_half(bool(own), False)(meta, sums, [mains[own]], (), scratch[-2:])

        scratch = [turned, turned, narrow] if attends else []
        if weighing:
            scratch = scratch + weight_scratch
        extra = ()
        if slot in (1, last + 1):
            extra = (later_share,)
        elif slot == last + 2:
            extra = (down, low_bias)
        elif slot == slots - 1:
            extra = (*main,)
        res, kept = kernel_call(
            body, meta, ins, outs, scratch, (*kept, *extra), after=after.get(slot, ()), flops=SLOT_FLOPS
        )
        if slot == 2:
            last_in += [cotangent_v, waves[0], waves[1]]
        if slot == 2 * last:
            _, (*kept, later_cotangent) = kernel_call(
                lambda *_: None, meta, [], [], kept=(*kept, later_cotangent), after=[waves[slot - 1]]
            )
            last_in.append(hop(later_cotangent, (0, last)))
        if slot == slots - 1:
            *kept, main[0], main[1] = kept
        if slot == 0:
            _, (*kept, first_share) = kernel_call(lambda *_: None, meta, [], [], kept=(*kept, first_share))
            down, low_bias = join(1, first_share, swap(first_share, 1), borrowed)
        if slot == 1:
            *kept, later_share = kept
            later_share = hop(later_share, (last - 1, last))
        if slot == last + 1:
            *kept, later_share = kept
            later_half = swap(later_share, 1)
        if slot == last + 2:
            *kept, down, low_bias = kept
            down, low_bias = join(last, later_share, later_half, (down, low_bias))
        sent[slot] = res[0]
        if slot == slots - 2:
            side, main = list(res[-4:-2]), list(res[-2:])
        if "both" in uses:
            finals.append(res[1])
        pairs = hops_after(slot)
        if slot in homeward:
            pairs.append((last, homeward[slot]))
        if slot == slots - 2:
            last_pairs = pairs
        elif pairs:
            waves[slot] = hop(res[0], *pairs)
    def weigh(own, after):
        _, (main[own],) = kernel_call(
            main_half(bool(own), False), meta, weight_refs(lengths_v, kept), [], weight_scratch,
            (main[own],), where=(0,), after=after,
        )

    def add_cores(keep, got, segs, after=()):
        blocks, _ = kernel_call(
            core_add(chip_masks), meta, [keep, got], [((block, keep.shape[1]), BF16)] * n_chip,
            where=segs, after=after,
        )
        return [blocks[0]] + [swap(blocks[i], chip_masks[i], segs) for i in range(n_chip - 1, 0, -1)]

    side_got = swap(side[0], 1, feeds)
    weigh(0, [side_got])
    main_got = swap(main[0], 1)
    side_blocks = add_cores(side[1], side_got, feeds, [main[0]])
    weigh(1, [side_blocks[0]])
    main_blocks = add_cores(main[1], main_got, None)
    (low_own, high_own), _ = kernel_call(
        chip_sum, meta, side_blocks, [((block, low_ext), BF16), ((block, half_width), BF16)], where=feeds
    )
    (total,), _ = kernel_call(chip_sum, meta, main_blocks, [((block, ext), BF16)])
    _, (message,) = kernel_call(lambda *_: None, meta, [], [], kept=(sent[slots - 2],), after=[total])
    waves[slots - 2] = hop(message, *last_pairs)
    outputs_at = [waves[next(k for k, v in homeward.items() if v == s)] for s in range(last)]
    outputs_at.append(finals[turns.index(last)])
    start = slots - segments
    grads_at = [sent[slots - 1]] + [waves[start + turns.index(s)] for s in range(1, segments)]

    low_got = hop(low_own, *[(s, s - 1) for s in feeds])
    (mine, again), _ = kernel_call(
        payload, meta, [total, high_own, low_got], [((block, ext + half_width), BF16)] * 2
    )
    _, (again,) = kernel_call(lambda *_: None, meta, [], [], kept=(again,), after=[waves[slots - 2]])

    gathered = [again] + [swap(mine, m) for m in chip_masks[1:]]
    gathered += [swap(b, 1) for b in gathered]

    results, _ = kernel_call(
        widen(masks, segments), meta, [*gathered, *outputs_at, *grads_at],
        [
            narrow, narrow,
            ((1, width, hidden), F32), ((1, width, half_width), F32), ((1, 3 * width), F32),
            ((1, width), F32), ((1, width), F32), ((1, width), F32), ((1, LANES), F32),
        ],
        [
            ((shards, block, hidden), F32), ((shards, block, half_width), F32),
            ((width, LANES), BF16), ((8, 3 * width), F32), ((1, LANES), F32),
        ],
        copies=2 * shards + 8,
        hbm_outs=tuple(range(9)),
    )
    return (*results[:8], results[8][:, :2])


def solution(mesh):
    over = P(("segment", "dp"), None)
    by_segment = [P("segment", None, None)] * 2 + [P("segment", None)] * 4
    in_specs = (over, P(None, "dp"), over, *by_segment)
    out_specs = (over, over, *by_segment, P("segment", None))
    return jax.shard_map(
        on_device, mesh=mesh, in_specs=in_specs, out_specs=out_specs, check_vma=False
    )
```

```python
import functools

import jax
import jax.numpy as jnp
from jax import lax
from jax.experimental import pallas as pl
from jax.experimental.pallas import tpu as pltpu
from jax.sharding import PartitionSpec as P

HEADS = 8
EPS = 1e-05
LANES = 128
VMEM_LIMIT = 22 * 1024 * 1024
SLOT_FLOPS = 40 * 10**9
F32 = jnp.float32
BF16 = jnp.bfloat16
GELU_IN = 0.7978845608028654
GELU_CUBE = 0.044715 * GELU_IN

BIAS, OUT_BIAS, GAIN, SHIFT, RESID_SQ, BRANCH_SQ, COUNT, SMALLS = 0, 4, 5, 6, 7, 8, 9, 16


def dot_nn(left, right):
    return jnp.dot(left, right, preferred_element_type=F32)


def dot_nt(left, right):
    return lax.dot_general(left, right, (((1,), (1,)), ((), ())), preferred_element_type=F32)


def kernel_call(
    body, meta, ins, outs, scratch=(), kept=(), copies=0, hbm_ins=(), smem_ins=(), hbm_outs=(), where=None,
    after=(), flops=1,
):
    ins = [*ins, *after]
    n_in, n_kept, n_out = len(ins), len(kept), len(outs)

    def kernel(z_ref, d_ref, *refs):
        at = 0
        groups = []
        for n in (n_in, n_kept, n_out, n_kept):
            groups.append(refs[at : at + n])
            at += n

        def run():
            body((z_ref[0], d_ref[0]), groups[0][: n_in - len(after)], groups[2], groups[3], refs[at:])

        if where is None:
            run()
        else:
            here = z_ref[0] == where[0]
            for other in where[1:]:
                here = here | (z_ref[0] == other)
            pl.when(here)(run)

    smem = pl.BlockSpec(memory_space=pltpu.SMEM)
    vmem = pl.BlockSpec(memory_space=pltpu.VMEM)
    hbm = pl.BlockSpec(memory_space=pltpu.HBM)

    def held(x, space=pltpu.VMEM):
        return pltpu.with_memory_space_constraint(x, space)

    results = pl.pallas_call(
        kernel,
        out_shape=[
            jax.ShapeDtypeStruct(*o) if i in hbm_outs else pltpu.VMEM(*o) for i, o in enumerate(outs)
        ]
        + [pltpu.VMEM(k.shape, k.dtype) for k in kept],
        in_specs=[smem] * 2
        + [smem if i in smem_ins else hbm if i in hbm_ins else vmem for i in range(n_in)]
        + [vmem] * n_kept,
        out_specs=[hbm if i in hbm_outs else vmem for i in range(n_out)] + [vmem] * n_kept,
        scratch_shapes=[pltpu.VMEM(*s) for s in scratch]
        + ([pltpu.SemaphoreType.DMA((copies,))] if copies else []),
        input_output_aliases={2 + n_in + i: n_out + i for i in range(n_kept)},
        compiler_params=pltpu.CompilerParams(vmem_limit_bytes=VMEM_LIMIT),
        cost_estimate=pl.CostEstimate(flops=flops, bytes_accessed=1, transcendentals=1),
    )(
        *meta,
        *[
            x if i in smem_ins else held(x, pltpu.HBM if i in hbm_ins else pltpu.VMEM)
            for i, x in enumerate(ins)
        ],
        *[held(k) for k in kept],
    )
    return tuple(results[:n_out]), tuple(results[n_out:])


NORM_ROWS = 32
NORM_BACK_ROWS = 128


def norm_forward(inputs, branch, seq_len, vec, st, out, back=None):
    gain, shift = vec.gain, vec.shift
    sums = [0.0] * 4
    grads = []
    block = NORM_ROWS if back is None else NORM_BACK_ROWS
    for first in range(0, inputs.shape[0], block):
        rows = slice(first, first + block)
        part = branch[rows]
        resid = inputs[rows].astype(F32) + part
        mean = jnp.mean(resid, axis=-1, keepdims=True)
        centred = resid - mean
        var = jnp.mean(centred * centred, axis=-1, keepdims=True)
        inv_std = lax.rsqrt(var + EPS)
        xhat = centred * inv_std
        out[rows, :] = (xhat * gain + shift).astype(BF16)
        live = first + lax.broadcasted_iota(jnp.int32, resid.shape, 0) < seq_len
        sums[0] += jnp.sum(jnp.where(live, resid * resid, 0.0), axis=0, keepdims=True)
        sums[1] += jnp.sum(jnp.where(live, part * part, 0.0), axis=0, keepdims=True)
        if back is None:
            st.xhat[rows, :] = xhat
            st.inv_std[rows, :] = jnp.broadcast_to(inv_std, (block, st.inv_std.shape[1]))
        else:
            grads.append(norm_back_rows(back[rows].astype(F32), xhat, inv_std, gain, sums))
    st.add(RESID_SQ, sums[0])
    st.add(BRANCH_SQ, sums[1])
    if back is not None:
        st.add(GAIN, sums[2])
        st.add(SHIFT, sums[3])
        return jnp.concatenate(grads, axis=0)


def norm_back_rows(grad, xhat, inv_std, gain, sums):
    gy = grad * gain
    along = grad * xhat
    first = jnp.mean(gy, axis=-1, keepdims=True)
    second = jnp.mean(along * gain, axis=-1, keepdims=True)
    sums[2] += jnp.sum(along, axis=0, keepdims=True)
    sums[3] += jnp.sum(grad, axis=0, keepdims=True)
    return (gy - first - xhat * second) * inv_std


def norm_backward(grad, vec, st):
    gain = vec.gain
    sums = [0.0] * 4
    grads = []
    for first in range(0, grad.shape[0], NORM_BACK_ROWS):
        rows = slice(first, first + NORM_BACK_ROWS)
        grads.append(
            norm_back_rows(grad[rows].astype(F32), st.xhat[rows, :], st.inv_std[rows, 0:1], gain, sums)
        )
    st.add(GAIN, sums[2])
    st.add(SHIFT, sums[3])
    return jnp.concatenate(grads, axis=0)


class Vectors:
    def __init__(self, in_bias, out_bias, gain, shift, low_bias=None):
        self.refs = (in_bias, out_bias, gain, shift, low_bias)

    def in_bias(self, i, width):
        return self.refs[0][0:1, i * width : (i + 1) * width].astype(F32)

    def first_bias(self, i, width):
        return self.refs[4][0:1, :width].astype(F32) if i == 0 else self.in_bias(i - 1, width)

    out_bias = property(lambda self: self.refs[1][...].astype(F32))
    gain = property(lambda self: self.refs[2][...].astype(F32))
    shift = property(lambda self: self.refs[3][...].astype(F32))


class Store:
    def __init__(self, kept, j):
        acts, wide, aux, xhat, inv_std, grad_wide, grad_branch, sums = kept[:8]
        self.x, self.wide, self.aux, self.xhat, self.inv_std, self.gwide, self.db = (
            a.at[j] for a in (acts, wide, aux, xhat, inv_std, grad_wide, grad_branch)
        )
        self.sums, self.first = sums, j == 0

    def add(self, row, value):
        if self.first:
            self.sums[row : row + 1, :] = value
        else:
            self.sums[row : row + 1, :] = self.sums[row : row + 1, :] + value


def attend_forward(inputs, w, vec, seq_len, st, send, scratch):
    vt, ctxt = scratch[:2]
    rows, width = inputs.shape
    size = width // HEADS
    st.x[...] = inputs
    q = (dot_nn(inputs, w[:, :width]) + vec.in_bias(0, width)).astype(BF16) * jnp.asarray(size**-0.5, BF16)
    st.wide[:, :width] = q
    k = dot_nn(inputs, w[:, width : 2 * width]).astype(BF16)
    st.wide[:, width : 2 * width] = k
    v = (dot_nn(inputs, w[:, 2 * width : 3 * width]) + vec.in_bias(1, width)).astype(BF16)
    st.wide[:, 2 * width : 3 * width] = v
    vt[...] = v.T
    key_live = lax.broadcasted_iota(jnp.int32, (rows, rows), 0) < seq_len
    lane = lax.broadcasted_iota(jnp.int32, (rows, 2 * size), 1)
    def score(head):
        first = (head // 2) * 2 * size
        qp = q[:, first : first + 2 * size]
        kp = k[:, first : first + 2 * size]
        mine = (lane >= size) if head % 2 else (lane < size)
        return dot_nt(jnp.where(mine, kp, jnp.zeros_like(kp)), qp)

    ahead = score(0)
    for head in range(HEADS):
        scores = jnp.where(key_live, ahead, -1e30)
        if head + 1 < HEADS:
            ahead = score(head + 1)
        top = jnp.max(scores, axis=0, keepdims=True)
        expo = jnp.exp(scores - top)
        total = jnp.sum(expo, axis=0, keepdims=True)
        probs = (expo * (1.0 / total)).astype(BF16)
        st.aux[:, head * rows : (head + 1) * rows] = probs
        ctxt[head * size : (head + 1) * size, :] = dot_nn(
            vt[head * size : (head + 1) * size, :], probs
        ).astype(BF16)
    ctx = ctxt[...].T
    st.wide[:, 3 * width :] = ctx
    branch = dot_nn(ctx, w[:, 3 * width :]) + vec.out_bias
    norm_forward(inputs, branch, seq_len, vec, st, send)


def feed_branch(inputs, w, down, vec, st):
    width = inputs.shape[1]
    st.x[...] = inputs
    step = 2 * width

    def before(c):
        bias = jnp.concatenate([vec.first_bias(2 * c, width), vec.first_bias(2 * c + 1, width)], axis=1)
        return dot_nn(inputs, w[:, c * step : (c + 1) * step]) + bias

    branch = None
    ahead = before(0)
    for c in range(w.shape[1] // step):
        cols = slice(c * step, (c + 1) * step)
        x = ahead
        if cols.stop < w.shape[1]:
            ahead = before(c + 1)
        square = x * x
        t = jnp.tanh(x * (GELU_IN + GELU_CUBE * square))
        s = 0.5 + 0.5 * t
        act = x * s
        slope = s + act * (1.0 - t) * (GELU_IN + (3.0 * GELU_CUBE) * square)
        hidden = act.astype(BF16)
        st.wide[:, cols] = hidden
        st.aux[:, cols] = slope.astype(BF16)
        part = dot_nt(hidden, down[:, cols])
        branch = part if branch is None else branch + part
    return branch + vec.out_bias


def feed_forward(inputs, w, down, vec, seq_len, st, send):
    branch = feed_branch(inputs, w, down, vec, st)
    norm_forward(inputs, branch, seq_len, vec, st, send)


def feed_grads(dresid, w, down, st, send):
    width = dresid.shape[1]
    dbranch = dresid.astype(BF16)
    st.db[...] = dbranch
    total = dresid
    step = 2 * width
    ahead = dot_nn(dbranch, down[:, :step])
    for c in range(w.shape[1] // step):
        cols = slice(c * step, (c + 1) * step)
        dhidden = ahead
        if cols.stop < w.shape[1]:
            ahead = dot_nn(dbranch, down[:, cols.stop : cols.stop + step])
        dpre = (dhidden * st.aux[:, cols].astype(F32)).astype(BF16)
        st.gwide[:, cols] = dpre
        total = total + dot_nt(dpre, w[:, cols])
    send[...] = total.astype(BF16)


def feed_backward(grad, w, down, vec, st, send):
    dresid = norm_backward(grad, vec, st)
    feed_grads(dresid, w, down, st, send)


def feed_both(inputs, grad, w, down, vec, seq_len, st, y_out, send):
    branch = feed_branch(inputs, w, down, vec, st)
    dresid = norm_forward(inputs, branch, seq_len, vec, st, y_out, grad)
    feed_grads(dresid, w, down, st, send)


def attend_backward(grad, w, vec, st, send, scratch):
    kt, dqt = scratch[:2]
    rows, width = grad.shape
    size = width // HEADS
    dresid = norm_backward(grad, vec, st)
    dbranch = dresid.astype(BF16)
    st.gwide[:, 3 * width :] = dbranch
    dctx = dot_nt(dbranch, w[:, 3 * width :]).astype(BF16)
    q, v = st.wide[:, :width], st.wide[:, 2 * width : 3 * width]
    kt[...] = (st.wide[:, width : 2 * width] * jnp.asarray(size**-0.5, BF16)).T
    lane = lax.broadcasted_iota(jnp.int32, (rows, 2 * size), 1)
    none = jnp.zeros((rows, 2 * size), BF16)

    def own(value, head):
        first = (head // 2) * 2 * size
        mine = (lane >= size) if head % 2 else (lane < size)
        return jnp.where(mine, value[:, first : first + 2 * size], none)

    def probs_grad(head):
        first = (head // 2) * 2 * size
        return dot_nt(own(v, head), dctx[:, first : first + 2 * size])

    ahead = probs_grad(0)
    for head in range(HEADS):
        dprobs = ahead
        if head + 1 < HEADS:
            ahead = probs_grad(head + 1)
        probs_low = st.aux[:, head * rows : (head + 1) * rows]
        probs = probs_low.astype(F32)
        inner = jnp.sum(probs * dprobs, axis=0, keepdims=True)
        dscores = (probs * (dprobs - inner)).astype(BF16)
        dv_part = dot_nn(probs_low, own(dctx, head))
        dk_part = dot_nn(dscores, own(q, head))
        dqt[head * size : (head + 1) * size, :] = dot_nn(
            kt[head * size : (head + 1) * size, :], dscores
        ).astype(BF16)
        if head % 2 == 0:
            dv, dk = dv_part, dk_part
        else:
            at = width + (head // 2) * 2 * size
            st.gwide[:, at : at + 2 * size] = (dk + dk_part).astype(BF16)
            st.gwide[:, width + at : width + at + 2 * size] = (dv + dv_part).astype(BF16)
    dx = dresid + dot_nt(st.gwide[:, width : 3 * width], w[:, width : 3 * width])
    st.gwide[:, :width] = dqt[...].T
    send[...] = (dx + dot_nt(st.gwide[:, :width], w[:, :width])).astype(BF16)


def roles_of(slot, segments):
    last = segments - 1
    found = []
    for z in range(segments):
        j = slot - 2 * z
        if 0 <= j < segments:
            found.append((z, "both" if z == last else "forward", j))
        j = slot - (4 * last - 2 * z)
        if z < last and 0 <= j < segments:
            found.append((z, "backward", j))
    return found


def half_rows(meta, own, width):
    bit = lax.rem(meta[1], 2)
    bit = bit if own else 1 - bit
    return pl.multiple_of(bit * (width // 2), width // 2)


def load_turned(at, source, lanes):
    for j in range(source.shape[0]):
        rows = source.shape[1]
        at[: lanes.size, j * rows : (j + 1) * rows] = source[j, :, lanes].T


def weight_refs(lengths, kept):
    acts, wide, _, _, _, grad_wide, grad_branch, sums = kept[:8]
    return [lengths, acts, wide, grad_wide, grad_branch, sums]


def main_half(own, feed):
    def body(meta, ins, outs, kept, scratch):
        lengths, acts, wide, grad_wide, grad_branch, sums = ins
        (out,) = kept or outs
        at, sm = scratch
        count, rows, width = acts.shape
        half, full, total = width // 2, wide.shape[2], count * rows
        start = half_rows(meta, own, width)
        mine = pl.ds(start, half)
        sm[...] = jnp.zeros_like(sm)
        sm[:SMALLS, :] = sums[...]
        tokens = jnp.sum(lengths[:, 0:1].astype(F32), axis=0, keepdims=True)
        sm[COUNT : COUNT + 1, :] = jnp.broadcast_to(tokens, (1, width))
        at[half:, :] = jnp.ones((at.shape[0] - half, total), BF16)
        load_turned(at, acts, mine)
        grads = grad_wide[...].reshape(total, full)
        for c in range(full // width):
            cols = slice(c * width, (c + 1) * width)
            if c == 3 and not feed:
                load_turned(at, wide, pl.ds(pl.multiple_of(3 * width + start, half), half))
            grad = dot_nn(at[...], grads[:, cols])
            out[:, cols] = grad[:half].astype(BF16)
            place = BIAS + (3, 0, 1, 2)[c] if feed else (BIAS, None, BIAS + 1, OUT_BIAS)[c]
            if place is not None:
                sm[place : place + 1, :] = grad[half : half + 1]
        if feed:
            sm[OUT_BIAS : OUT_BIAS + 1, :] = jnp.sum(
                grad_branch[...].reshape(total, width).astype(F32), axis=0, keepdims=True
            )
        out[:, full:] = sm[:, mine].T.astype(BF16)

    return body


def side_half(own):
    def body(meta, ins, outs, kept, scratch):
        wide, grad_wide, grad_branch = ins[:3]
        (out,) = kept or outs
        at, sm = scratch
        count, rows, width = grad_branch.shape
        half, full, total = width // 2, wide.shape[2], count * rows
        mine = pl.ds(half_rows(meta, own, width), half)
        sm[...] = jnp.broadcast_to(
            jnp.sum(
                grad_wide[:, :, :width].reshape(total, width).astype(F32), axis=0, keepdims=True
            ),
            sm.shape,
        )
        out[:, full // 2 : full // 2 + LANES] = sm[:, mine].T.astype(BF16)
        load_turned(at, grad_branch, mine)
        hid = wide[...].reshape(total, full)
        for c in range(full // width):
            cols = slice(c * width, (c + 1) * width)
            grad = dot_nn(at[:half, :], hid[:, cols]).astype(BF16)
            put = c * width + (LANES if c * width >= full // 2 else 0)
            out[:, put : put + width] = grad

    return body


def core_add(masks):
    def body(meta, ins, outs, kept, scratch):
        size = outs[0].shape[0]
        chip = lax.div(meta[1], 2)
        for mask, out in zip(masks, outs, strict=True):
            rows = pl.ds(pl.multiple_of(jnp.bitwise_xor(chip, mask // 2) * size, size), size)
            at = 0
            for keep, got in zip(ins[0::2], ins[1::2], strict=True):
                cols = slice(at, at + keep.shape[1])
                at += keep.shape[1]
                out[:, cols] = (keep[rows, :].astype(F32) + got[rows, :].astype(F32)).astype(BF16)

    return body


def summed(refs, cols):
    total = refs[0][:, cols].astype(F32)
    for r in refs[1:]:
        total = total + r[:, cols].astype(F32)
    return total.astype(BF16)


def chip_sum(meta, ins, outs, kept, scratch):
    at = 0
    for out in outs or kept:
        out[...] = summed(ins, slice(at, at + out.shape[1]))
        at += out.shape[1]


def added(one, two, rows):
    return (one[rows, :].astype(F32) + two[rows, :].astype(F32)).astype(BF16)


def first_cut(meta, ins, outs, kept, scratch):
    keep, got = ins
    upper_stay, upper_go, lower_stay, lower_go = outs
    size = upper_stay.shape[0]
    half = size // 2
    chip = lax.div(meta[1], 2)
    x, y = lax.rem(chip, 2), lax.div(chip, 2)
    for other in range(2):
        put = slice(other * half, (other + 1) * half)
        for out, q, low in (
            (upper_go, 2 * other + 1 - x, 0),
            (lower_go, 2 * (1 - y) + other, half),
            (upper_stay, 2 * other + x, 0),
            (lower_stay, 2 * y + other, half),
        ):
            out[put, :] = added(keep, got, pl.ds(pl.multiple_of(q * size + low, half), half))


def second_cut(meta, ins, outs, kept, scratch):
    upper, upper_got, lower, lower_got = ins
    half = outs[0].shape[0]
    chip = lax.div(meta[1], 2)
    x, y = lax.rem(chip, 2), lax.div(chip, 2)
    for one, two, bit, stay, go in (
        (upper, upper_got, y, outs[0], outs[1]),
        (lower, lower_got, x, outs[2], outs[3]),
    ):
        go[...] = added(one, two, pl.ds(pl.multiple_of((1 - bit) * half, half), half))
        stay[...] = added(one, two, pl.ds(pl.multiple_of(bit * half, half), half))


def cut_sum(meta, ins, outs, kept, scratch):
    half = ins[0].shape[0]
    for i in range(2):
        at = 0
        for out in outs:
            cols = slice(at, at + out.shape[1])
            out[i * half : (i + 1) * half, :] = summed(ins[2 * i : 2 * i + 2], cols)
            at += out.shape[1]


def cross_message(meta, ins, outs, kept, scratch):
    low, grad = ins
    (out,) = outs
    size, width = low.shape[0], out.shape[1]

    @pl.when(lax.rem(meta[0], 2) == 1)
    def _():
        for i in range(0, low.shape[1], width):
            cols = min(width, low.shape[1] - i)
            out[i // width * size : (i // width + 1) * size, :cols] = low[:, i : i + cols]

    @pl.when(meta[0] == 0)
    def _():
        out[...] = grad[...]


def side_share(meta, ins, outs, kept, scratch):
    high, message = ins
    (out,) = outs
    half = high.shape[1]

    @pl.when(lax.rem(meta[0], 2) == 1)
    def _():
        out[:, :half] = high[...]
        out[:, half:] = jnp.zeros((out.shape[0], out.shape[1] - half), BF16)

    @pl.when(lax.rem(meta[0], 2) == 0)
    def _():
        size, width = out.shape[0], message.shape[1]
        for i in range(0, out.shape[1], width):
            cols = min(width, out.shape[1] - i)
            out[:, i : i + cols] = message[i // width * size : (i // width + 1) * size, :cols]


def block_row(meta, mask, width, size):
    chip, core = lax.div(meta[1], 2), lax.rem(meta[1], 2)
    side = jnp.bitwise_xor(core, mask % 2)
    at = side * (width // 2) + jnp.bitwise_xor(chip, mask // 2) * size
    return pl.multiple_of(at, size)


def begin(meta, ins, outs, kept, scratch):
    lens, side, in_bias, *rest = ins
    share, again, zero_sums, lens_v, bias_v, *outs = outs
    sems = scratch[-1]
    width, block = side.shape[0], share.shape[0] - 16
    rows = pl.ds(half_rows(meta, True, width), block)
    pairs = [(in_bias, bias_v), (side.at[rows], share.at[:block]), (side.at[rows], again.at[:block])]
    pairs += list(zip(rest, outs[: len(rest)], strict=True))
    copies = [pltpu.make_async_copy(src, dst, sems.at[i]) for i, (src, dst) in enumerate(pairs)]
    for c in copies:
        c.start()
    zero_sums[...] = jnp.zeros_like(zero_sums)
    for j in range(lens_v.shape[0]):
        lens_v[j : j + 1, :] = jnp.full((1, LANES), lens[j], jnp.int32)
    copies[0].wait()
    for ref in (share, again):
        ref[block:, width:] = jnp.zeros((16, share.shape[1] - width), BF16)
        ref[block:, :width] = jnp.broadcast_to(bias_v[:, 2 * width :], (16, width))
    for c in copies[1:]:
        c.wait()


def join_down(meta, ins, outs, kept, scratch):
    lent, other, side = ins
    down, low_bias = kept
    width, half = side.shape
    block = width // 2
    copy = pltpu.make_async_copy(side, down.at[:, half:], scratch[-1].at[0])
    copy.start()
    down[pl.ds(half_rows(meta, True, width), block), :half] = lent[:block]
    down[pl.ds(half_rows(meta, False, width), block), :half] = other[:block]
    low_bias[...] = lent[block:, :width]
    copy.wait()


class Results:
    def __init__(self, sems):
        self.sems, self.copies = sems, []

    def out(self, src, dst):
        self.picked([src], dst, None)

    def picked(self, refs, dst, which):
        sem = self.sems.at[len(self.copies)]
        for j, r in enumerate(refs):
            start = pltpu.make_async_copy(r, dst, sem).start
            start() if which is None else pl.when(which == j)(start)
        self.copies.append(pltpu.make_async_copy(refs[0], dst, sem))

    def finish(self):
        for c in self.copies:
            c.wait()


def widen_main(masks, segments):
    def body(meta, ins, outs, kept, scratch):
        n = len(masks)
        blocks, finals, backs = ins[:n], ins[n : n + segments], ins[n + segments :]
        out_y, out_g, main_h, out_b, gain_h, shift_h, stats_h, small_v = outs
        full, cols, stat, sems = scratch
        res = Results(sems)
        res.picked(finals, out_y, meta[0])
        res.picked(backs, out_g, meta[0])
        width, main = main_h.shape[1], main_h.shape[2]
        size = blocks[0].shape[0]
        for i, mask in enumerate(masks):
            at = block_row(meta, mask, width, size)
            cols[pl.ds(at, size), :] = blocks[i][:, main:]
            full[i] = blocks[i][:, :main].astype(F32)
            res.out(full.at[i], main_h.at[0, pl.ds(at, size)])
        small = cols[...].T.astype(F32)
        small_v[...] = small[: small_v.shape[0]]
        squares = jnp.sum(small[RESID_SQ : BRANCH_SQ + 1], axis=1, keepdims=True)
        values = jnp.sqrt(squares / (small[COUNT : COUNT + 1, 0:1] * width))
        lane = lax.broadcasted_iota(jnp.int32, (1, LANES), 1)
        stat[...] = jnp.where(lane == 0, values[0:1], values[1:2])
        res.out(small_v.at[OUT_BIAS : OUT_BIAS + 1], out_b)
        res.out(small_v.at[GAIN : GAIN + 1], gain_h)
        res.out(small_v.at[SHIFT : SHIFT + 1], shift_h)
        res.out(stat, stats_h)
        res.finish()

    return body


def widen_side(masks):
    def body(meta, ins, outs, kept, scratch):
        *blocks, small = ins
        side_h, in_b = outs
        full, cols, vecs, sems = scratch
        res = Results(sems)
        width, half = side_h.shape[1], side_h.shape[2]
        size = blocks[0].shape[0]
        for i, mask in enumerate(masks):
            at = block_row(meta, mask, width, size)
            cols[pl.ds(at, size), :] = blocks[i][:, half:]
            full[i] = blocks[i][:, :half].astype(F32)
            res.out(full.at[i], side_h.at[0, pl.ds(at, size)])
        lent = cols[...].T.astype(F32)[0:1]
        feed = jnp.full((1, width), lax.rem(meta[0], 2), jnp.int32) == 1
        vecs[0:1, :width] = small[BIAS : BIAS + 1]
        vecs[0:1, width : 2 * width] = small[BIAS + 1 : BIAS + 2]
        vecs[0:1, 2 * width :] = jnp.where(feed, small[BIAS + 2 : BIAS + 3], lent)
        res.out(vecs.at[0:1], in_b)
        res.finish()

    return body


def on_device(
    tokens, lengths, cotangent, main_weight, side_weight, in_bias, out_bias, norm_gain, norm_shift
):
    segments, shards = lax.axis_size("segment"), lax.axis_size("dp")
    z, d = lax.axis_index("segment"), lax.axis_index("dp")
    rows, width = tokens.shape
    main_mat, side_mat = main_weight[0], side_weight[0]
    hidden = main_mat.shape[1]
    half_width = side_mat.shape[1]
    block = width // shards
    last = segments - 1
    feeds = tuple(range(1, segments, 2))
    chip_masks = tuple(range(0, shards, 2))
    masks = chip_masks + tuple(m + 1 for m in chip_masks)
    meta = (z.reshape(1), d.reshape(1))

    def hop(value, *pairs):
        return lax.ppermute(value, "segment", list(pairs))

    def swap(value, mask):
        return lax.ppermute(value, "dp", [(i, i ^ mask) for i in range(shards)])

    ext = hidden + LANES
    low_ext = half_width + LANES
    kept_shapes = [
        ((segments, rows, width), BF16),
        ((segments, rows, hidden), BF16),
        ((segments, rows, hidden), BF16),
        ((segments, rows, width), F32),
        ((segments, rows, LANES), F32),
        ((segments, rows, hidden), BF16),
        ((segments, rows, width), BF16),
    ]
    lent = ((width // 2 + 16, half_width), BF16)
    borrowed_shapes = [((width, hidden), BF16), ((16, width), BF16)]
    narrow = ((rows, width), BF16)
    loads = [out_bias, norm_gain, norm_shift, main_mat, tokens, cotangent, cotangent]
    loaded, _ = kernel_call(
        begin, meta, [lengths.reshape(segments), side_mat, in_bias, *loads],
        [lent, lent, ((SMALLS, width), F32), ((segments, LANES), jnp.int32), (in_bias.shape, BF16)]
        + [(x.shape, x.dtype) for x in loads]
        + kept_shapes + borrowed_shapes,
        copies=3 + len(loads), smem_ins=(0,), hbm_ins=tuple(range(1, 3 + len(loads))),
    )
    share, later_share, sums, lengths_v, bias_v, *loaded = loaded
    out_bias_v, gain_v, shift_v, main_v, tokens_v, cotangent_v, later_cotangent, *kept = loaded
    kept, borrowed = (*kept[:-2], sums), tuple(kept[-2:])

    turns = tuple(range(last, -1, -1))
    first_share = hop(share, (0, 1))
    first_in = [hop(tokens_v, (home, 0)) for home in turns[:2]]
    riders = {
        0: [(turns[2], 0, "tokens"), (turns[1], last, "cotangent")],
        1: [(turns[2], last, "cotangent")],
    }

    def join(s, share, other, blank):
        return kernel_call(
            join_down, meta, [share, other, side_mat], [], kept=blank, hbm_ins=(2,), copies=1, where=(s,)
        )[1]

    turned = ((width, rows), BF16)
    n_chip = len(chip_masks)
    weight_scratch = [((width // 2 + 16, segments * rows), BF16), ((LANES, width), F32)]

    slots = 4 * last + segments
    waves, sent, finals = {}, {}, []
    after, last_in = {}, []
    side, main = [], []
    half_out = ((width // 2, ext), BF16)

    def hops_after(slot):
        pairs = []
        for z_role, what, j in roles_of(slot, segments):
            if what == "forward":
                pairs.append((z_role, z_role + 1))
            elif z_role > 0:
                pairs.append((z_role, z_role - 1))
            elif turns[j] > 0:
                pairs.append((z_role, turns[j]))
        return pairs + [(source, to) for source, to, _ in riders.get(slot, ())]

    homeward = {}
    for slot in range(2 * last + segments, slots):
        taken = [to for _, to in hops_after(slot)]
        free = [home for home in range(1, last) if home not in taken and home not in homeward.values()]
        if free:
            homeward[slot] = free[-1]
    for slot in range(slots):
        roles = roles_of(slot, segments)
        uses = [r[1] for r in roles]
        attends = any(r[0] % 2 == 0 for r in roles)
        feed_roles = any(r[0] % 2 == 1 for r in roles)
        names, ins = [], []

        def give(name, value):
            names.append(name)
            ins.append(value)

        for name, value in zip(
            ("main", "in_bias", "out_bias", "gain", "shift", "lengths"),
            (main_v, bias_v, out_bias_v, gain_v, shift_v, lengths_v),
        ):
            give(name, value)
        if feed_roles and slot != last + 2:
            give("down", down)
            give("low_bias", low_bias)
        if slot < 2:
            give("first", first_in[slot])
            give("cotangent", cotangent_v)
        if slot in (0, last):
            give("tokens", tokens_v)
        if slot - 2 in waves:
            give("wave", waves[slot - 2])
        if "both" in uses:
            give("last", last_in[slot - 2 * last])
        if slot in homeward:
            give("home", finals[turns.index(homeward[slot])])
        outs = [narrow] + ([narrow] if "both" in uses else [])
        weighing = slots - 2 <= slot
        if weighing:
            outs += [half_out] * (4 if slot == slots - 2 else 0)

        def body(
            meta, in_refs, out_refs, kept_refs, scratch, slot=slot, roles=roles, names=tuple(names)
        ):
            ref = dict(zip(names, in_refs))
            if slot == last + 2:
                ref["down"], ref["low_bias"] = kept_refs[-2:]
            vec = Vectors(
                ref["in_bias"], ref["out_bias"], ref["gain"], ref["shift"], ref.get("low_bias")
            )
            for z_role, what, j in roles:

                @pl.when(meta[0] == z_role)
                def _(z_role=z_role, what=what, j=j):
                    st = Store(kept_refs, j)
                    seq_len = ref["lengths"][turns[j] : turns[j] + 1, 0:1]
                    w, send = ref["main"], out_refs[0]
                    if what == "backward":
                        if z_role % 2:
                            feed_backward(ref["wave"][...], w, ref["down"], vec, st, send)
                        else:
                            attend_backward(ref["wave"][...], w, vec, st, send, scratch)
                        return
                    own = slot == last and z_role == 0
                    inputs = ref["tokens" if own else "first" if "first" in ref else "wave"][...]
                    if what == "both":
                        feed_both(
                            inputs, ref["last"][...], w, ref["down"], vec, seq_len, st, out_refs[1], send
                        )
                    elif z_role % 2:
                        feed_forward(inputs, w, ref["down"], vec, seq_len, st, send)
                    else:
                        attend_forward(inputs, w, vec, seq_len, st, send, scratch)

            for source, _, what in riders.get(slot, ()):

                @pl.when(meta[0] == source)
                def _(what=what):
                    out_refs[0][...] = ref[what][...]

            if "home" in ref:

                @pl.when(meta[0] == last)
                def _():
                    out_refs[0][...] = ref["home"][...]

            if weighing:
                sums = weight_refs(ref["lengths"], kept_refs)
                first = slot == slots - 2
                sides, mains = (out_refs[-4:-2], out_refs[-2:]) if first else ((), kept_refs[-2:])
                feed_here = lax.rem(meta[0], 2) == 1

                @pl.when(feed_here)
                def _():
                    for own in range(2):
                        if first:
                            side_half(bool(own))(meta, sums[2:], [sides[own]], (), scratch[-2:])
                        else:
                            main_half(bool(own), True)(meta, sums, [mains[own]], (), scratch[-2:])

                if first:

                    @pl.when(jnp.logical_not(feed_here) & (meta[0] > 0))
                    def _():
                        for own in range(2):
                            main_half(bool(own), False)(meta, sums, [mains[own]], (), scratch[-2:])

        scratch = [turned, turned, narrow] if attends else []
        if weighing:
            scratch = scratch + weight_scratch
        extra = ()
        if slot in (1, last + 1):
            extra = (later_share,)
        elif slot == last + 2:
            extra = (down, low_bias)
        elif slot == slots - 1:
            extra = (*main,)
        res, kept = kernel_call(
            body, meta, ins, outs, scratch, (*kept, *extra), after=after.get(slot, ()), flops=SLOT_FLOPS
        )
        if slot == 2:
            last_in += [cotangent_v, waves[0], waves[1]]
        if slot == 2 * last:
            _, (*kept, later_cotangent) = kernel_call(
                lambda *_: None, meta, [], [], kept=(*kept, later_cotangent), after=[waves[slot - 1]]
            )
            last_in.append(hop(later_cotangent, (0, last)))
        if slot == slots - 1:
            *kept, main[0], main[1] = kept
        if slot == 0:
            _, (*kept, first_share) = kernel_call(lambda *_: None, meta, [], [], kept=(*kept, first_share))
            down, low_bias = join(1, first_share, swap(first_share, 1), borrowed)
        if slot == 1:
            *kept, later_share = kept
            later_share = hop(later_share, (last - 1, last))
        if slot == last + 1:
            *kept, later_share = kept
            later_half = swap(later_share, 1)
        if slot == last + 2:
            *kept, down, low_bias = kept
            down, low_bias = join(last, later_share, later_half, (down, low_bias))
        sent[slot] = res[0]
        if slot == slots - 2:
            side, main = list(res[-4:-2]), list(res[-2:])
        if "both" in uses:
            finals.append(res[1])
        pairs = hops_after(slot)
        if slot in homeward:
            pairs.append((last, homeward[slot]))
        if pairs and slot != slots - 2:
            waves[slot] = hop(res[0], *pairs)
    def weigh(own, after):
        _, (main[own],) = kernel_call(
            main_half(bool(own), False), meta, weight_refs(lengths_v, kept), [], weight_scratch,
            (main[own],), where=(0,), after=after,
        )

    def add_cores(keep, got, segs, after=()):
        blocks, _ = kernel_call(
            core_add(chip_masks), meta, [keep, got], [((block, keep.shape[1]), BF16)] * n_chip,
            where=segs, after=after,
        )
        return [blocks[0]] + [swap(blocks[i], chip_masks[i]) for i in range(n_chip - 1, 0, -1)]

    def add_in_steps(keep, got, segs, after=()):
        rows_of = (keep.shape[0] // 4, keep.shape[1])
        (up, up_go, down, down_go), _ = kernel_call(
            first_cut, meta, [keep, got], [(rows_of, BF16)] * 4, where=segs, after=after
        )
        rows_of = (rows_of[0] // 2, rows_of[1])
        (up, up_go, down, down_go), _ = kernel_call(
            second_cut, meta, [up, swap(up_go, 2), down, swap(down_go, 4)],
            [(rows_of, BF16)] * 4, where=segs,
        )
        return [up, swap(up_go, 4), down, swap(down_go, 2)]

    reduce, last_sum = (add_in_steps, cut_sum) if n_chip == 4 else (add_cores, chip_sum)
    side_got = swap(side[0], 1)
    weigh(0, [side_got])
    main_got = swap(main[0], 1)
    side_blocks = reduce(side[1], side_got, feeds, [main[0]])
    weigh(1, [side_blocks[0]] if n_chip != 4 else [])
    main_blocks = reduce(main[1], main_got, None)
    (low_own, high_own), _ = kernel_call(
        last_sum, meta, side_blocks, [((block, low_ext), BF16), ((block, half_width), BF16)], where=feeds,
        after=main_blocks[:1],
    )
    (total,), _ = kernel_call(last_sum, meta, main_blocks, [((block, ext), BF16)])
    (message,), _ = kernel_call(cross_message, meta, [low_own, sent[slots - 2]], [narrow])
    waves[slots - 2] = hop(message, *[(s, s - 1) for s in feeds], (0, turns[-2]))
    first_home = hop(finals[turns.index(0)], (last, 0))
    outputs_at = [first_home] + [
        waves[next(k for k, v in homeward.items() if v == s)] for s in range(1, last)
    ]
    outputs_at.append(finals[turns.index(last)])
    start = slots - segments
    grads_at = [sent[slots - 1]] + [waves[start + turns.index(s)] for s in range(1, segments)]

    def gather(share):
        blocks = [share] + [swap(share, m) for m in reversed(chip_masks[1:])]
        blocks = [blocks[0], *reversed(blocks[1:])]
        return blocks + [swap(b, 1) for b in blocks]

    main_all = gather(total)
    (side_mine,), _ = kernel_call(
        side_share, meta, [high_own, waves[slots - 2]], [((block, low_ext), BF16)],
        after=[main_all[2]],
    )
    (out_y, out_g, main_grad, out_bias_grad, gain_grad, shift_grad, stats, small), _ = kernel_call(
        widen_main(masks, segments), meta, [*main_all, *outputs_at, *grads_at],
        [narrow, narrow, ((1, width, hidden), F32)]
        + [((1, width), F32)] * 3
        + [((1, LANES), F32), ((SMALLS, width), F32)],
        [((shards, block, hidden), F32), ((width, LANES), BF16), ((1, LANES), F32)],
        copies=shards + 6, hbm_outs=tuple(range(7)),
    )
    (side_grad, in_bias_grad), _ = kernel_call(
        widen_side(masks), meta, [*gather(side_mine), small],
        [((1, width, half_width), F32), ((1, 3 * width), F32)],
        [((shards, block, half_width), F32), ((width, LANES), BF16), ((8, 3 * width), F32)],
        copies=shards + 1, hbm_outs=(0, 1),
    )
    return (
        out_y, out_g, main_grad, side_grad, in_bias_grad, out_bias_grad, gain_grad, shift_grad, stats[:, :2]
    )


def solution(mesh):
    over = P(("segment", "dp"), None)
    by_segment = [P("segment", None, None)] * 2 + [P("segment", None)] * 4
    in_specs = (over, P(None, "dp"), over, *by_segment)
    out_specs = (over, over, *by_segment, P("segment", None))
    return jax.shard_map(
        on_device, mesh=mesh, in_specs=in_specs, out_specs=out_specs, check_vma=False
    )
```

```python
import functools

import jax
import jax.numpy as jnp
from jax import lax
from jax.experimental import pallas as pl
from jax.experimental.pallas import tpu as pltpu
from jax.sharding import PartitionSpec as P

HEADS = 8
EPS = 1e-05
LANES = 128
VMEM_LIMIT = 12 * 1024 * 1024
SLOT_FLOPS = 40 * 10**9
FEED_EARLY, ATTEND_EARLY = 2, 3
F32 = jnp.float32
BF16 = jnp.bfloat16
GELU_IN = 0.7978845608028654
GELU_CUBE = 0.044715 * GELU_IN

BIAS, OUT_BIAS, GAIN, SHIFT, RESID_SQ, BRANCH_SQ, COUNT, SMALLS = 0, 4, 5, 6, 7, 8, 9, 16


def dot_nn(left, right):
    return jnp.dot(left, right, preferred_element_type=F32)


def dot_nt(left, right):
    return lax.dot_general(left, right, (((1,), (1,)), ((), ())), preferred_element_type=F32)


def kernel_call(
    body, meta, ins, outs, scratch=(), kept=(), copies=0, hbm_ins=(), smem_ins=(), hbm_outs=(), where=None,
    after=(), flops=1,
):
    ins = [*ins, *after]
    n_in, n_kept, n_out = len(ins), len(kept), len(outs)

    def kernel(z_ref, d_ref, *refs):
        at = 0
        groups = []
        for n in (n_in, n_kept, n_out, n_kept):
            groups.append(refs[at : at + n])
            at += n

        def run():
            body((z_ref[0], d_ref[0]), groups[0][: n_in - len(after)], groups[2], groups[3], refs[at:])

        if where is None:
            run()
        else:
            here = z_ref[0] == where[0]
            for other in where[1:]:
                here = here | (z_ref[0] == other)
            pl.when(here)(run)

    smem = pl.BlockSpec(memory_space=pltpu.SMEM)
    vmem = pl.BlockSpec(memory_space=pltpu.VMEM)
    hbm = pl.BlockSpec(memory_space=pltpu.HBM)

    def held(x, space=pltpu.VMEM):
        return pltpu.with_memory_space_constraint(x, space)

    results = pl.pallas_call(
        kernel,
        out_shape=[
            jax.ShapeDtypeStruct(*o) if i in hbm_outs else pltpu.VMEM(*o) for i, o in enumerate(outs)
        ]
        + [pltpu.VMEM(k.shape, k.dtype) for k in kept],
        in_specs=[smem] * 2
        + [smem if i in smem_ins else hbm if i in hbm_ins else vmem for i in range(n_in)]
        + [vmem] * n_kept,
        out_specs=[hbm if i in hbm_outs else vmem for i in range(n_out)] + [vmem] * n_kept,
        scratch_shapes=[pltpu.VMEM(*s) for s in scratch]
        + ([pltpu.SemaphoreType.DMA((copies,))] if copies else []),
        input_output_aliases={2 + n_in + i: n_out + i for i in range(n_kept)},
        compiler_params=pltpu.CompilerParams(vmem_limit_bytes=VMEM_LIMIT),
        cost_estimate=pl.CostEstimate(flops=flops, bytes_accessed=1, transcendentals=1),
    )(
        *meta,
        *[
            x if i in smem_ins else held(x, pltpu.HBM if i in hbm_ins else pltpu.VMEM)
            for i, x in enumerate(ins)
        ],
        *[held(k) for k in kept],
    )
    return tuple(results[:n_out]), tuple(results[n_out:])


NORM_ROWS = 32
NORM_BACK_ROWS = 128


def norm_forward(inputs, branch, seq_len, vec, st, out, back=None):
    gain, shift = vec.gain, vec.shift
    sums = [0.0] * 4
    grads = []
    block = NORM_ROWS if back is None else NORM_BACK_ROWS
    for first in range(0, inputs.shape[0], block):
        rows = slice(first, first + block)
        part = branch[rows]
        resid = inputs[rows].astype(F32) + part
        mean = jnp.mean(resid, axis=-1, keepdims=True)
        centred = resid - mean
        var = jnp.mean(centred * centred, axis=-1, keepdims=True)
        inv_std = lax.rsqrt(var + EPS)
        xhat = centred * inv_std
        out[rows, :] = (xhat * gain + shift).astype(BF16)
        live = first + lax.broadcasted_iota(jnp.int32, resid.shape, 0) < seq_len
        sums[0] += jnp.sum(jnp.where(live, resid * resid, 0.0), axis=0, keepdims=True)
        sums[1] += jnp.sum(jnp.where(live, part * part, 0.0), axis=0, keepdims=True)
        if back is None:
            st.xhat[rows, :] = xhat
            st.inv_std[rows, :] = jnp.broadcast_to(inv_std, (block, st.inv_std.shape[1]))
        else:
            grads.append(norm_back_rows(back[rows].astype(F32), xhat, inv_std, gain, sums))
    st.add(RESID_SQ, sums[0])
    st.add(BRANCH_SQ, sums[1])
    if back is not None:
        st.add(GAIN, sums[2])
        st.add(SHIFT, sums[3])
        return jnp.concatenate(grads, axis=0)


def norm_back_rows(grad, xhat, inv_std, gain, sums):
    gy = grad * gain
    along = grad * xhat
    first = jnp.mean(gy, axis=-1, keepdims=True)
    second = jnp.mean(along * gain, axis=-1, keepdims=True)
    sums[2] += jnp.sum(along, axis=0, keepdims=True)
    sums[3] += jnp.sum(grad, axis=0, keepdims=True)
    return (gy - first - xhat * second) * inv_std


def norm_backward(grad, vec, st):
    gain = vec.gain
    sums = [0.0] * 4
    grads = []
    for first in range(0, grad.shape[0], NORM_BACK_ROWS):
        rows = slice(first, first + NORM_BACK_ROWS)
        grads.append(
            norm_back_rows(grad[rows].astype(F32), st.xhat[rows, :], st.inv_std[rows, 0:1], gain, sums)
        )
    st.add(GAIN, sums[2])
    st.add(SHIFT, sums[3])
    return jnp.concatenate(grads, axis=0)


class Vectors:
    def __init__(self, in_bias, out_bias, gain, shift, low_bias=None):
        self.refs = (in_bias, out_bias, gain, shift, low_bias)

    def in_bias(self, i, width):
        return self.refs[0][0:1, i * width : (i + 1) * width].astype(F32)

    def first_bias(self, i, width):
        return self.refs[4][0:1, :width].astype(F32) if i == 0 else self.in_bias(i - 1, width)

    out_bias = property(lambda self: self.refs[1][...].astype(F32))
    gain = property(lambda self: self.refs[2][...].astype(F32))
    shift = property(lambda self: self.refs[3][...].astype(F32))


class Store:
    def __init__(self, kept, j):
        acts, wide, aux, xhat, inv_std, grad_wide, grad_branch, sums = kept[:8]
        self.x, self.wide, self.aux, self.xhat, self.inv_std, self.gwide, self.db = (
            a.at[j] for a in (acts, wide, aux, xhat, inv_std, grad_wide, grad_branch)
        )
        self.sums, self.first = sums, j == 0

    def add(self, row, value):
        if self.first:
            self.sums[row : row + 1, :] = value
        else:
            self.sums[row : row + 1, :] = self.sums[row : row + 1, :] + value


def attend_forward(inputs, w, vec, seq_len, st, send, scratch):
    vt, ctxt = scratch[:2]
    rows, width = inputs.shape
    size = width // HEADS
    st.x[...] = inputs
    q = (dot_nn(inputs, w[:, :width]) + vec.in_bias(0, width)).astype(BF16) * jnp.asarray(size**-0.5, BF16)
    st.wide[:, :width] = q
    k = dot_nn(inputs, w[:, width : 2 * width]).astype(BF16)
    st.wide[:, width : 2 * width] = k
    v = (dot_nn(inputs, w[:, 2 * width : 3 * width]) + vec.in_bias(1, width)).astype(BF16)
    st.wide[:, 2 * width : 3 * width] = v
    vt[...] = v.T
    key_live = lax.broadcasted_iota(jnp.int32, (rows, rows), 0) < seq_len
    lane = lax.broadcasted_iota(jnp.int32, (rows, 2 * size), 1)
    def score(head):
        first = (head // 2) * 2 * size
        qp = q[:, first : first + 2 * size]
        kp = k[:, first : first + 2 * size]
        mine = (lane >= size) if head % 2 else (lane < size)
        return dot_nt(jnp.where(mine, kp, jnp.zeros_like(kp)), qp)

    ahead = score(0)
    for head in range(HEADS):
        scores = jnp.where(key_live, ahead, -1e30)
        if head + 1 < HEADS:
            ahead = score(head + 1)
        top = jnp.max(scores, axis=0, keepdims=True)
        expo = jnp.exp(scores - top)
        total = jnp.sum(expo, axis=0, keepdims=True)
        probs = (expo * (1.0 / total)).astype(BF16)
        st.aux[:, head * rows : (head + 1) * rows] = probs
        ctxt[head * size : (head + 1) * size, :] = dot_nn(
            vt[head * size : (head + 1) * size, :], probs
        ).astype(BF16)
    ctx = ctxt[...].T
    st.wide[:, 3 * width :] = ctx
    branch = dot_nn(ctx, w[:, 3 * width :]) + vec.out_bias
    norm_forward(inputs, branch, seq_len, vec, st, send)


def feed_branch(inputs, w, down, vec, st):
    width = inputs.shape[1]
    st.x[...] = inputs
    step = 2 * width

    def before(c):
        bias = jnp.concatenate([vec.first_bias(2 * c, width), vec.first_bias(2 * c + 1, width)], axis=1)
        return dot_nn(inputs, w[:, c * step : (c + 1) * step]) + bias

    branch = None
    ahead = before(0)
    for c in range(w.shape[1] // step):
        cols = slice(c * step, (c + 1) * step)
        x = ahead
        if cols.stop < w.shape[1]:
            ahead = before(c + 1)
        square = x * x
        t = jnp.tanh(x * (GELU_IN + GELU_CUBE * square))
        s = 0.5 + 0.5 * t
        act = x * s
        slope = s + act * (1.0 - t) * (GELU_IN + (3.0 * GELU_CUBE) * square)
        hidden = act.astype(BF16)
        st.wide[:, cols] = hidden
        st.aux[:, cols] = slope.astype(BF16)
        part = dot_nt(hidden, down[:, cols])
        branch = part if branch is None else branch + part
    return branch + vec.out_bias


def feed_forward(inputs, w, down, vec, seq_len, st, send):
    branch = feed_branch(inputs, w, down, vec, st)
    norm_forward(inputs, branch, seq_len, vec, st, send)


def feed_grads(dresid, w, down, st, send):
    width = dresid.shape[1]
    dbranch = dresid.astype(BF16)
    st.db[...] = dbranch
    total = dresid
    step = 2 * width
    ahead = dot_nn(dbranch, down[:, :step])
    for c in range(w.shape[1] // step):
        cols = slice(c * step, (c + 1) * step)
        dhidden = ahead
        if cols.stop < w.shape[1]:
            ahead = dot_nn(dbranch, down[:, cols.stop : cols.stop + step])
        dpre = (dhidden * st.aux[:, cols].astype(F32)).astype(BF16)
        st.gwide[:, cols] = dpre
        total = total + dot_nt(dpre, w[:, cols])
    send[...] = total.astype(BF16)


def feed_backward(grad, w, down, vec, st, send):
    dresid = norm_backward(grad, vec, st)
    feed_grads(dresid, w, down, st, send)


def feed_both(inputs, grad, w, down, vec, seq_len, st, y_out, send):
    branch = feed_branch(inputs, w, down, vec, st)
    dresid = norm_forward(inputs, branch, seq_len, vec, st, y_out, grad)
    feed_grads(dresid, w, down, st, send)


def attend_backward(grad, w, vec, st, send, scratch):
    kt, dqt = scratch[:2]
    rows, width = grad.shape
    size = width // HEADS
    dresid = norm_backward(grad, vec, st)
    dbranch = dresid.astype(BF16)
    st.gwide[:, 3 * width :] = dbranch
    dctx = dot_nt(dbranch, w[:, 3 * width :]).astype(BF16)
    q, v = st.wide[:, :width], st.wide[:, 2 * width : 3 * width]
    kt[...] = (st.wide[:, width : 2 * width] * jnp.asarray(size**-0.5, BF16)).T
    lane = lax.broadcasted_iota(jnp.int32, (rows, 2 * size), 1)
    none = jnp.zeros((rows, 2 * size), BF16)

    def own(value, head):
        first = (head // 2) * 2 * size
        mine = (lane >= size) if head % 2 else (lane < size)
        return jnp.where(mine, value[:, first : first + 2 * size], none)

    def probs_grad(head):
        first = (head // 2) * 2 * size
        return dot_nt(own(v, head), dctx[:, first : first + 2 * size])

    ahead = probs_grad(0)
    for head in range(HEADS):
        dprobs = ahead
        if head + 1 < HEADS:
            ahead = probs_grad(head + 1)
        probs_low = st.aux[:, head * rows : (head + 1) * rows]
        probs = probs_low.astype(F32)
        inner = jnp.sum(probs * dprobs, axis=0, keepdims=True)
        dscores = (probs * (dprobs - inner)).astype(BF16)
        dv_part = dot_nn(probs_low, own(dctx, head))
        dk_part = dot_nn(dscores, own(q, head))
        dqt[head * size : (head + 1) * size, :] = dot_nn(
            kt[head * size : (head + 1) * size, :], dscores
        ).astype(BF16)
        if head % 2 == 0:
            dv, dk = dv_part, dk_part
        else:
            at = width + (head // 2) * 2 * size
            st.gwide[:, at : at + 2 * size] = (dk + dk_part).astype(BF16)
            st.gwide[:, width + at : width + at + 2 * size] = (dv + dv_part).astype(BF16)
    dx = dresid + dot_nt(st.gwide[:, width : 3 * width], w[:, width : 3 * width])
    st.gwide[:, :width] = dqt[...].T
    send[...] = (dx + dot_nt(st.gwide[:, :width], w[:, :width])).astype(BF16)


def roles_of(slot, segments):
    last = segments - 1
    found = []
    for z in range(segments):
        j = slot - 2 * z
        if 0 <= j < segments:
            found.append((z, "both" if z == last else "forward", j))
        j = slot - (4 * last - 2 * z)
        if z < last and 0 <= j < segments:
            found.append((z, "backward", j))
    return found


def half_rows(meta, own, width):
    bit = lax.rem(meta[1], 2)
    bit = bit if own else 1 - bit
    return pl.multiple_of(bit * (width // 2), width // 2)


def weight_refs(lengths, kept):
    acts, wide, _, _, _, grad_wide, grad_branch, sums = kept[:8]
    return [lengths, acts, wide, grad_wide, grad_branch, sums]


def load_turned(at, source, lanes):
    rows = source.shape[1]
    for j in range(source.shape[0]):
        at[: lanes.size, j * rows : (j + 1) * rows] = source[j, :, lanes].T


def main_products(meta, refs, at, own, feed, sentences):
    _, acts, wide, grad_wide = refs[:4]
    rows, width = acts.shape[1:]
    half, full = width // 2, wide.shape[2]
    total = (sentences.stop - sentences.start) * rows
    start = half_rows(meta, own, width)
    at[half:, :total] = jnp.ones((at.shape[0] - half, total), BF16)
    load_turned(at, acts.at[sentences], pl.ds(start, half))
    for c in range(full // width):
        cols = slice(c * width, (c + 1) * width)
        if c == 3 and not feed:
            lanes = pl.ds(pl.multiple_of(3 * width + start, half), half)
            load_turned(at, wide.at[sentences], lanes)
        yield c, cols, dot_nn(at[:, :total], grad_wide[sentences, :, cols].reshape(total, width))


def side_products(meta, refs, at, own, sentences):
    wide, _, grad_branch = refs[2:5]
    rows, width = grad_branch.shape[1:]
    half, full = width // 2, wide.shape[2]
    total = (sentences.stop - sentences.start) * rows
    load_turned(at, grad_branch.at[sentences], pl.ds(half_rows(meta, own, width), half))
    for c in range(full // width):
        cols = slice(c * width, (c + 1) * width)
        yield c, cols, dot_nn(at[:half, :total], wide[sentences, :, cols].reshape(total, width))


def early_sums(feed, stop):
    def body(meta, ins, outs, kept, scratch):
        lengths = ins[0]
        refs = weight_refs(lengths, kept)
        for own in range(2):
            for _, cols, grad in main_products(meta, refs, scratch[0], bool(own), feed, slice(0, stop)):
                outs[0][own, :, cols] = grad
            if feed:
                for _, cols, grad in side_products(meta, refs, scratch[0], bool(own), slice(0, stop)):
                    outs[1][own, :, cols] = grad

    return body


def main_half(own, feed, first=0, early=None):
    def body(meta, refs, out, scratch):
        lengths, acts, wide, _, grad_branch, sums = refs
        at, sm = scratch
        count, rows, width = acts.shape
        half, full = width // 2, wide.shape[2]
        sm[...] = jnp.zeros_like(sm)
        sm[:SMALLS, :] = sums[...]
        tokens = jnp.sum(lengths[:, 0:1].astype(F32), axis=0, keepdims=True)
        sm[COUNT : COUNT + 1, :] = jnp.broadcast_to(tokens, (1, width))
        for c, cols, grad in main_products(meta, refs, at, own, feed, slice(first, count)):
            if early is not None:
                grad = grad + early[int(own), :, cols]
            out[:, cols] = grad[:half].astype(BF16)
            place = BIAS + (3, 0, 1, 2)[c] if feed else (BIAS, None, BIAS + 1, OUT_BIAS)[c]
            if place is not None:
                sm[place : place + 1, :] = grad[half : half + 1]
        if feed:
            sm[OUT_BIAS : OUT_BIAS + 1, :] = jnp.sum(
                grad_branch[...].reshape(count * rows, width).astype(F32), axis=0, keepdims=True
            )
        out[:, full:] = sm[:, pl.ds(half_rows(meta, own, width), half)].T.astype(BF16)

    return body


def side_half(own, first, early):
    def body(meta, refs, out, scratch):
        wide, grad_wide, grad_branch = refs[2:5]
        at, sm = scratch
        count, rows, width = grad_branch.shape
        half, full, total = width // 2, wide.shape[2], count * rows
        sm[...] = jnp.broadcast_to(
            jnp.sum(
                grad_wide[:, :, :width].reshape(total, width).astype(F32), axis=0, keepdims=True
            ),
            sm.shape,
        )
        mine = pl.ds(half_rows(meta, own, width), half)
        out[:, full // 2 : full // 2 + LANES] = sm[:, mine].T.astype(BF16)
        for c, cols, grad in side_products(meta, refs, at, own, slice(first, count)):
            put = c * width + (LANES if c * width >= full // 2 else 0)
            out[:, put : put + width] = (grad + early[int(own), :, cols]).astype(BF16)

    return body


def core_add(masks):
    def body(meta, ins, outs, kept, scratch):
        size = outs[0].shape[0]
        chip = lax.div(meta[1], 2)
        for mask, out in zip(masks, outs, strict=True):
            rows = pl.ds(pl.multiple_of(jnp.bitwise_xor(chip, mask // 2) * size, size), size)
            at = 0
            for keep, got in zip(ins[0::2], ins[1::2], strict=True):
                cols = slice(at, at + keep.shape[1])
                at += keep.shape[1]
                out[:, cols] = (keep[rows, :].astype(F32) + got[rows, :].astype(F32)).astype(BF16)

    return body


def summed(refs, cols):
    total = refs[0][:, cols].astype(F32)
    for r in refs[1:]:
        total = total + r[:, cols].astype(F32)
    return total.astype(BF16)


def chip_sum(meta, ins, outs, kept, scratch):
    at = 0
    for out in outs or kept:
        out[...] = summed(ins, slice(at, at + out.shape[1]))
        at += out.shape[1]


def added(one, two, rows):
    return (one[rows, :].astype(F32) + two[rows, :].astype(F32)).astype(BF16)


def first_cut(meta, ins, outs, kept, scratch):
    keep, got = ins
    upper_stay, upper_go, lower_stay, lower_go = outs
    size = upper_stay.shape[0]
    half = size // 2
    chip = lax.div(meta[1], 2)
    x, y = lax.rem(chip, 2), lax.div(chip, 2)
    for other in range(2):
        put = slice(other * half, (other + 1) * half)
        for out, q, low in (
            (upper_go, 2 * other + 1 - x, 0),
            (lower_go, 2 * (1 - y) + other, half),
            (upper_stay, 2 * other + x, 0),
            (lower_stay, 2 * y + other, half),
        ):
            out[put, :] = added(keep, got, pl.ds(pl.multiple_of(q * size + low, half), half))


def second_cut(meta, ins, outs, kept, scratch):
    upper, upper_got, lower, lower_got = ins
    half = outs[0].shape[0]
    chip = lax.div(meta[1], 2)
    x, y = lax.rem(chip, 2), lax.div(chip, 2)
    for one, two, bit, stay, go in (
        (upper, upper_got, y, outs[0], outs[1]),
        (lower, lower_got, x, outs[2], outs[3]),
    ):
        go[...] = added(one, two, pl.ds(pl.multiple_of((1 - bit) * half, half), half))
        stay[...] = added(one, two, pl.ds(pl.multiple_of(bit * half, half), half))


def cut_sum(meta, ins, outs, kept, scratch):
    half = ins[0].shape[0]
    for i in range(2):
        at = 0
        for out in outs:
            cols = slice(at, at + out.shape[1])
            out[i * half : (i + 1) * half, :] = summed(ins[2 * i : 2 * i + 2], cols)
            at += out.shape[1]


def cross_message(meta, ins, outs, kept, scratch):
    low, grad = ins
    (out,) = outs
    size, width = low.shape[0], out.shape[1]

    @pl.when(lax.rem(meta[0], 2) == 1)
    def _():
        for i in range(0, low.shape[1], width):
            cols = min(width, low.shape[1] - i)
            out[i // width * size : (i // width + 1) * size, :cols] = low[:, i : i + cols]

    @pl.when(meta[0] == 0)
    def _():
        out[...] = grad[...]


def side_share(meta, ins, outs, kept, scratch):
    high, message = ins
    (out,) = outs
    half = high.shape[1]

    @pl.when(lax.rem(meta[0], 2) == 1)
    def _():
        out[:, :half] = high[...]
        out[:, half:] = jnp.zeros((out.shape[0], out.shape[1] - half), BF16)

    @pl.when(lax.rem(meta[0], 2) == 0)
    def _():
        size, width = out.shape[0], message.shape[1]
        for i in range(0, out.shape[1], width):
            cols = min(width, out.shape[1] - i)
            out[:, i : i + cols] = message[i // width * size : (i // width + 1) * size, :cols]


def block_row(meta, mask, width, size):
    chip, core = lax.div(meta[1], 2), lax.rem(meta[1], 2)
    side = jnp.bitwise_xor(core, mask % 2)
    at = side * (width // 2) + jnp.bitwise_xor(chip, mask // 2) * size
    return pl.multiple_of(at, size)


def load_lent(side, in_bias, share, sems, first, meta):
    width, block = side.shape[0], share.shape[0] - 16
    rows = pl.ds(half_rows(meta, True, width), block)
    copy = pltpu.make_async_copy(side.at[rows], share.at[:block], sems.at[first])
    copy.start()
    share[block:, width:] = jnp.zeros((16, share.shape[1] - width), BF16)
    share[block:, :width] = jnp.broadcast_to(in_bias[:, 2 * width :], (16, width))
    return copy


def begin_sending(meta, ins, outs, kept, scratch):
    side, in_bias, tokens = ins
    share, bias_v, tokens_v = outs
    sems = scratch[-1]
    copies = [
        pltpu.make_async_copy(in_bias, bias_v, sems.at[0]),
        pltpu.make_async_copy(tokens, tokens_v, sems.at[1]),
    ]
    for c in copies:
        c.start()
    copies[0].wait()
    load_lent(side, bias_v, share, sems, 2, meta).wait()
    copies[1].wait()


def begin(meta, ins, outs, kept, scratch):
    lens, side, bias_v, *rest = ins
    again, zero_sums, lens_v, *outs = outs
    sems = scratch[-1]
    copies = [
        pltpu.make_async_copy(src, dst, sems.at[i])
        for i, (src, dst) in enumerate(zip(rest, outs[: len(rest)], strict=True))
    ]
    for c in copies:
        c.start()
    copies.append(load_lent(side, bias_v, again, sems, len(rest), meta))
    zero_sums[...] = jnp.zeros_like(zero_sums)
    for j in range(lens_v.shape[0]):
        lens_v[j : j + 1, :] = jnp.full((1, LANES), lens[j], jnp.int32)
    for c in copies:
        c.wait()


def join_down(meta, ins, outs, kept, scratch):
    lent, other, side = ins
    down, low_bias = kept
    width, half = side.shape
    block = width // 2
    copy = pltpu.make_async_copy(side, down.at[:, half:], scratch[-1].at[0])
    copy.start()
    down[pl.ds(half_rows(meta, True, width), block), :half] = lent[:block]
    down[pl.ds(half_rows(meta, False, width), block), :half] = other[:block]
    low_bias[...] = lent[block:, :width]
    copy.wait()


class Results:
    def __init__(self, sems):
        self.sems, self.copies = sems, []

    def out(self, src, dst):
        self.picked([src], dst, None)

    def picked(self, refs, dst, which):
        sem = self.sems.at[len(self.copies)]
        for j, r in enumerate(refs):
            start = pltpu.make_async_copy(r, dst, sem).start
            start() if which is None else pl.when(which == j)(start)
        self.copies.append(pltpu.make_async_copy(refs[0], dst, sem))

    def finish(self):
        for c in self.copies:
            c.wait()


def widen_main(masks, segments):
    def body(meta, ins, outs, kept, scratch):
        n = len(masks)
        blocks, finals, backs = ins[:n], ins[n : n + segments], ins[n + segments :]
        out_y, out_g, main_h, out_b, gain_h, shift_h, stats_h, small_v = outs
        full, cols, stat, sems = scratch
        res = Results(sems)
        res.picked(finals, out_y, meta[0])
        res.picked(backs, out_g, meta[0])
        width, main = main_h.shape[1], main_h.shape[2]
        size = blocks[0].shape[0]
        for i, mask in enumerate(masks):
            at = block_row(meta, mask, width, size)
            cols[pl.ds(at, size), :] = blocks[i][:, main:]
            full[i] = blocks[i][:, :main].astype(F32)
            res.out(full.at[i], main_h.at[0, pl.ds(at, size)])
        small = cols[...].T.astype(F32)
        small_v[...] = small[: small_v.shape[0]]
        squares = jnp.sum(small[RESID_SQ : BRANCH_SQ + 1], axis=1, keepdims=True)
        values = jnp.sqrt(squares / (small[COUNT : COUNT + 1, 0:1] * width))
        lane = lax.broadcasted_iota(jnp.int32, (1, LANES), 1)
        stat[...] = jnp.where(lane == 0, values[0:1], values[1:2])
        res.out(small_v.at[OUT_BIAS : OUT_BIAS + 1], out_b)
        res.out(small_v.at[GAIN : GAIN + 1], gain_h)
        res.out(small_v.at[SHIFT : SHIFT + 1], shift_h)
        res.out(stat, stats_h)
        res.finish()

    return body


def widen_side(masks):
    def body(meta, ins, outs, kept, scratch):
        *blocks, small = ins
        side_h, in_b = outs
        full, cols, vecs, sems = scratch
        res = Results(sems)
        width, half = side_h.shape[1], side_h.shape[2]
        size = blocks[0].shape[0]
        for i, mask in enumerate(masks):
            at = block_row(meta, mask, width, size)
            cols[pl.ds(at, size), :] = blocks[i][:, half:]
            full[i] = blocks[i][:, :half].astype(F32)
            res.out(full.at[i], side_h.at[0, pl.ds(at, size)])
        lent = cols[...].T.astype(F32)[0:1]
        feed = jnp.full((1, width), lax.rem(meta[0], 2), jnp.int32) == 1
        vecs[0:1, :width] = small[BIAS : BIAS + 1]
        vecs[0:1, width : 2 * width] = small[BIAS + 1 : BIAS + 2]
        vecs[0:1, 2 * width :] = jnp.where(feed, small[BIAS + 2 : BIAS + 3], lent)
        res.out(vecs.at[0:1], in_b)
        res.finish()

    return body


def on_device(
    tokens, lengths, cotangent, main_weight, side_weight, in_bias, out_bias, norm_gain, norm_shift
):
    segments, shards = lax.axis_size("segment"), lax.axis_size("dp")
    z, d = lax.axis_index("segment"), lax.axis_index("dp")
    rows, width = tokens.shape
    main_mat, side_mat = main_weight[0], side_weight[0]
    hidden = main_mat.shape[1]
    half_width = side_mat.shape[1]
    block = width // shards
    last = segments - 1
    feeds = tuple(range(1, segments, 2))
    chip_masks = tuple(range(0, shards, 2))
    masks = chip_masks + tuple(m + 1 for m in chip_masks)
    meta = (z.reshape(1), d.reshape(1))

    def hop(value, *pairs):
        return lax.ppermute(value, "segment", list(pairs))

    def swap(value, mask):
        return lax.ppermute(value, "dp", [(i, i ^ mask) for i in range(shards)])

    ext = hidden + LANES
    low_ext = half_width + LANES
    kept_shapes = [
        ((segments, rows, width), BF16),
        ((segments, rows, hidden), BF16),
        ((segments, rows, hidden), BF16),
        ((segments, rows, width), F32),
        ((segments, rows, LANES), F32),
        ((segments, rows, hidden), BF16),
        ((segments, rows, width), BF16),
        ((2, rows, width), BF16),
    ]
    lent = ((width // 2 + 16, half_width), BF16)
    borrowed_shapes = [((width, hidden), BF16), ((16, width), BF16)]
    narrow = ((rows, width), BF16)
    (share, bias_v, tokens_v), _ = kernel_call(
        begin_sending, meta, [side_mat, in_bias, tokens], [lent, (in_bias.shape, BF16), narrow],
        copies=3, hbm_ins=(0, 1, 2),
    )
    loads = [out_bias, norm_gain, norm_shift, main_mat, cotangent, cotangent]
    loaded, _ = kernel_call(
        begin, meta, [lengths.reshape(segments), side_mat, bias_v, *loads],
        [lent, ((SMALLS, width), F32), ((segments, LANES), jnp.int32)]
        + [(x.shape, x.dtype) for x in loads]
        + kept_shapes + borrowed_shapes,
        copies=1 + len(loads), smem_ins=(0,), hbm_ins=(1, *range(3, 3 + len(loads))), flops=SLOT_FLOPS,
    )
    later_share, sums, lengths_v, *loaded = loaded
    out_bias_v, gain_v, shift_v, main_v, cotangent_v, later_cotangent, *kept = loaded
    *kept, saved, down, low_bias = kept
    kept, borrowed = (*kept, sums, saved), (down, low_bias)

    turns = tuple(range(last, -1, -1))
    first_share = hop(share, (0, 1))
    first_in = [hop(tokens_v, (home, 0)) for home in turns[:2]]
    riders = {
        0: [(turns[2], 0, "tokens"), (turns[1], last, "cotangent")],
        1: [(turns[2], last, "cotangent")],
    }

    def join(s, share, other, blank):
        return kernel_call(
            join_down, meta, [share, other, side_mat], [], kept=blank, hbm_ins=(2,), copies=1, where=(s,)
        )[1]

    turned = ((width, rows), BF16)
    n_chip = len(chip_masks)
    weight_scratch = [((width // 2 + 16, segments * rows), BF16), ((LANES, width), F32)]

    slots = 4 * last + segments
    waves, sent, finals = {}, {}, []
    after, last_in = {}, []
    side, main = [], []
    half_out = ((width // 2, ext), BF16)

    def hops_after(slot):
        pairs = []
        for z_role, what, j in roles_of(slot, segments):
            if what == "forward":
                pairs.append((z_role, z_role + 1))
            elif z_role > 0:
                pairs.append((z_role, z_role - 1))
            elif turns[j] > 0:
                pairs.append((z_role, turns[j]))
        return pairs + [(source, to) for source, to, _ in riders.get(slot, ())]

    homeward = {}
    for slot in range(2 * last + segments + 2, slots):
        taken = [to for _, to in hops_after(slot)]
        free = [home for home in range(1, last) if home not in taken and home not in homeward.values()]
        if free:
            homeward[slot] = free[-1]
    for slot in range(slots):
        roles = roles_of(slot, segments)
        uses = [r[1] for r in roles]
        attends = any(r[0] % 2 == 0 for r in roles)
        feed_roles = any(r[0] % 2 == 1 for r in roles)
        names, ins = [], []

        def give(name, value):
            names.append(name)
            ins.append(value)

        for name, value in zip(
            ("main", "in_bias", "out_bias", "gain", "shift", "lengths"),
            (main_v, bias_v, out_bias_v, gain_v, shift_v, lengths_v),
        ):
            give(name, value)
        if feed_roles and slot != last + 2:
            give("down", down)
            give("low_bias", low_bias)
        if slot < 2:
            give("first", first_in[slot])
            give("cotangent", cotangent_v)
        if slot in (0, last):
            give("tokens", tokens_v)
        if slot - 2 in waves:
            give("wave", waves[slot - 2])
        if "both" in uses and slot - 2 * last in (0, last):
            give("last", last_in[slot - 2 * last])
        if slot in homeward:
            give("home", finals[turns.index(homeward[slot])])
        outs = [narrow] + ([narrow] if "both" in uses else [])
        weighing = slots - 2 <= slot
        if weighing:
            give("early_side", early_side)
            give("early_main", early_main)
            outs += [half_out] * (4 if slot == slots - 2 else 0)

        def body(
            meta, in_refs, out_refs, kept_refs, scratch, slot=slot, roles=roles, names=tuple(names)
        ):
            ref = dict(zip(names, in_refs))
            if slot == last + 2:
                ref["down"], ref["low_bias"] = kept_refs[-2:]
            vec = Vectors(
                ref["in_bias"], ref["out_bias"], ref["gain"], ref["shift"], ref.get("low_bias")
            )
            for z_role, what, j in roles:

                @pl.when(meta[0] == z_role)
                def _(z_role=z_role, what=what, j=j):
                    st = Store(kept_refs, j)
                    seq_len = ref["lengths"][turns[j] : turns[j] + 1, 0:1]
                    w, send = ref["main"], out_refs[0]
                    if what == "backward":
                        if z_role % 2:
                            feed_backward(ref["wave"][...], w, ref["down"], vec, st, send)
                        else:
                            attend_backward(ref["wave"][...], w, vec, st, send, scratch)
                        return
                    own = slot == last and z_role == 0
                    inputs = ref["tokens" if own else "first" if "first" in ref else "wave"][...]
                    if what == "both":
                        feed_both(
                            inputs, ref["last"][...] if "last" in ref else kept_refs[8][j - 1], w, ref["down"], vec, seq_len, st, out_refs[1], send
                        )
                    elif z_role % 2:
                        feed_forward(inputs, w, ref["down"], vec, seq_len, st, send)
                    else:
                        attend_forward(inputs, w, vec, seq_len, st, send, scratch)

            for source, _, what in riders.get(slot, ()):

                @pl.when(meta[0] == source)
                def _(what=what):
                    out_refs[0][...] = ref[what][...]

            if slot in (2, 3):

                @pl.when(meta[0] == last)
                def _():
                    kept_refs[8][slot - 2] = ref["wave"][...]

            if "home" in ref:

                @pl.when(meta[0] == last)
                def _():
                    out_refs[0][...] = ref["home"][...]

            if weighing:
                sums = weight_refs(ref["lengths"], kept_refs)
                first = slot == slots - 2
                sides, mains = (out_refs[-4:-2], out_refs[-2:]) if first else ((), kept_refs[-2:])
                feed_here = lax.rem(meta[0], 2) == 1

                @pl.when(feed_here)
                def _():
                    for own in range(2):
                        if first:
                            side_half(bool(own), FEED_EARLY, ref["early_side"])(
                                meta, sums, sides[own], scratch[-2:]
                            )
                        else:
                            main_half(bool(own), True, FEED_EARLY, ref["early_main"])(
                                meta, sums, mains[own], scratch[-2:]
                            )

                if first:

                    @pl.when(jnp.logical_not(feed_here) & (meta[0] > 0))
                    def _():
                        for own in range(2):
                            main_half(bool(own), False)(meta, sums, mains[own], scratch[-2:])

        scratch = [turned, turned, narrow] if attends else []
        if weighing:
            scratch = scratch + weight_scratch
        extra = ()
        if slot in (1, last + 1):
            extra = (later_share,)
        elif slot == last + 2:
            extra = (down, low_bias)
        elif slot == slots - 1:
            extra = (*main,)
        res, kept = kernel_call(
            body, meta, ins, outs, scratch, (*kept, *extra), after=after.get(slot, ()), flops=SLOT_FLOPS
        )
        if slot == 2:
            last_in += [cotangent_v, None, None]
        if slot == 2 * last:
            _, (*kept, later_cotangent) = kernel_call(
                lambda *_: None, meta, [], [], kept=(*kept, later_cotangent), after=[waves[slot - 1]]
            )
            last_in.append(hop(later_cotangent, (0, last)))
        if slot == slots - 1:
            *kept, main[0], main[1] = kept
        if slot == 0:
            _, (*kept, first_share) = kernel_call(lambda *_: None, meta, [], [], kept=(*kept, first_share))
            down, low_bias = join(1, first_share, swap(first_share, 1), borrowed)
        if slot == 1:
            *kept, later_share = kept
            later_share = hop(later_share, (last - 1, last))
        if slot == last + 1:
            *kept, later_share = kept
            later_half = swap(later_share, 1)
        if slot == last + 2:
            *kept, down, low_bias = kept
            down, low_bias = join(last, later_share, later_half, (down, low_bias))
        sent[slot] = res[0]
        if slot == slots - segments - 1:
            early_shapes = [((2, width // 2 + extra_rows, hidden), F32) for extra_rows in (16, 0)]
            (early_main, early_side), kept = kernel_call(
                early_sums(True, FEED_EARLY), meta, [lengths_v], early_shapes, weight_scratch, kept, where=feeds
            )
        if slot == slots - 2:
            side, main = list(res[-4:-2]), list(res[-2:])

            def early_attend(meta, ins, outs, kept, scratch):
                early_sums(False, ATTEND_EARLY)(meta, ins, kept[-1:], kept, scratch)

            _, (*kept, early_main) = kernel_call(
                early_attend, meta, [lengths_v], [], weight_scratch, (*kept, early_main), where=(0,)
            )
        if "both" in uses:
            finals.append(res[1])
        pairs = hops_after(slot)
        if slot in homeward:
            pairs.append((last, homeward[slot]))
        if pairs and slot != slots - 2:
            waves[slot] = hop(res[0], *pairs)
    def weigh(own, after):
        def body(meta, ins, outs, kept, scratch):
            main_half(bool(own), False, ATTEND_EARLY, ins[-1])(meta, ins[:-1], kept[0], scratch)

        _, (main[own],) = kernel_call(
            body, meta, [*weight_refs(lengths_v, kept), early_main], [], weight_scratch,
            (main[own],), where=(0,), after=after,
        )

    def add_cores(keep, got, segs, after=()):
        blocks, _ = kernel_call(
            core_add(chip_masks), meta, [keep, got], [((block, keep.shape[1]), BF16)] * n_chip,
            where=segs, after=after,
        )
        return [blocks[0]] + [swap(blocks[i], chip_masks[i]) for i in range(n_chip - 1, 0, -1)]

    def add_in_steps(keep, got, segs, after=()):
        rows_of = (keep.shape[0] // 4, keep.shape[1])
        (up, up_go, down, down_go), _ = kernel_call(
            first_cut, meta, [keep, got], [(rows_of, BF16)] * 4, where=segs, after=after
        )
        rows_of = (rows_of[0] // 2, rows_of[1])
        (up, up_go, down, down_go), _ = kernel_call(
            second_cut, meta, [up, swap(up_go, 2), down, swap(down_go, 4)],
            [(rows_of, BF16)] * 4, where=segs,
        )
        return [up, swap(up_go, 4), down, swap(down_go, 2)]

    reduce, last_sum = (add_in_steps, cut_sum) if n_chip == 4 else (add_cores, chip_sum)
    side_got = swap(side[0], 1)
    weigh(0, [side_got])
    main_got = swap(main[0], 1)
    side_blocks = reduce(side[1], side_got, feeds, [main[0]])
    weigh(1, [side_blocks[0]] if n_chip != 4 else [])
    main_blocks = reduce(main[1], main_got, None)
    (low_own, high_own), _ = kernel_call(
        last_sum, meta, side_blocks, [((block, low_ext), BF16), ((block, half_width), BF16)], where=feeds,
        after=main_blocks[:1],
    )
    (total,), _ = kernel_call(last_sum, meta, main_blocks, [((block, ext), BF16)])
    (message,), _ = kernel_call(cross_message, meta, [low_own, sent[slots - 2]], [narrow])
    waves[slots - 2] = hop(message, *[(s, s - 1) for s in feeds], (0, turns[-2]))
    first_home = hop(finals[turns.index(0)], (last, 0))
    outputs_at = [first_home] + [
        waves[next(k for k, v in homeward.items() if v == s)] for s in range(1, last)
    ]
    outputs_at.append(finals[turns.index(last)])
    start = slots - segments
    grads_at = [sent[slots - 1]] + [waves[start + turns.index(s)] for s in range(1, segments)]

    def gather(share):
        blocks = [share] + [swap(share, m) for m in reversed(chip_masks[1:])]
        blocks = [blocks[0], *reversed(blocks[1:])]
        return blocks + [swap(b, 1) for b in blocks]

    main_all = gather(total)
    (side_mine,), _ = kernel_call(
        side_share, meta, [high_own, waves[slots - 2]], [((block, low_ext), BF16)],
        after=[main_all[2]],
    )
    (out_y, out_g, main_grad, out_bias_grad, gain_grad, shift_grad, stats, small), _ = kernel_call(
        widen_main(masks, segments), meta, [*main_all, *outputs_at, *grads_at],
        [narrow, narrow, ((1, width, hidden), F32)]
        + [((1, width), F32)] * 3
        + [((1, LANES), F32), ((SMALLS, width), F32)],
        [((shards, block, hidden), F32), ((width, LANES), BF16), ((1, LANES), F32)],
        copies=shards + 6, hbm_outs=tuple(range(7)),
    )
    (side_grad, in_bias_grad), _ = kernel_call(
        widen_side(masks), meta, [*gather(side_mine), small],
        [((1, width, half_width), F32), ((1, 3 * width), F32)],
        [((shards, block, half_width), F32), ((width, LANES), BF16), ((8, 3 * width), F32)],
        copies=shards + 1, hbm_outs=(0, 1),
    )
    return (
        out_y, out_g, main_grad, side_grad, in_bias_grad, out_bias_grad, gain_grad, shift_grad, stats[:, :2]
    )


def solution(mesh):
    over = P(("segment", "dp"), None)
    by_segment = [P("segment", None, None)] * 2 + [P("segment", None)] * 4
    in_specs = (over, P(None, "dp"), over, *by_segment)
    out_specs = (over, over, *by_segment, P("segment", None))
    return jax.shard_map(
        on_device, mesh=mesh, in_specs=in_specs, out_specs=out_specs, check_vma=False
    )
```

```python
import functools

import jax
import jax.numpy as jnp
from jax import lax
from jax.experimental import pallas as pl
from jax.experimental.pallas import tpu as pltpu
from jax.sharding import PartitionSpec as P

HEADS = 8
EPS = 1e-05
LANES = 128
VMEM_LIMIT = 12 * 1024 * 1024
SLOT_FLOPS = 40 * 10**9
FEED_EARLY, ATTEND_EARLY = 2, 2
F32 = jnp.float32
BF16 = jnp.bfloat16
GELU_IN = 0.7978845608028654
GELU_CUBE = 0.044715 * GELU_IN

BIAS, OUT_BIAS, GAIN, SHIFT, RESID_SQ, BRANCH_SQ, COUNT, SMALLS = 0, 4, 5, 6, 7, 8, 9, 16


def dot_nn(left, right):
    return jnp.dot(left, right, preferred_element_type=F32)


def dot_nt(left, right):
    return lax.dot_general(left, right, (((1,), (1,)), ((), ())), preferred_element_type=F32)


def kernel_call(
    body, meta, ins, outs, scratch=(), kept=(), copies=0, hbm_ins=(), smem_ins=(), hbm_outs=(), where=None,
    after=(), flops=1,
):
    ins = [*ins, *after]
    n_in, n_kept, n_out = len(ins), len(kept), len(outs)

    def kernel(z_ref, d_ref, *refs):
        at = 0
        groups = []
        for n in (n_in, n_kept, n_out, n_kept):
            groups.append(refs[at : at + n])
            at += n

        def run():
            body((z_ref[0], d_ref[0]), groups[0][: n_in - len(after)], groups[2], groups[3], refs[at:])

        if where is None:
            run()
        else:
            here = z_ref[0] == where[0]
            for other in where[1:]:
                here = here | (z_ref[0] == other)
            pl.when(here)(run)

    smem = pl.BlockSpec(memory_space=pltpu.SMEM)
    vmem = pl.BlockSpec(memory_space=pltpu.VMEM)
    hbm = pl.BlockSpec(memory_space=pltpu.HBM)

    def held(x, space=pltpu.VMEM):
        return pltpu.with_memory_space_constraint(x, space)

    results = pl.pallas_call(
        kernel,
        out_shape=[
            jax.ShapeDtypeStruct(*o) if i in hbm_outs else pltpu.VMEM(*o) for i, o in enumerate(outs)
        ]
        + [pltpu.VMEM(k.shape, k.dtype) for k in kept],
        in_specs=[smem] * 2
        + [smem if i in smem_ins else hbm if i in hbm_ins else vmem for i in range(n_in)]
        + [vmem] * n_kept,
        out_specs=[hbm if i in hbm_outs else vmem for i in range(n_out)] + [vmem] * n_kept,
        scratch_shapes=[pltpu.VMEM(*s) for s in scratch]
        + ([pltpu.SemaphoreType.DMA((copies,))] if copies else []),
        input_output_aliases={2 + n_in + i: n_out + i for i in range(n_kept)},
        compiler_params=pltpu.CompilerParams(vmem_limit_bytes=VMEM_LIMIT),
        cost_estimate=pl.CostEstimate(flops=flops, bytes_accessed=1, transcendentals=1),
    )(
        *meta,
        *[
            x if i in smem_ins else held(x, pltpu.HBM if i in hbm_ins else pltpu.VMEM)
            for i, x in enumerate(ins)
        ],
        *[held(k) for k in kept],
    )
    return tuple(results[:n_out]), tuple(results[n_out:])


NORM_ROWS = 32
NORM_BACK_ROWS = 64


def norm_forward(inputs, branch, seq_len, vec, st, out, back=None):
    gain, shift = vec.gain, vec.shift
    sums = [0.0] * 4
    grads = []
    block = NORM_ROWS if back is None else NORM_BACK_ROWS
    for first in range(0, inputs.shape[0], block):
        rows = slice(first, first + block)
        part = branch[rows]
        resid = inputs[rows].astype(F32) + part
        mean = jnp.mean(resid, axis=-1, keepdims=True)
        centred = resid - mean
        var = jnp.mean(centred * centred, axis=-1, keepdims=True)
        inv_std = lax.rsqrt(var + EPS)
        xhat = centred * inv_std
        out[rows, :] = (xhat * gain + shift).astype(BF16)
        live = first + lax.broadcasted_iota(jnp.int32, resid.shape, 0) < seq_len
        sums[0] += jnp.sum(jnp.where(live, resid * resid, 0.0), axis=0, keepdims=True)
        sums[1] += jnp.sum(jnp.where(live, part * part, 0.0), axis=0, keepdims=True)
        if back is None:
            st.xhat[rows, :] = xhat
            st.inv_std[rows, :] = jnp.broadcast_to(inv_std, (block, st.inv_std.shape[1]))
        else:
            grads.append(norm_back_rows(back[rows].astype(F32), xhat, inv_std, gain, sums))
    st.add(RESID_SQ, sums[0])
    st.add(BRANCH_SQ, sums[1])
    if back is not None:
        st.add(GAIN, sums[2])
        st.add(SHIFT, sums[3])
        return jnp.concatenate(grads, axis=0)


def norm_back_rows(grad, xhat, inv_std, gain, sums):
    gy = grad * gain
    along = grad * xhat
    first = jnp.mean(gy, axis=-1, keepdims=True)
    second = jnp.mean(along * gain, axis=-1, keepdims=True)
    sums[2] += jnp.sum(along, axis=0, keepdims=True)
    sums[3] += jnp.sum(grad, axis=0, keepdims=True)
    return (gy - first - xhat * second) * inv_std


def norm_backward(grad, vec, st):
    gain = vec.gain
    sums = [0.0] * 4
    grads = []
    for first in range(0, grad.shape[0], NORM_BACK_ROWS):
        rows = slice(first, first + NORM_BACK_ROWS)
        grads.append(
            norm_back_rows(grad[rows].astype(F32), st.xhat[rows, :], st.inv_std[rows, 0:1], gain, sums)
        )
    st.add(GAIN, sums[2])
    st.add(SHIFT, sums[3])
    return jnp.concatenate(grads, axis=0)


class Vectors:
    def __init__(self, in_bias, out_bias, gain, shift, low_bias=None):
        self.refs = (in_bias, out_bias, gain, shift, low_bias)

    def in_bias(self, i, width):
        return self.refs[0][0:1, i * width : (i + 1) * width].astype(F32)

    def first_bias(self, i, width):
        return self.refs[4][0:1, :width].astype(F32) if i == 0 else self.in_bias(i - 1, width)

    out_bias = property(lambda self: self.refs[1][...].astype(F32))
    gain = property(lambda self: self.refs[2][...].astype(F32))
    shift = property(lambda self: self.refs[3][...].astype(F32))


class Store:
    def __init__(self, kept, j):
        acts, wide, aux, xhat, inv_std, grad_wide, grad_branch, sums = kept[:8]
        self.x, self.wide, self.aux, self.xhat, self.inv_std, self.gwide, self.db = (
            a.at[j] for a in (acts, wide, aux, xhat, inv_std, grad_wide, grad_branch)
        )
        self.sums, self.first = sums, j == 0

    def add(self, row, value):
        if self.first:
            self.sums[row : row + 1, :] = value
        else:
            self.sums[row : row + 1, :] = self.sums[row : row + 1, :] + value


def attend_forward(inputs, w, vec, seq_len, st, send, scratch):
    vt, ctxt = scratch[:2]
    rows, width = inputs.shape
    size = width // HEADS
    st.x[...] = inputs
    q = (dot_nn(inputs, w[:, :width]) + vec.in_bias(0, width)).astype(BF16) * jnp.asarray(size**-0.5, BF16)
    st.wide[:, :width] = q
    k = dot_nn(inputs, w[:, width : 2 * width]).astype(BF16)
    st.wide[:, width : 2 * width] = k
    v = (dot_nn(inputs, w[:, 2 * width : 3 * width]) + vec.in_bias(1, width)).astype(BF16)
    st.wide[:, 2 * width : 3 * width] = v
    vt[...] = v.T
    key_live = lax.broadcasted_iota(jnp.int32, (rows, rows), 0) < seq_len
    lane = lax.broadcasted_iota(jnp.int32, (rows, 2 * size), 1)
    def score(head):
        first = (head // 2) * 2 * size
        qp = q[:, first : first + 2 * size]
        kp = k[:, first : first + 2 * size]
        mine = (lane >= size) if head % 2 else (lane < size)
        return dot_nt(jnp.where(mine, kp, jnp.zeros_like(kp)), qp)

    ahead = score(0)
    for head in range(HEADS):
        scores = jnp.where(key_live, ahead, -1e30)
        if head + 1 < HEADS:
            ahead = score(head + 1)
        top = jnp.max(scores, axis=0, keepdims=True)
        expo = jnp.exp(scores - top)
        total = jnp.sum(expo, axis=0, keepdims=True)
        probs = (expo * (1.0 / total)).astype(BF16)
        st.aux[:, head * rows : (head + 1) * rows] = probs
        ctxt[head * size : (head + 1) * size, :] = dot_nn(
            vt[head * size : (head + 1) * size, :], probs
        ).astype(BF16)
    ctx = ctxt[...].T
    st.wide[:, 3 * width :] = ctx
    branch = dot_nn(ctx, w[:, 3 * width :]) + vec.out_bias
    norm_forward(inputs, branch, seq_len, vec, st, send)


def feed_branch(inputs, w, down, vec, st):
    width = inputs.shape[1]
    st.x[...] = inputs
    step = 2 * width

    def before(c):
        bias = jnp.concatenate([vec.first_bias(2 * c, width), vec.first_bias(2 * c + 1, width)], axis=1)
        return dot_nn(inputs, w[:, c * step : (c + 1) * step]) + bias

    branch = None
    ahead = before(0)
    for c in range(w.shape[1] // step):
        cols = slice(c * step, (c + 1) * step)
        x = ahead
        if cols.stop < w.shape[1]:
            ahead = before(c + 1)
        square = x * x
        t = jnp.tanh(x * (GELU_IN + GELU_CUBE * square))
        s = 0.5 + 0.5 * t
        act = x * s
        slope = s + act * (1.0 - t) * (GELU_IN + (3.0 * GELU_CUBE) * square)
        hidden = act.astype(BF16)
        st.wide[:, cols] = hidden
        st.aux[:, cols] = slope.astype(BF16)
        part = dot_nt(hidden, down[:, cols])
        branch = part if branch is None else branch + part
    return branch + vec.out_bias


def feed_forward(inputs, w, down, vec, seq_len, st, send):
    branch = feed_branch(inputs, w, down, vec, st)
    norm_forward(inputs, branch, seq_len, vec, st, send)


def feed_grads(dresid, w, down, st, send):
    width = dresid.shape[1]
    dbranch = dresid.astype(BF16)
    st.db[...] = dbranch
    total = dresid
    step = 2 * width
    ahead = dot_nn(dbranch, down[:, :step])
    for c in range(w.shape[1] // step):
        cols = slice(c * step, (c + 1) * step)
        dhidden = ahead
        if cols.stop < w.shape[1]:
            ahead = dot_nn(dbranch, down[:, cols.stop : cols.stop + step])
        dpre = (dhidden * st.aux[:, cols].astype(F32)).astype(BF16)
        st.gwide[:, cols] = dpre
        total = total + dot_nt(dpre, w[:, cols])
    send[...] = total.astype(BF16)


def feed_backward(grad, w, down, vec, st, send):
    dresid = norm_backward(grad, vec, st)
    feed_grads(dresid, w, down, st, send)


def feed_both(inputs, grad, w, down, vec, seq_len, st, y_out, send):
    branch = feed_branch(inputs, w, down, vec, st)
    dresid = norm_forward(inputs, branch, seq_len, vec, st, y_out, grad)
    feed_grads(dresid, w, down, st, send)


def attend_backward(grad, w, vec, st, send, scratch):
    kt, dqt = scratch[:2]
    rows, width = grad.shape
    size = width // HEADS
    dresid = norm_backward(grad, vec, st)
    dbranch = dresid.astype(BF16)
    st.gwide[:, 3 * width :] = dbranch
    dctx = dot_nt(dbranch, w[:, 3 * width :]).astype(BF16)
    q, v = st.wide[:, :width], st.wide[:, 2 * width : 3 * width]
    kt[...] = (st.wide[:, width : 2 * width] * jnp.asarray(size**-0.5, BF16)).T
    lane = lax.broadcasted_iota(jnp.int32, (rows, 2 * size), 1)
    none = jnp.zeros((rows, 2 * size), BF16)

    def own(value, head):
        first = (head // 2) * 2 * size
        mine = (lane >= size) if head % 2 else (lane < size)
        return jnp.where(mine, value[:, first : first + 2 * size], none)

    def probs_grad(head):
        first = (head // 2) * 2 * size
        return dot_nt(own(v, head), dctx[:, first : first + 2 * size])

    ahead = probs_grad(0)
    for head in range(HEADS):
        dprobs = ahead
        if head + 1 < HEADS:
            ahead = probs_grad(head + 1)
        probs_low = st.aux[:, head * rows : (head + 1) * rows]
        probs = probs_low.astype(F32)
        inner = jnp.sum(probs * dprobs, axis=0, keepdims=True)
        dscores = (probs * (dprobs - inner)).astype(BF16)
        dv_part = dot_nn(probs_low, own(dctx, head))
        dk_part = dot_nn(dscores, own(q, head))
        dqt[head * size : (head + 1) * size, :] = dot_nn(
            kt[head * size : (head + 1) * size, :], dscores
        ).astype(BF16)
        if head % 2 == 0:
            dv, dk = dv_part, dk_part
        else:
            at = width + (head // 2) * 2 * size
            st.gwide[:, at : at + 2 * size] = (dk + dk_part).astype(BF16)
            st.gwide[:, width + at : width + at + 2 * size] = (dv + dv_part).astype(BF16)
    dx = dresid + dot_nt(st.gwide[:, width : 3 * width], w[:, width : 3 * width])
    st.gwide[:, :width] = dqt[...].T
    send[...] = (dx + dot_nt(st.gwide[:, :width], w[:, :width])).astype(BF16)


def roles_of(slot, segments):
    last = segments - 1
    found = []
    for z in range(segments):
        j = slot - 2 * z
        if 0 <= j < segments:
            found.append((z, "both" if z == last else "forward", j))
        j = slot - (4 * last - 2 * z)
        if z < last and 0 <= j < segments:
            found.append((z, "backward", j))
    return found


def half_rows(meta, own, width):
    bit = lax.rem(meta[1], 2)
    bit = bit if own else 1 - bit
    return pl.multiple_of(bit * (width // 2), width // 2)


def weight_refs(lengths, kept):
    acts, wide, _, _, _, grad_wide, grad_branch, sums = kept[:8]
    return [lengths, acts, wide, grad_wide, grad_branch, sums]


def load_turned(at, source, lanes):
    rows = source.shape[1]
    for j in range(source.shape[0]):
        at[: lanes.size, j * rows : (j + 1) * rows] = source[j, :, lanes].T


def main_products(meta, refs, at, own, feed, sentences):
    _, acts, wide, grad_wide = refs[:4]
    rows, width = acts.shape[1:]
    half, full = width // 2, wide.shape[2]
    total = (sentences.stop - sentences.start) * rows
    start = half_rows(meta, own, width)
    at[half:, :total] = jnp.ones((at.shape[0] - half, total), BF16)
    load_turned(at, acts.at[sentences], pl.ds(start, half))
    for c in range(full // width):
        cols = slice(c * width, (c + 1) * width)
        if c == 3 and not feed:
            lanes = pl.ds(pl.multiple_of(3 * width + start, half), half)
            load_turned(at, wide.at[sentences], lanes)
        yield c, cols, dot_nn(at[:, :total], grad_wide[sentences, :, cols].reshape(total, width))


def side_products(meta, refs, at, own, sentences):
    wide, _, grad_branch = refs[2:5]
    rows, width = grad_branch.shape[1:]
    half, full = width // 2, wide.shape[2]
    total = (sentences.stop - sentences.start) * rows
    load_turned(at, grad_branch.at[sentences], pl.ds(half_rows(meta, own, width), half))
    for c in range(full // width):
        cols = slice(c * width, (c + 1) * width)
        yield c, cols, dot_nn(at[:half, :total], wide[sentences, :, cols].reshape(total, width))


def early_sums(feed, stop):
    def body(meta, ins, outs, kept, scratch):
        lengths = ins[0]
        refs = weight_refs(lengths, kept)
        for own in range(2):
            for _, cols, grad in main_products(meta, refs, scratch[0], bool(own), feed, slice(0, stop)):
                outs[0][own, :, cols] = grad
            if feed:
                for _, cols, grad in side_products(meta, refs, scratch[0], bool(own), slice(0, stop)):
                    outs[1][own, :, cols] = grad

    return body


def main_half(own, feed, first=0, early=None):
    def body(meta, refs, out, scratch):
        lengths, acts, wide, _, grad_branch, sums = refs
        at, sm = scratch
        count, rows, width = acts.shape
        half, full = width // 2, wide.shape[2]
        sm[...] = jnp.zeros_like(sm)
        sm[:SMALLS, :] = sums[...]
        tokens = jnp.sum(lengths[:, 0:1].astype(F32), axis=0, keepdims=True)
        sm[COUNT : COUNT + 1, :] = jnp.broadcast_to(tokens, (1, width))
        for c, cols, grad in main_products(meta, refs, at, own, feed, slice(first, count)):
            if early is not None:
                grad = grad + early[int(own), :, cols]
            out[:, cols] = grad[:half].astype(BF16)
            place = BIAS + (3, 0, 1, 2)[c] if feed else (BIAS, None, BIAS + 1, OUT_BIAS)[c]
            if place is not None:
                sm[place : place + 1, :] = grad[half : half + 1]
        if feed:
            sm[OUT_BIAS : OUT_BIAS + 1, :] = jnp.sum(
                grad_branch[...].reshape(count * rows, width).astype(F32), axis=0, keepdims=True
            )
        out[:, full:] = sm[:, pl.ds(half_rows(meta, own, width), half)].T.astype(BF16)

    return body


def side_half(own, first, early):
    def body(meta, refs, out, scratch):
        wide, grad_wide, grad_branch = refs[2:5]
        at, sm = scratch
        count, rows, width = grad_branch.shape
        half, full, total = width // 2, wide.shape[2], count * rows
        sm[...] = jnp.broadcast_to(
            jnp.sum(
                grad_wide[:, :, :width].reshape(total, width).astype(F32), axis=0, keepdims=True
            ),
            sm.shape,
        )
        mine = pl.ds(half_rows(meta, own, width), half)
        out[:, full // 2 : full // 2 + LANES] = sm[:, mine].T.astype(BF16)
        for c, cols, grad in side_products(meta, refs, at, own, slice(first, count)):
            put = c * width + (LANES if c * width >= full // 2 else 0)
            out[:, put : put + width] = (grad + early[int(own), :, cols]).astype(BF16)

    return body


def core_add(masks):
    def body(meta, ins, outs, kept, scratch):
        size = outs[0].shape[0]
        chip = lax.div(meta[1], 2)
        for mask, out in zip(masks, outs, strict=True):
            rows = pl.ds(pl.multiple_of(jnp.bitwise_xor(chip, mask // 2) * size, size), size)
            at = 0
            for keep, got in zip(ins[0::2], ins[1::2], strict=True):
                cols = slice(at, at + keep.shape[1])
                at += keep.shape[1]
                out[:, cols] = (keep[rows, :].astype(F32) + got[rows, :].astype(F32)).astype(BF16)

    return body


def summed(refs, cols):
    total = refs[0][:, cols].astype(F32)
    for r in refs[1:]:
        total = total + r[:, cols].astype(F32)
    return total.astype(BF16)


def chip_sum(meta, ins, outs, kept, scratch):
    at = 0
    for out in outs or kept:
        out[...] = summed(ins, slice(at, at + out.shape[1]))
        at += out.shape[1]


def added(one, two, rows):
    return (one[rows, :].astype(F32) + two[rows, :].astype(F32)).astype(BF16)


def first_cut(meta, ins, outs, kept, scratch):
    keep, got = ins
    upper_stay, upper_go, lower_stay, lower_go = outs
    size = upper_stay.shape[0]
    half = size // 2
    chip = lax.div(meta[1], 2)
    x, y = lax.rem(chip, 2), lax.div(chip, 2)
    for other in range(2):
        put = slice(other * half, (other + 1) * half)
        for out, q, low in (
            (upper_go, 2 * other + 1 - x, 0),
            (lower_go, 2 * (1 - y) + other, half),
            (upper_stay, 2 * other + x, 0),
            (lower_stay, 2 * y + other, half),
        ):
            out[put, :] = added(keep, got, pl.ds(pl.multiple_of(q * size + low, half), half))


def second_cut(meta, ins, outs, kept, scratch):
    upper, upper_got, lower, lower_got = ins
    half = outs[0].shape[0]
    chip = lax.div(meta[1], 2)
    x, y = lax.rem(chip, 2), lax.div(chip, 2)
    for one, two, bit, stay, go in (
        (upper, upper_got, y, outs[0], outs[1]),
        (lower, lower_got, x, outs[2], outs[3]),
    ):
        go[...] = added(one, two, pl.ds(pl.multiple_of((1 - bit) * half, half), half))
        stay[...] = added(one, two, pl.ds(pl.multiple_of(bit * half, half), half))


def cut_sum(meta, ins, outs, kept, scratch):
    half = ins[0].shape[0]
    for i in range(2):
        at = 0
        for out in outs:
            cols = slice(at, at + out.shape[1])
            out[i * half : (i + 1) * half, :] = summed(ins[2 * i : 2 * i + 2], cols)
            at += out.shape[1]


def cross_message(meta, ins, outs, kept, scratch):
    low, grad = ins
    (out,) = outs
    size, width = low.shape[0], out.shape[1]

    @pl.when(lax.rem(meta[0], 2) == 1)
    def _():
        for i in range(0, low.shape[1], width):
            cols = min(width, low.shape[1] - i)
            out[i // width * size : (i // width + 1) * size, :cols] = low[:, i : i + cols]

    @pl.when(meta[0] == 0)
    def _():
        out[...] = grad[...]


def side_share(meta, ins, outs, kept, scratch):
    high, message = ins
    (out,) = outs
    half = high.shape[1]

    @pl.when(lax.rem(meta[0], 2) == 1)
    def _():
        out[:, :half] = high[...]
        out[:, half:] = jnp.zeros((out.shape[0], out.shape[1] - half), BF16)

    @pl.when(lax.rem(meta[0], 2) == 0)
    def _():
        size, width = out.shape[0], message.shape[1]
        for i in range(0, out.shape[1], width):
            cols = min(width, out.shape[1] - i)
            out[:, i : i + cols] = message[i // width * size : (i // width + 1) * size, :cols]


def block_row(meta, mask, width, size):
    chip, core = lax.div(meta[1], 2), lax.rem(meta[1], 2)
    side = jnp.bitwise_xor(core, mask % 2)
    at = side * (width // 2) + jnp.bitwise_xor(chip, mask // 2) * size
    return pl.multiple_of(at, size)


def load_lent(side, in_bias, share, sems, first, meta):
    width, block = side.shape[0], share.shape[0] - 16
    rows = pl.ds(half_rows(meta, True, width), block)
    copy = pltpu.make_async_copy(side.at[rows], share.at[:block], sems.at[first])
    copy.start()
    share[block:, width:] = jnp.zeros((16, share.shape[1] - width), BF16)
    share[block:, :width] = jnp.broadcast_to(in_bias[:, 2 * width :], (16, width))
    return copy


def begin_sending(meta, ins, outs, kept, scratch):
    side, in_bias, tokens = ins
    share, bias_v, tokens_v = outs
    sems = scratch[-1]
    copies = [
        pltpu.make_async_copy(in_bias, bias_v, sems.at[0]),
        pltpu.make_async_copy(tokens, tokens_v, sems.at[1]),
    ]
    for c in copies:
        c.start()
    copies[0].wait()
    load_lent(side, bias_v, share, sems, 2, meta).wait()
    copies[1].wait()


def begin(meta, ins, outs, kept, scratch):
    lens, side, bias_v, *rest = ins
    again, zero_sums, lens_v, *outs = outs
    sems = scratch[-1]
    copies = [
        pltpu.make_async_copy(src, dst, sems.at[i])
        for i, (src, dst) in enumerate(zip(rest, outs[: len(rest)], strict=True))
    ]
    for c in copies:
        c.start()
    copies.append(load_lent(side, bias_v, again, sems, len(rest), meta))
    zero_sums[...] = jnp.zeros_like(zero_sums)
    for j in range(lens_v.shape[0]):
        lens_v[j : j + 1, :] = jnp.full((1, LANES), lens[j], jnp.int32)
    for c in copies:
        c.wait()


def join_down(meta, ins, outs, kept, scratch):
    lent, other, side = ins
    down, low_bias = kept
    width, half = side.shape
    block = width // 2
    copy = pltpu.make_async_copy(side, down.at[:, half:], scratch[-1].at[0])
    copy.start()
    down[pl.ds(half_rows(meta, True, width), block), :half] = lent[:block]
    down[pl.ds(half_rows(meta, False, width), block), :half] = other[:block]
    low_bias[...] = lent[block:, :width]
    copy.wait()


class Results:
    def __init__(self, sems):
        self.sems, self.copies = sems, []

    def out(self, src, dst):
        self.picked([src], dst, None)

    def picked(self, refs, dst, which):
        sem = self.sems.at[len(self.copies)]
        for j, r in enumerate(refs):
            start = pltpu.make_async_copy(r, dst, sem).start
            start() if which is None else pl.when(which == j)(start)
        self.copies.append(pltpu.make_async_copy(refs[0], dst, sem))

    def finish(self):
        for c in self.copies:
            c.wait()


def widen_main(masks, segments):
    def body(meta, ins, outs, kept, scratch):
        n = len(masks)
        blocks, finals, backs = ins[:n], ins[n : n + segments], ins[n + segments :]
        out_y, out_g, main_h, out_b, gain_h, shift_h, stats_h, small_v = outs
        full, cols, stat, sems = scratch
        res = Results(sems)
        res.picked(finals, out_y, meta[0])
        res.picked(backs, out_g, meta[0])
        width, main = main_h.shape[1], main_h.shape[2]
        size = blocks[0].shape[0]
        for i, mask in enumerate(masks):
            at = block_row(meta, mask, width, size)
            cols[pl.ds(at, size), :] = blocks[i][:, main:]
            full[i] = blocks[i][:, :main].astype(F32)
            res.out(full.at[i], main_h.at[0, pl.ds(at, size)])
        small = cols[...].T.astype(F32)
        small_v[...] = small[: small_v.shape[0]]
        squares = jnp.sum(small[RESID_SQ : BRANCH_SQ + 1], axis=1, keepdims=True)
        values = jnp.sqrt(squares / (small[COUNT : COUNT + 1, 0:1] * width))
        lane = lax.broadcasted_iota(jnp.int32, (1, LANES), 1)
        stat[...] = jnp.where(lane == 0, values[0:1], values[1:2])
        res.out(small_v.at[OUT_BIAS : OUT_BIAS + 1], out_b)
        res.out(small_v.at[GAIN : GAIN + 1], gain_h)
        res.out(small_v.at[SHIFT : SHIFT + 1], shift_h)
        res.out(stat, stats_h)
        res.finish()

    return body


def widen_side(masks):
    def body(meta, ins, outs, kept, scratch):
        *blocks, small = ins
        side_h, in_b = outs
        full, cols, vecs, sems = scratch
        res = Results(sems)
        width, half = side_h.shape[1], side_h.shape[2]
        size = blocks[0].shape[0]
        for i, mask in enumerate(masks):
            at = block_row(meta, mask, width, size)
            cols[pl.ds(at, size), :] = blocks[i][:, half:]
            full[i] = blocks[i][:, :half].astype(F32)
            res.out(full.at[i], side_h.at[0, pl.ds(at, size)])
        lent = cols[...].T.astype(F32)[0:1]
        feed = jnp.full((1, width), lax.rem(meta[0], 2), jnp.int32) == 1
        vecs[0:1, :width] = small[BIAS : BIAS + 1]
        vecs[0:1, width : 2 * width] = small[BIAS + 1 : BIAS + 2]
        vecs[0:1, 2 * width :] = jnp.where(feed, small[BIAS + 2 : BIAS + 3], lent)
        res.out(vecs.at[0:1], in_b)
        res.finish()

    return body


def on_device(
    tokens, lengths, cotangent, main_weight, side_weight, in_bias, out_bias, norm_gain, norm_shift
):
    segments, shards = lax.axis_size("segment"), lax.axis_size("dp")
    z, d = lax.axis_index("segment"), lax.axis_index("dp")
    rows, width = tokens.shape
    main_mat, side_mat = main_weight[0], side_weight[0]
    hidden = main_mat.shape[1]
    half_width = side_mat.shape[1]
    block = width // shards
    last = segments - 1
    feeds = tuple(range(1, segments, 2))
    chip_masks = tuple(range(0, shards, 2))
    masks = chip_masks + tuple(m + 1 for m in chip_masks)
    meta = (z.reshape(1), d.reshape(1))

    def hop(value, *pairs):
        return lax.ppermute(value, "segment", list(pairs))

    def swap(value, mask):
        return lax.ppermute(value, "dp", [(i, i ^ mask) for i in range(shards)])

    ext = hidden + LANES
    low_ext = half_width + LANES
    kept_shapes = [
        ((segments, rows, width), BF16),
        ((segments, rows, hidden), BF16),
        ((segments, rows, hidden), BF16),
        ((segments, rows, width), F32),
        ((segments, rows, LANES), F32),
        ((segments, rows, hidden), BF16),
        ((segments, rows, width), BF16),
        ((2, rows, width), BF16),
    ]
    lent = ((width // 2 + 16, half_width), BF16)
    borrowed_shapes = [((width, hidden), BF16), ((16, width), BF16)]
    narrow = ((rows, width), BF16)
    (share, bias_v, tokens_v), _ = kernel_call(
        begin_sending, meta, [side_mat, in_bias, tokens], [lent, (in_bias.shape, BF16), narrow],
        copies=3, hbm_ins=(0, 1, 2),
    )
    loads = [out_bias, norm_gain, norm_shift, main_mat, cotangent, cotangent]
    loaded, _ = kernel_call(
        begin, meta, [lengths.reshape(segments), side_mat, bias_v, *loads],
        [lent, ((SMALLS, width), F32), ((segments, LANES), jnp.int32)]
        + [(x.shape, x.dtype) for x in loads]
        + kept_shapes + borrowed_shapes,
        copies=1 + len(loads), smem_ins=(0,), hbm_ins=(1, *range(3, 3 + len(loads))), flops=SLOT_FLOPS,
    )
    later_share, sums, lengths_v, *loaded = loaded
    out_bias_v, gain_v, shift_v, main_v, cotangent_v, later_cotangent, *kept = loaded
    *kept, saved, down, low_bias = kept
    kept, borrowed = (*kept, sums, saved), (down, low_bias)

    turns = tuple(range(last, -1, -1))
    first_share = hop(share, (0, 1))
    first_in = [hop(tokens_v, (home, 0)) for home in turns[:2]]
    riders = {
        0: [(turns[2], 0, "tokens"), (turns[1], last, "cotangent")],
        1: [(turns[2], last, "cotangent")],
    }

    def join(s, share, other, blank):
        return kernel_call(
            join_down, meta, [share, other, side_mat], [], kept=blank, hbm_ins=(2,), copies=1, where=(s,)
        )[1]

    turned = ((width, rows), BF16)
    n_chip = len(chip_masks)
    weight_scratch = [((width // 2 + 16, segments * rows), BF16), ((LANES, width), F32)]

    slots = 4 * last + segments
    waves, sent, finals = {}, {}, []
    after, last_in = {}, []
    side, main = [], []
    half_out = ((width // 2, ext), BF16)

    def hops_after(slot):
        pairs = []
        for z_role, what, j in roles_of(slot, segments):
            if what == "forward":
                pairs.append((z_role, z_role + 1))
            elif z_role > 0:
                pairs.append((z_role, z_role - 1))
            elif turns[j] > 0:
                pairs.append((z_role, turns[j]))
        return pairs + [(source, to) for source, to, _ in riders.get(slot, ())]

    homeward = {}
    for slot in range(2 * last + segments + 2, slots):
        taken = [to for _, to in hops_after(slot)]
        free = [home for home in range(1, last) if home not in taken and home not in homeward.values()]
        if free:
            homeward[slot] = free[-1]
    for slot in range(slots):
        roles = roles_of(slot, segments)
        uses = [r[1] for r in roles]
        attends = any(r[0] % 2 == 0 for r in roles)
        feed_roles = any(r[0] % 2 == 1 for r in roles)
        names, ins = [], []

        def give(name, value):
            names.append(name)
            ins.append(value)

        for name, value in zip(
            ("main", "in_bias", "out_bias", "gain", "shift", "lengths"),
            (main_v, bias_v, out_bias_v, gain_v, shift_v, lengths_v),
        ):
            give(name, value)
        if feed_roles and slot != last + 2:
            give("down", down)
            give("low_bias", low_bias)
        if slot < 2:
            give("first", first_in[slot])
            give("cotangent", cotangent_v)
        if slot in (0, last):
            give("tokens", tokens_v)
        if slot - 2 in waves:
            give("wave", waves[slot - 2])
        if "both" in uses and slot - 2 * last in (0, last):
            give("last", last_in[slot - 2 * last])
        if slot in homeward:
            give("home", finals[turns.index(homeward[slot])])
        outs = [narrow] + ([narrow] if "both" in uses else [])
        weighing = slots - 2 <= slot
        if weighing:
            give("early_side", early_side)
            give("early_main", early_main)
            outs += [half_out] * (4 if slot == slots - 2 else 0)

        def body(
            meta, in_refs, out_refs, kept_refs, scratch, slot=slot, roles=roles, names=tuple(names)
        ):
            ref = dict(zip(names, in_refs))
            if slot == last + 2:
                ref["down"], ref["low_bias"] = kept_refs[-2:]
            vec = Vectors(
                ref["in_bias"], ref["out_bias"], ref["gain"], ref["shift"], ref.get("low_bias")
            )
            for z_role, what, j in roles:

                @pl.when(meta[0] == z_role)
                def _(z_role=z_role, what=what, j=j):
                    st = Store(kept_refs, j)
                    seq_len = ref["lengths"][turns[j] : turns[j] + 1, 0:1]
                    w, send = ref["main"], out_refs[0]
                    if what == "backward":
                        if z_role % 2:
                            feed_backward(ref["wave"][...], w, ref["down"], vec, st, send)
                        else:
                            attend_backward(ref["wave"][...], w, vec, st, send, scratch)
                        return
                    own = slot == last and z_role == 0
                    inputs = ref["tokens" if own else "first" if "first" in ref else "wave"][...]
                    if what == "both":
                        feed_both(
                            inputs, ref["last"][...] if "last" in ref else kept_refs[8][j - 1], w, ref["down"], vec, seq_len, st, out_refs[1], send
                        )
                    elif z_role % 2:
                        feed_forward(inputs, w, ref["down"], vec, seq_len, st, send)
                    else:
                        attend_forward(inputs, w, vec, seq_len, st, send, scratch)

            for source, _, what in riders.get(slot, ()):

                @pl.when(meta[0] == source)
                def _(what=what):
                    out_refs[0][...] = ref[what][...]

            if slot in (2, 3):

                @pl.when(meta[0] == last)
                def _():
                    kept_refs[8][slot - 2] = ref["wave"][...]

            if "home" in ref:

                @pl.when(meta[0] == last)
                def _():
                    out_refs[0][...] = ref["home"][...]

            if weighing:
                sums = weight_refs(ref["lengths"], kept_refs)
                first = slot == slots - 2
                sides, mains = (out_refs[-4:-2], out_refs[-2:]) if first else ((), kept_refs[-2:])
                feed_here = lax.rem(meta[0], 2) == 1

                @pl.when(feed_here)
                def _():
                    for own in range(2):
                        if first:
                            side_half(bool(own), FEED_EARLY, ref["early_side"])(
                                meta, sums, sides[own], scratch[-2:]
                            )
                        else:
                            main_half(bool(own), True, FEED_EARLY, ref["early_main"])(
                                meta, sums, mains[own], scratch[-2:]
                            )

                if first:

                    @pl.when(jnp.logical_not(feed_here) & (meta[0] > 0))
                    def _():
                        for own in range(2):
                            main_half(bool(own), False)(meta, sums, mains[own], scratch[-2:])

        scratch = [turned, turned, narrow] if attends else []
        if weighing:
            scratch = scratch + weight_scratch
        extra = ()
        if slot in (1, last + 1):
            extra = (later_share,)
        elif slot == last + 2:
            extra = (down, low_bias)
        elif slot == slots - 1:
            extra = (*main,)
        res, kept = kernel_call(
            body, meta, ins, outs, scratch, (*kept, *extra), after=after.get(slot, ()), flops=SLOT_FLOPS
        )
        if slot == 2:
            last_in += [cotangent_v, None, None]
        if slot == 2 * last:
            _, (*kept, later_cotangent) = kernel_call(
                lambda *_: None, meta, [], [], kept=(*kept, later_cotangent), after=[waves[slot - 1]]
            )
            last_in.append(hop(later_cotangent, (0, last)))
        if slot == slots - 1:
            *kept, main[0], main[1] = kept
        if slot == 0:
            _, (*kept, first_share) = kernel_call(lambda *_: None, meta, [], [], kept=(*kept, first_share))
            down, low_bias = join(1, first_share, swap(first_share, 1), borrowed)
        if slot == 1:
            *kept, later_share = kept
            later_share = hop(later_share, (last - 1, last))
        if slot == last + 1:
            *kept, later_share = kept
            later_half = swap(later_share, 1)
        if slot == last + 2:
            *kept, down, low_bias = kept
            down, low_bias = join(last, later_share, later_half, (down, low_bias))
        sent[slot] = res[0]
        if slot == slots - segments - 1:
            early_shapes = [((2, width // 2 + extra_rows, hidden), F32) for extra_rows in (16, 0)]
            (early_main, early_side), kept = kernel_call(
                early_sums(True, FEED_EARLY), meta, [lengths_v], early_shapes, weight_scratch, kept, where=feeds
            )
        if slot == slots - 2:
            side, main = list(res[-4:-2]), list(res[-2:])

            def early_attend(meta, ins, outs, kept, scratch):
                early_sums(False, ATTEND_EARLY)(meta, ins, kept[-1:], kept, scratch)

            _, (*kept, early_main) = kernel_call(
                early_attend, meta, [lengths_v], [], weight_scratch, (*kept, early_main), where=(0,)
            )
        if "both" in uses:
            finals.append(res[1])
        pairs = hops_after(slot)
        if slot in homeward:
            pairs.append((last, homeward[slot]))
        if pairs and slot != slots - 2:
            waves[slot] = hop(res[0], *pairs)
    def weigh(own, after):
        def body(meta, ins, outs, kept, scratch):
            main_half(bool(own), False, ATTEND_EARLY, ins[-1])(meta, ins[:-1], kept[0], scratch)

        _, (main[own],) = kernel_call(
            body, meta, [*weight_refs(lengths_v, kept), early_main], [], weight_scratch,
            (main[own],), where=(0,), after=after,
        )

    def add_cores(keep, got, segs, after=()):
        blocks, _ = kernel_call(
            core_add(chip_masks), meta, [keep, got], [((block, keep.shape[1]), BF16)] * n_chip,
            where=segs, after=after,
        )
        return [blocks[0]] + [swap(blocks[i], chip_masks[i]) for i in range(n_chip - 1, 0, -1)]

    def add_in_steps(keep, got, segs, after=()):
        rows_of = (keep.shape[0] // 4, keep.shape[1])
        (up, up_go, down, down_go), _ = kernel_call(
            first_cut, meta, [keep, got], [(rows_of, BF16)] * 4, where=segs, after=after
        )
        rows_of = (rows_of[0] // 2, rows_of[1])
        (up, up_go, down, down_go), _ = kernel_call(
            second_cut, meta, [up, swap(up_go, 2), down, swap(down_go, 4)],
            [(rows_of, BF16)] * 4, where=segs,
        )
        return [up, swap(up_go, 4), down, swap(down_go, 2)]

    reduce, last_sum = (add_in_steps, cut_sum) if n_chip == 4 else (add_cores, chip_sum)
    side_got = swap(side[0], 1)
    weigh(0, [side_got])
    main_got = swap(main[0], 1)
    side_blocks = reduce(side[1], side_got, feeds, [main[0]])
    weigh(1, [side_blocks[0]] if n_chip != 4 else [])
    main_blocks = reduce(main[1], main_got, None)
    (low_own, high_own), _ = kernel_call(
        last_sum, meta, side_blocks, [((block, low_ext), BF16), ((block, half_width), BF16)], where=feeds,
        after=main_blocks[:1],
    )
    (total,), _ = kernel_call(last_sum, meta, main_blocks, [((block, ext), BF16)])
    (message,), _ = kernel_call(cross_message, meta, [low_own, sent[slots - 2]], [narrow])
    waves[slots - 2] = hop(message, *[(s, s - 1) for s in feeds], (0, turns[-2]))
    first_home = hop(finals[turns.index(0)], (last, 0))
    outputs_at = [first_home] + [
        waves[next(k for k, v in homeward.items() if v == s)] for s in range(1, last)
    ]
    outputs_at.append(finals[turns.index(last)])
    start = slots - segments
    grads_at = [sent[slots - 1]] + [waves[start + turns.index(s)] for s in range(1, segments)]

    def gather(share):
        blocks = [share] + [swap(share, m) for m in reversed(chip_masks[1:])]
        blocks = [blocks[0], *reversed(blocks[1:])]
        return blocks + [swap(b, 1) for b in blocks]

    main_all = gather(total)
    (side_mine,), _ = kernel_call(
        side_share, meta, [high_own, waves[slots - 2]], [((block, low_ext), BF16)],
        after=[main_all[2]],
    )
    (out_y, out_g, main_grad, out_bias_grad, gain_grad, shift_grad, stats, small), _ = kernel_call(
        widen_main(masks, segments), meta, [*main_all, *outputs_at, *grads_at],
        [narrow, narrow, ((1, width, hidden), F32)]
        + [((1, width), F32)] * 3
        + [((1, LANES), F32), ((SMALLS, width), F32)],
        [((shards, block, hidden), F32), ((width, LANES), BF16), ((1, LANES), F32)],
        copies=shards + 6, hbm_outs=tuple(range(7)),
    )
    (side_grad, in_bias_grad), _ = kernel_call(
        widen_side(masks), meta, [*gather(side_mine), small],
        [((1, width, half_width), F32), ((1, 3 * width), F32)],
        [((shards, block, half_width), F32), ((width, LANES), BF16), ((8, 3 * width), F32)],
        copies=shards + 1, hbm_outs=(0, 1),
    )
    return (
        out_y, out_g, main_grad, side_grad, in_bias_grad, out_bias_grad, gain_grad, shift_grad, stats[:, :2]
    )


def solution(mesh):
    over = P(("segment", "dp"), None)
    by_segment = [P("segment", None, None)] * 2 + [P("segment", None)] * 4
    in_specs = (over, P(None, "dp"), over, *by_segment)
    out_specs = (over, over, *by_segment, P("segment", None))
    return jax.shard_map(
        on_device, mesh=mesh, in_specs=in_specs, out_specs=out_specs, check_vma=False
    )
```

```python
import functools

import jax
import jax.numpy as jnp
from jax import lax
from jax.experimental import pallas as pl
from jax.experimental.pallas import tpu as pltpu
from jax.sharding import PartitionSpec as P

HEADS = 8
EPS = 1e-05
LANES = 128
VMEM_LIMIT = 12 * 1024 * 1024
SLOT_FLOPS = 16 * 10**9
FEED_EARLY, ATTEND_EARLY = 2, 3
F32 = jnp.float32
BF16 = jnp.bfloat16
GELU_IN = 0.7978845608028654
GELU_CUBE = 0.044715 * GELU_IN

BIAS, OUT_BIAS, GAIN, SHIFT, RESID_SQ, BRANCH_SQ, COUNT, SMALLS = 0, 4, 5, 6, 7, 8, 9, 16


def dot_nn(left, right):
    return jnp.dot(left, right, preferred_element_type=F32)


def dot_nt(left, right):
    return lax.dot_general(left, right, (((1,), (1,)), ((), ())), preferred_element_type=F32)


def kernel_call(
    body, meta, ins, outs, scratch=(), kept=(), copies=0, hbm_ins=(), smem_ins=(), hbm_outs=(), where=None,
    after=(), flops=1,
):
    ins = [*ins, *after]
    n_in, n_kept, n_out = len(ins), len(kept), len(outs)

    def kernel(z_ref, d_ref, *refs):
        at = 0
        groups = []
        for n in (n_in, n_kept, n_out, n_kept):
            groups.append(refs[at : at + n])
            at += n

        def run():
            body((z_ref[0], d_ref[0]), groups[0][: n_in - len(after)], groups[2], groups[3], refs[at:])

        if where is None:
            run()
        else:
            here = z_ref[0] == where[0]
            for other in where[1:]:
                here = here | (z_ref[0] == other)
            pl.when(here)(run)

    smem = pl.BlockSpec(memory_space=pltpu.SMEM)
    vmem = pl.BlockSpec(memory_space=pltpu.VMEM)
    hbm = pl.BlockSpec(memory_space=pltpu.HBM)

    def held(x, space=pltpu.VMEM):
        return pltpu.with_memory_space_constraint(x, space)

    results = pl.pallas_call(
        kernel,
        out_shape=[
            jax.ShapeDtypeStruct(*o) if i in hbm_outs else pltpu.VMEM(*o) for i, o in enumerate(outs)
        ]
        + [pltpu.VMEM(k.shape, k.dtype) for k in kept],
        in_specs=[smem] * 2
        + [smem if i in smem_ins else hbm if i in hbm_ins else vmem for i in range(n_in)]
        + [vmem] * n_kept,
        out_specs=[hbm if i in hbm_outs else vmem for i in range(n_out)] + [vmem] * n_kept,
        scratch_shapes=[pltpu.VMEM(*s) for s in scratch]
        + ([pltpu.SemaphoreType.DMA((copies,))] if copies else []),
        input_output_aliases={2 + n_in + i: n_out + i for i in range(n_kept)},
        compiler_params=pltpu.CompilerParams(vmem_limit_bytes=VMEM_LIMIT),
        cost_estimate=pl.CostEstimate(flops=flops, bytes_accessed=1, transcendentals=1),
    )(
        *meta,
        *[
            x if i in smem_ins else held(x, pltpu.HBM if i in hbm_ins else pltpu.VMEM)
            for i, x in enumerate(ins)
        ],
        *[held(k) for k in kept],
    )
    return tuple(results[:n_out]), tuple(results[n_out:])


NORM_ROWS = 32
NORM_BACK_ROWS = 128


def norm_forward(inputs, branch, seq_len, vec, st, out, back=None):
    gain, shift = vec.gain, vec.shift
    sums = [0.0] * 4
    grads = []
    block = NORM_ROWS if back is None else NORM_BACK_ROWS
    for first in range(0, inputs.shape[0], block):
        rows = slice(first, first + block)
        part = branch[rows]
        resid = inputs[rows].astype(F32) + part
        mean = jnp.mean(resid, axis=-1, keepdims=True)
        centred = resid - mean
        var = jnp.mean(centred * centred, axis=-1, keepdims=True)
        inv_std = lax.rsqrt(var + EPS)
        xhat = centred * inv_std
        out[rows, :] = (xhat * gain + shift).astype(BF16)
        live = first + lax.broadcasted_iota(jnp.int32, resid.shape, 0) < seq_len
        sums[0] += jnp.sum(jnp.where(live, resid * resid, 0.0), axis=0, keepdims=True)
        sums[1] += jnp.sum(jnp.where(live, part * part, 0.0), axis=0, keepdims=True)
        if back is None:
            st.xhat[rows, :] = xhat
            st.inv_std[rows, :] = jnp.broadcast_to(inv_std, (block, st.inv_std.shape[1]))
        else:
            grads.append(norm_back_rows(back[rows].astype(F32), xhat, inv_std, gain, sums))
    st.add(RESID_SQ, sums[0])
    st.add(BRANCH_SQ, sums[1])
    if back is not None:
        st.add(GAIN, sums[2])
        st.add(SHIFT, sums[3])
        return jnp.concatenate(grads, axis=0)


def norm_back_rows(grad, xhat, inv_std, gain, sums):
    gy = grad * gain
    along = grad * xhat
    first = jnp.mean(gy, axis=-1, keepdims=True)
    second = jnp.mean(along * gain, axis=-1, keepdims=True)
    sums[2] += jnp.sum(along, axis=0, keepdims=True)
    sums[3] += jnp.sum(grad, axis=0, keepdims=True)
    return (gy - first - xhat * second) * inv_std


def norm_backward(grad, vec, st):
    gain = vec.gain
    sums = [0.0] * 4
    grads = []
    for first in range(0, grad.shape[0], NORM_BACK_ROWS):
        rows = slice(first, first + NORM_BACK_ROWS)
        grads.append(
            norm_back_rows(grad[rows].astype(F32), st.xhat[rows, :], st.inv_std[rows, 0:1], gain, sums)
        )
    st.add(GAIN, sums[2])
    st.add(SHIFT, sums[3])
    return jnp.concatenate(grads, axis=0)


class Vectors:
    def __init__(self, in_bias, out_bias, gain, shift, low_bias=None):
        self.refs = (in_bias, out_bias, gain, shift, low_bias)

    def in_bias(self, i, width):
        return self.refs[0][0:1, i * width : (i + 1) * width].astype(F32)

    def first_bias(self, i, width):
        return self.refs[4][0:1, :width].astype(F32) if i == 0 else self.in_bias(i - 1, width)

    out_bias = property(lambda self: self.refs[1][...].astype(F32))
    gain = property(lambda self: self.refs[2][...].astype(F32))
    shift = property(lambda self: self.refs[3][...].astype(F32))


class Store:
    def __init__(self, kept, j):
        acts, wide, aux, xhat, inv_std, grad_wide, grad_branch, sums = kept[:8]
        self.x, self.wide, self.aux, self.xhat, self.inv_std, self.gwide, self.db = (
            a.at[j] for a in (acts, wide, aux, xhat, inv_std, grad_wide, grad_branch)
        )
        self.sums, self.first = sums, j == 0

    def add(self, row, value):
        if self.first:
            self.sums[row : row + 1, :] = value
        else:
            self.sums[row : row + 1, :] = self.sums[row : row + 1, :] + value


def attend_forward(inputs, w, vec, seq_len, st, send, scratch):
    vt, ctxt = scratch[:2]
    rows, width = inputs.shape
    size = width // HEADS
    st.x[...] = inputs
    q = (dot_nn(inputs, w[:, :width]) + vec.in_bias(0, width)).astype(BF16) * jnp.asarray(size**-0.5, BF16)
    st.wide[:, :width] = q
    k = dot_nn(inputs, w[:, width : 2 * width]).astype(BF16)
    st.wide[:, width : 2 * width] = k
    v = (dot_nn(inputs, w[:, 2 * width : 3 * width]) + vec.in_bias(1, width)).astype(BF16)
    st.wide[:, 2 * width : 3 * width] = v
    vt[...] = v.T
    key_live = lax.broadcasted_iota(jnp.int32, (rows, rows), 0) < seq_len
    lane = lax.broadcasted_iota(jnp.int32, (rows, 2 * size), 1)
    def score(head):
        first = (head // 2) * 2 * size
        qp = q[:, first : first + 2 * size]
        kp = k[:, first : first + 2 * size]
        mine = (lane >= size) if head % 2 else (lane < size)
        return dot_nt(jnp.where(mine, kp, jnp.zeros_like(kp)), qp)

    ahead = score(0)
    for head in range(HEADS):
        scores = jnp.where(key_live, ahead, -1e30)
        if head + 1 < HEADS:
            ahead = score(head + 1)
        top = jnp.max(scores, axis=0, keepdims=True)
        expo = jnp.exp(scores - top)
        total = jnp.sum(expo, axis=0, keepdims=True)
        probs = (expo * (1.0 / total)).astype(BF16)
        st.aux[:, head * rows : (head + 1) * rows] = probs
        ctxt[head * size : (head + 1) * size, :] = dot_nn(
            vt[head * size : (head + 1) * size, :], probs
        ).astype(BF16)
    ctx = ctxt[...].T
    st.wide[:, 3 * width :] = ctx
    branch = dot_nn(ctx, w[:, 3 * width :]) + vec.out_bias
    norm_forward(inputs, branch, seq_len, vec, st, send)


def feed_branch(inputs, w, down, vec, st):
    width = inputs.shape[1]
    st.x[...] = inputs
    step = 2 * width

    def before(c):
        bias = jnp.concatenate([vec.first_bias(2 * c, width), vec.first_bias(2 * c + 1, width)], axis=1)
        return dot_nn(inputs, w[:, c * step : (c + 1) * step]) + bias

    branch = None
    ahead = before(0)
    for c in range(w.shape[1] // step):
        cols = slice(c * step, (c + 1) * step)
        x = ahead
        if cols.stop < w.shape[1]:
            ahead = before(c + 1)
        square = x * x
        t = jnp.tanh(x * (GELU_IN + GELU_CUBE * square))
        s = 0.5 + 0.5 * t
        act = x * s
        slope = s + act * (1.0 - t) * (GELU_IN + (3.0 * GELU_CUBE) * square)
        hidden = act.astype(BF16)
        st.wide[:, cols] = hidden
        st.aux[:, cols] = slope.astype(BF16)
        part = dot_nt(hidden, down[:, cols])
        branch = part if branch is None else branch + part
    return branch + vec.out_bias


def feed_forward(inputs, w, down, vec, seq_len, st, send):
    branch = feed_branch(inputs, w, down, vec, st)
    norm_forward(inputs, branch, seq_len, vec, st, send)


def feed_grads(dresid, w, down, st, send):
    width = dresid.shape[1]
    dbranch = dresid.astype(BF16)
    st.db[...] = dbranch
    total = dresid
    step = 2 * width
    ahead = dot_nn(dbranch, down[:, :step])
    for c in range(w.shape[1] // step):
        cols = slice(c * step, (c + 1) * step)
        dhidden = ahead
        if cols.stop < w.shape[1]:
            ahead = dot_nn(dbranch, down[:, cols.stop : cols.stop + step])
        dpre = (dhidden * st.aux[:, cols].astype(F32)).astype(BF16)
        st.gwide[:, cols] = dpre
        total = total + dot_nt(dpre, w[:, cols])
    send[...] = total.astype(BF16)


def feed_backward(grad, w, down, vec, st, send):
    dresid = norm_backward(grad, vec, st)
    feed_grads(dresid, w, down, st, send)


def feed_both(inputs, grad, w, down, vec, seq_len, st, y_out, send):
    branch = feed_branch(inputs, w, down, vec, st)
    dresid = norm_forward(inputs, branch, seq_len, vec, st, y_out, grad)
    feed_grads(dresid, w, down, st, send)


def attend_backward(grad, w, vec, st, send, scratch):
    kt, dqt = scratch[:2]
    rows, width = grad.shape
    size = width // HEADS
    dresid = norm_backward(grad, vec, st)
    dbranch = dresid.astype(BF16)
    st.gwide[:, 3 * width :] = dbranch
    dctx = dot_nt(dbranch, w[:, 3 * width :]).astype(BF16)
    q, v = st.wide[:, :width], st.wide[:, 2 * width : 3 * width]
    kt[...] = (st.wide[:, width : 2 * width] * jnp.asarray(size**-0.5, BF16)).T
    lane = lax.broadcasted_iota(jnp.int32, (rows, 2 * size), 1)
    none = jnp.zeros((rows, 2 * size), BF16)

    def own(value, head):
        first = (head // 2) * 2 * size
        mine = (lane >= size) if head % 2 else (lane < size)
        return jnp.where(mine, value[:, first : first + 2 * size], none)

    def probs_grad(head):
        first = (head // 2) * 2 * size
        return dot_nt(own(v, head), dctx[:, first : first + 2 * size])

    ahead = probs_grad(0)
    for head in range(HEADS):
        dprobs = ahead
        if head + 1 < HEADS:
            ahead = probs_grad(head + 1)
        probs_low = st.aux[:, head * rows : (head + 1) * rows]
        probs = probs_low.astype(F32)
        inner = jnp.sum(probs * dprobs, axis=0, keepdims=True)
        dscores = (probs * (dprobs - inner)).astype(BF16)
        dv_part = dot_nn(probs_low, own(dctx, head))
        dk_part = dot_nn(dscores, own(q, head))
        dqt[head * size : (head + 1) * size, :] = dot_nn(
            kt[head * size : (head + 1) * size, :], dscores
        ).astype(BF16)
        if head % 2 == 0:
            dv, dk = dv_part, dk_part
        else:
            at = width + (head // 2) * 2 * size
            st.gwide[:, at : at + 2 * size] = (dk + dk_part).astype(BF16)
            st.gwide[:, width + at : width + at + 2 * size] = (dv + dv_part).astype(BF16)
    dx = dresid + dot_nt(st.gwide[:, width : 3 * width], w[:, width : 3 * width])
    st.gwide[:, :width] = dqt[...].T
    send[...] = (dx + dot_nt(st.gwide[:, :width], w[:, :width])).astype(BF16)


def roles_of(slot, segments):
    last = segments - 1
    found = []
    for z in range(segments):
        j = slot - 2 * z
        if 0 <= j < segments:
            found.append((z, "both" if z == last else "forward", j))
        j = slot - (4 * last - 2 * z)
        if z < last and 0 <= j < segments:
            found.append((z, "backward", j))
    return found


def half_rows(meta, own, width):
    bit = lax.rem(meta[1], 2)
    bit = bit if own else 1 - bit
    return pl.multiple_of(bit * (width // 2), width // 2)


def weight_refs(lengths, kept):
    acts, wide, _, _, _, grad_wide, grad_branch, sums = kept[:8]
    return [lengths, acts, wide, grad_wide, grad_branch, sums]


def load_turned(at, source, lanes):
    rows = source.shape[1]
    for j in range(source.shape[0]):
        at[: lanes.size, j * rows : (j + 1) * rows] = source[j, :, lanes].T


def main_products(meta, refs, at, own, feed, sentences):
    _, acts, wide, grad_wide = refs[:4]
    rows, width = acts.shape[1:]
    half, full = width // 2, wide.shape[2]
    total = (sentences.stop - sentences.start) * rows
    start = half_rows(meta, own, width)
    at[half:, :total] = jnp.ones((at.shape[0] - half, total), BF16)
    load_turned(at, acts.at[sentences], pl.ds(start, half))
    for c in range(full // width):
        cols = slice(c * width, (c + 1) * width)
        if c == 3 and not feed:
            lanes = pl.ds(pl.multiple_of(3 * width + start, half), half)
            load_turned(at, wide.at[sentences], lanes)
        yield c, cols, dot_nn(at[:, :total], grad_wide[sentences, :, cols].reshape(total, width))


def side_products(meta, refs, at, own, sentences):
    wide, _, grad_branch = refs[2:5]
    rows, width = grad_branch.shape[1:]
    half, full = width // 2, wide.shape[2]
    total = (sentences.stop - sentences.start) * rows
    load_turned(at, grad_branch.at[sentences], pl.ds(half_rows(meta, own, width), half))
    for c in range(full // width):
        cols = slice(c * width, (c + 1) * width)
        yield c, cols, dot_nn(at[:half, :total], wide[sentences, :, cols].reshape(total, width))


def early_sums(feed, stop):
    def body(meta, ins, outs, kept, scratch):
        lengths = ins[0]
        refs = weight_refs(lengths, kept)
        for own in range(2):
            for _, cols, grad in main_products(meta, refs, scratch[0], bool(own), feed, slice(0, stop)):
                outs[0][own, :, cols] = grad
            if feed:
                for _, cols, grad in side_products(meta, refs, scratch[0], bool(own), slice(0, stop)):
                    outs[1][own, :, cols] = grad

    return body


def main_half(own, feed, first=0, early=None):
    def body(meta, refs, out, scratch):
        lengths, acts, wide, _, grad_branch, sums = refs
        at, sm = scratch
        count, rows, width = acts.shape
        half, full = width // 2, wide.shape[2]
        sm[...] = jnp.zeros_like(sm)
        sm[:SMALLS, :] = sums[...]
        tokens = jnp.sum(lengths[:, 0:1].astype(F32), axis=0, keepdims=True)
        sm[COUNT : COUNT + 1, :] = jnp.broadcast_to(tokens, (1, width))
        for c, cols, grad in main_products(meta, refs, at, own, feed, slice(first, count)):
            if early is not None:
                grad = grad + early[int(own), :, cols]
            out[:, cols] = grad[:half].astype(BF16)
            place = BIAS + (3, 0, 1, 2)[c] if feed else (BIAS, None, BIAS + 1, OUT_BIAS)[c]
            if place is not None:
                sm[place : place + 1, :] = grad[half : half + 1]
        if feed:
            sm[OUT_BIAS : OUT_BIAS + 1, :] = jnp.sum(
                grad_branch[...].reshape(count * rows, width).astype(F32), axis=0, keepdims=True
            )
        out[:, full:] = sm[:, pl.ds(half_rows(meta, own, width), half)].T.astype(BF16)

    return body


def side_half(own, first, early):
    def body(meta, refs, out, scratch):
        wide, grad_wide, grad_branch = refs[2:5]
        at, sm = scratch
        count, rows, width = grad_branch.shape
        half, full, total = width // 2, wide.shape[2], count * rows
        sm[...] = jnp.broadcast_to(
            jnp.sum(
                grad_wide[:, :, :width].reshape(total, width).astype(F32), axis=0, keepdims=True
            ),
            sm.shape,
        )
        mine = pl.ds(half_rows(meta, own, width), half)
        out[:, full // 2 : full // 2 + LANES] = sm[:, mine].T.astype(BF16)
        for c, cols, grad in side_products(meta, refs, at, own, slice(first, count)):
            put = c * width + (LANES if c * width >= full // 2 else 0)
            out[:, put : put + width] = (grad + early[int(own), :, cols]).astype(BF16)

    return body


def core_add(masks):
    def body(meta, ins, outs, kept, scratch):
        size = outs[0].shape[0]
        chip = lax.div(meta[1], 2)
        for mask, out in zip(masks, outs, strict=True):
            rows = pl.ds(pl.multiple_of(jnp.bitwise_xor(chip, mask // 2) * size, size), size)
            at = 0
            for keep, got in zip(ins[0::2], ins[1::2], strict=True):
                cols = slice(at, at + keep.shape[1])
                at += keep.shape[1]
                out[:, cols] = (keep[rows, :].astype(F32) + got[rows, :].astype(F32)).astype(BF16)

    return body


def summed(refs, cols):
    total = refs[0][:, cols].astype(F32)
    for r in refs[1:]:
        total = total + r[:, cols].astype(F32)
    return total.astype(BF16)


def chip_sum(meta, ins, outs, kept, scratch):
    at = 0
    for out in outs or kept:
        out[...] = summed(ins, slice(at, at + out.shape[1]))
        at += out.shape[1]


def added(one, two, rows):
    return (one[rows, :].astype(F32) + two[rows, :].astype(F32)).astype(BF16)


def first_cut(meta, ins, outs, kept, scratch):
    keep, got = ins
    upper_stay, upper_go, lower_stay, lower_go = outs
    size = upper_stay.shape[0]
    half = size // 2
    chip = lax.div(meta[1], 2)
    x, y = lax.rem(chip, 2), lax.div(chip, 2)
    for other in range(2):
        put = slice(other * half, (other + 1) * half)
        for out, q, low in (
            (upper_go, 2 * other + 1 - x, 0),
            (lower_go, 2 * (1 - y) + other, half),
            (upper_stay, 2 * other + x, 0),
            (lower_stay, 2 * y + other, half),
        ):
            out[put, :] = added(keep, got, pl.ds(pl.multiple_of(q * size + low, half), half))


def second_cut(meta, ins, outs, kept, scratch):
    upper, upper_got, lower, lower_got = ins
    half = outs[0].shape[0]
    chip = lax.div(meta[1], 2)
    x, y = lax.rem(chip, 2), lax.div(chip, 2)
    for one, two, bit, stay, go in (
        (upper, upper_got, y, outs[0], outs[1]),
        (lower, lower_got, x, outs[2], outs[3]),
    ):
        go[...] = added(one, two, pl.ds(pl.multiple_of((1 - bit) * half, half), half))
        stay[...] = added(one, two, pl.ds(pl.multiple_of(bit * half, half), half))


def cut_sum(meta, ins, outs, kept, scratch):
    half = ins[0].shape[0]
    for i in range(2):
        at = 0
        for out in outs:
            cols = slice(at, at + out.shape[1])
            out[i * half : (i + 1) * half, :] = summed(ins[2 * i : 2 * i + 2], cols)
            at += out.shape[1]


def cross_message(meta, ins, outs, kept, scratch):
    low, grad = ins
    (out,) = outs
    size, width = low.shape[0], out.shape[1]

    @pl.when(lax.rem(meta[0], 2) == 1)
    def _():
        for i in range(0, low.shape[1], width):
            cols = min(width, low.shape[1] - i)
            out[i // width * size : (i // width + 1) * size, :cols] = low[:, i : i + cols]

    @pl.when(meta[0] == 0)
    def _():
        out[...] = grad[...]


def side_share(meta, ins, outs, kept, scratch):
    high, message = ins
    (out,) = outs
    half = high.shape[1]

    @pl.when(lax.rem(meta[0], 2) == 1)
    def _():
        out[:, :half] = high[...]
        out[:, half:] = jnp.zeros((out.shape[0], out.shape[1] - half), BF16)

    @pl.when(lax.rem(meta[0], 2) == 0)
    def _():
        size, width = out.shape[0], message.shape[1]
        for i in range(0, out.shape[1], width):
            cols = min(width, out.shape[1] - i)
            out[:, i : i + cols] = message[i // width * size : (i // width + 1) * size, :cols]


def block_row(meta, mask, width, size):
    chip, core = lax.div(meta[1], 2), lax.rem(meta[1], 2)
    side = jnp.bitwise_xor(core, mask % 2)
    at = side * (width // 2) + jnp.bitwise_xor(chip, mask // 2) * size
    return pl.multiple_of(at, size)


def load_lent(side, in_bias, share, sems, first, meta):
    width, block = side.shape[0], share.shape[0] - 16
    rows = pl.ds(half_rows(meta, True, width), block)
    copy = pltpu.make_async_copy(side.at[rows], share.at[:block], sems.at[first])
    copy.start()
    share[block:, width:] = jnp.zeros((16, share.shape[1] - width), BF16)
    share[block:, :width] = jnp.broadcast_to(in_bias[:, 2 * width :], (16, width))
    return copy


def begin_sending(meta, ins, outs, kept, scratch):
    side, in_bias, tokens = ins
    share, bias_v, tokens_v = outs
    sems = scratch[-1]
    copies = [
        pltpu.make_async_copy(in_bias, bias_v, sems.at[0]),
        pltpu.make_async_copy(tokens, tokens_v, sems.at[1]),
    ]
    for c in copies:
        c.start()
    copies[0].wait()
    load_lent(side, bias_v, share, sems, 2, meta).wait()
    copies[1].wait()


def begin(meta, ins, outs, kept, scratch):
    lens, side, bias_v, *rest = ins
    again, zero_sums, lens_v, *outs = outs
    sems = scratch[-1]
    copies = [
        pltpu.make_async_copy(src, dst, sems.at[i])
        for i, (src, dst) in enumerate(zip(rest, outs[: len(rest)], strict=True))
    ]
    for c in copies:
        c.start()
    copies.append(load_lent(side, bias_v, again, sems, len(rest), meta))
    zero_sums[...] = jnp.zeros_like(zero_sums)
    for j in range(lens_v.shape[0]):
        lens_v[j : j + 1, :] = jnp.full((1, LANES), lens[j], jnp.int32)
    for c in copies:
        c.wait()


def join_down(meta, ins, outs, kept, scratch):
    lent, other, side = ins
    down, low_bias = kept
    width, half = side.shape
    block = width // 2
    copy = pltpu.make_async_copy(side, down.at[:, half:], scratch[-1].at[0])
    copy.start()
    down[pl.ds(half_rows(meta, True, width), block), :half] = lent[:block]
    down[pl.ds(half_rows(meta, False, width), block), :half] = other[:block]
    low_bias[...] = lent[block:, :width]
    copy.wait()


class Results:
    def __init__(self, sems):
        self.sems, self.copies = sems, []

    def out(self, src, dst):
        self.picked([src], dst, None)

    def picked(self, refs, dst, which):
        sem = self.sems.at[len(self.copies)]
        for j, r in enumerate(refs):
            start = pltpu.make_async_copy(r, dst, sem).start
            start() if which is None else pl.when(which == j)(start)
        self.copies.append(pltpu.make_async_copy(refs[0], dst, sem))

    def finish(self):
        for c in self.copies:
            c.wait()


def widen_main(masks, segments):
    def body(meta, ins, outs, kept, scratch):
        n = len(masks)
        blocks, finals, backs = ins[:n], ins[n : n + segments], ins[n + segments :]
        out_y, out_g, main_h, out_b, gain_h, shift_h, stats_h, small_v = outs
        full, cols, stat, sems = scratch
        res = Results(sems)
        res.picked(finals, out_y, meta[0])
        res.picked(backs, out_g, meta[0])
        width, main = main_h.shape[1], main_h.shape[2]
        size = blocks[0].shape[0]
        for i, mask in enumerate(masks):
            at = block_row(meta, mask, width, size)
            cols[pl.ds(at, size), :] = blocks[i][:, main:]
            full[i] = blocks[i][:, :main].astype(F32)
            res.out(full.at[i], main_h.at[0, pl.ds(at, size)])
        small = cols[...].T.astype(F32)
        small_v[...] = small[: small_v.shape[0]]
        squares = jnp.sum(small[RESID_SQ : BRANCH_SQ + 1], axis=1, keepdims=True)
        values = jnp.sqrt(squares / (small[COUNT : COUNT + 1, 0:1] * width))
        lane = lax.broadcasted_iota(jnp.int32, (1, LANES), 1)
        stat[...] = jnp.where(lane == 0, values[0:1], values[1:2])
        res.out(small_v.at[OUT_BIAS : OUT_BIAS + 1], out_b)
        res.out(small_v.at[GAIN : GAIN + 1], gain_h)
        res.out(small_v.at[SHIFT : SHIFT + 1], shift_h)
        res.out(stat, stats_h)
        res.finish()

    return body


def widen_side(masks):
    def body(meta, ins, outs, kept, scratch):
        *blocks, small = ins
        side_h, in_b = outs
        full, cols, vecs, sems = scratch
        res = Results(sems)
        width, half = side_h.shape[1], side_h.shape[2]
        size = blocks[0].shape[0]
        for i, mask in enumerate(masks):
            at = block_row(meta, mask, width, size)
            cols[pl.ds(at, size), :] = blocks[i][:, half:]
            full[i] = blocks[i][:, :half].astype(F32)
            res.out(full.at[i], side_h.at[0, pl.ds(at, size)])
        lent = cols[...].T.astype(F32)[0:1]
        feed = jnp.full((1, width), lax.rem(meta[0], 2), jnp.int32) == 1
        vecs[0:1, :width] = small[BIAS : BIAS + 1]
        vecs[0:1, width : 2 * width] = small[BIAS + 1 : BIAS + 2]
        vecs[0:1, 2 * width :] = jnp.where(feed, small[BIAS + 2 : BIAS + 3], lent)
        res.out(vecs.at[0:1], in_b)
        res.finish()

    return body


def on_device(
    tokens, lengths, cotangent, main_weight, side_weight, in_bias, out_bias, norm_gain, norm_shift
):
    segments, shards = lax.axis_size("segment"), lax.axis_size("dp")
    z, d = lax.axis_index("segment"), lax.axis_index("dp")
    rows, width = tokens.shape
    main_mat, side_mat = main_weight[0], side_weight[0]
    hidden = main_mat.shape[1]
    half_width = side_mat.shape[1]
    block = width // shards
    last = segments - 1
    feeds = tuple(range(1, segments, 2))
    chip_masks = tuple(range(0, shards, 2))
    masks = chip_masks + tuple(m + 1 for m in chip_masks)
    meta = (z.reshape(1), d.reshape(1))

    def hop(value, *pairs):
        return lax.ppermute(value, "segment", list(pairs))

    def swap(value, mask):
        return lax.ppermute(value, "dp", [(i, i ^ mask) for i in range(shards)])

    ext = hidden + LANES
    low_ext = half_width + LANES
    kept_shapes = [
        ((segments, rows, width), BF16),
        ((segments, rows, hidden), BF16),
        ((segments, rows, hidden), BF16),
        ((segments, rows, width), F32),
        ((segments, rows, LANES), F32),
        ((segments, rows, hidden), BF16),
        ((segments, rows, width), BF16),
        ((2, rows, width), BF16),
    ]
    lent = ((width // 2 + 16, half_width), BF16)
    borrowed_shapes = [((width, hidden), BF16), ((16, width), BF16)]
    narrow = ((rows, width), BF16)
    (share, bias_v, tokens_v), _ = kernel_call(
        begin_sending, meta, [side_mat, in_bias, tokens], [lent, (in_bias.shape, BF16), narrow],
        copies=3, hbm_ins=(0, 1, 2),
    )
    loads = [out_bias, norm_gain, norm_shift, main_mat, cotangent, cotangent]
    loaded, _ = kernel_call(
        begin, meta, [lengths.reshape(segments), side_mat, bias_v, *loads],
        [lent, ((SMALLS, width), F32), ((segments, LANES), jnp.int32)]
        + [(x.shape, x.dtype) for x in loads]
        + kept_shapes + borrowed_shapes,
        copies=1 + len(loads), smem_ins=(0,), hbm_ins=(1, *range(3, 3 + len(loads))), flops=SLOT_FLOPS,
    )
    later_share, sums, lengths_v, *loaded = loaded
    out_bias_v, gain_v, shift_v, main_v, cotangent_v, later_cotangent, *kept = loaded
    *kept, saved, down, low_bias = kept
    kept, borrowed = (*kept, sums, saved), (down, low_bias)

    turns = tuple(range(last, -1, -1))
    first_share = hop(share, (0, 1))
    first_in = [hop(tokens_v, (home, 0)) for home in turns[:2]]
    riders = {
        0: [(turns[2], 0, "tokens"), (turns[1], last, "cotangent")],
        1: [(turns[2], last, "cotangent")],
    }

    def join(s, share, other, blank):
        return kernel_call(
            join_down, meta, [share, other, side_mat], [], kept=blank, hbm_ins=(2,), copies=1, where=(s,)
        )[1]

    turned = ((width, rows), BF16)
    n_chip = len(chip_masks)
    weight_scratch = [((width // 2 + 16, segments * rows), BF16), ((LANES, width), F32)]

    slots = 4 * last + segments
    waves, sent, finals = {}, {}, []
    after, last_in = {}, []
    side, main = [], []
    half_out = ((width // 2, ext), BF16)

    def hops_after(slot):
        pairs = []
        for z_role, what, j in roles_of(slot, segments):
            if what == "forward":
                pairs.append((z_role, z_role + 1))
            elif z_role > 0:
                pairs.append((z_role, z_role - 1))
            elif turns[j] > 0:
                pairs.append((z_role, turns[j]))
        return pairs + [(source, to) for source, to, _ in riders.get(slot, ())]

    homeward = {}
    for slot in range(2 * last + segments + 2, slots):
        taken = [to for _, to in hops_after(slot)]
        free = [home for home in range(1, last) if home not in taken and home not in homeward.values()]
        if free:
            homeward[slot] = free[-1]
    for slot in range(slots):
        roles = roles_of(slot, segments)
        uses = [r[1] for r in roles]
        attends = any(r[0] % 2 == 0 for r in roles)
        feed_roles = any(r[0] % 2 == 1 for r in roles)
        names, ins = [], []

        def give(name, value):
            names.append(name)
            ins.append(value)

        for name, value in zip(
            ("main", "in_bias", "out_bias", "gain", "shift", "lengths"),
            (main_v, bias_v, out_bias_v, gain_v, shift_v, lengths_v),
        ):
            give(name, value)
        if feed_roles and slot != last + 2:
            give("down", down)
            give("low_bias", low_bias)
        if slot < 2:
            give("first", first_in[slot])
            give("cotangent", cotangent_v)
        if slot in (0, last):
            give("tokens", tokens_v)
        if slot - 2 in waves:
            give("wave", waves[slot - 2])
        if "both" in uses and slot - 2 * last in (0, last):
            give("last", last_in[slot - 2 * last])
        if slot in homeward:
            give("home", finals[turns.index(homeward[slot])])
        outs = [narrow] + ([narrow] if "both" in uses else [])
        weighing = slots - 2 <= slot
        if weighing:
            give("early_side", early_side)
            give("early_main", early_main)
            outs += [half_out] * (4 if slot == slots - 2 else 0)

        def body(
            meta, in_refs, out_refs, kept_refs, scratch, slot=slot, roles=roles, names=tuple(names)
        ):
            ref = dict(zip(names, in_refs))
            if slot == last + 2:
                ref["down"], ref["low_bias"] = kept_refs[-2:]
            vec = Vectors(
                ref["in_bias"], ref["out_bias"], ref["gain"], ref["shift"], ref.get("low_bias")
            )
            for z_role, what, j in roles:

                @pl.when(meta[0] == z_role)
                def _(z_role=z_role, what=what, j=j):
                    st = Store(kept_refs, j)
                    seq_len = ref["lengths"][turns[j] : turns[j] + 1, 0:1]
                    w, send = ref["main"], out_refs[0]
                    if what == "backward":
                        if z_role % 2:
                            feed_backward(ref["wave"][...], w, ref["down"], vec, st, send)
                        else:
                            attend_backward(ref["wave"][...], w, vec, st, send, scratch)
                        return
                    own = slot == last and z_role == 0
                    inputs = ref["tokens" if own else "first" if "first" in ref else "wave"][...]
                    if what == "both":
                        feed_both(
                            inputs, ref["last"][...] if "last" in ref else kept_refs[8][j - 1], w, ref["down"], vec, seq_len, st, out_refs[1], send
                        )
                    elif z_role % 2:
                        feed_forward(inputs, w, ref["down"], vec, seq_len, st, send)
                    else:
                        attend_forward(inputs, w, vec, seq_len, st, send, scratch)

            for source, _, what in riders.get(slot, ()):

                @pl.when(meta[0] == source)
                def _(what=what):
                    out_refs[0][...] = ref[what][...]

            if slot in (2, 3):

                @pl.when(meta[0] == last)
                def _():
                    kept_refs[8][slot - 2] = ref["wave"][...]

            if "home" in ref:

                @pl.when(meta[0] == last)
                def _():
                    out_refs[0][...] = ref["home"][...]

            if weighing:
                sums = weight_refs(ref["lengths"], kept_refs)
                first = slot == slots - 2
                sides, mains = (out_refs[-4:-2], out_refs[-2:]) if first else ((), kept_refs[-2:])
                feed_here = lax.rem(meta[0], 2) == 1

                @pl.when(feed_here)
                def _():
                    for own in range(2):
                        if first:
                            side_half(bool(own), FEED_EARLY, ref["early_side"])(
                                meta, sums, sides[own], scratch[-2:]
                            )
                        else:
                            main_half(bool(own), True, FEED_EARLY, ref["early_main"])(
                                meta, sums, mains[own], scratch[-2:]
                            )

                if first:

                    @pl.when(jnp.logical_not(feed_here) & (meta[0] > 0))
                    def _():
                        for own in range(2):
                            main_half(bool(own), False)(meta, sums, mains[own], scratch[-2:])

        scratch = [turned, turned, narrow] if attends else []
        if weighing:
            scratch = scratch + weight_scratch
        extra = ()
        if slot in (1, last + 1):
            extra = (later_share,)
        elif slot == last + 2:
            extra = (down, low_bias)
        elif slot == slots - 1:
            extra = (*main,)
        res, kept = kernel_call(
            body, meta, ins, outs, scratch, (*kept, *extra), after=after.get(slot, ()), flops=SLOT_FLOPS
        )
        if slot == 2:
            last_in += [cotangent_v, None, None]
        if slot == 2 * last:
            _, (*kept, later_cotangent) = kernel_call(
                lambda *_: None, meta, [], [], kept=(*kept, later_cotangent), after=[waves[slot - 1]]
            )
            last_in.append(hop(later_cotangent, (0, last)))
        if slot == slots - 1:
            *kept, main[0], main[1] = kept
        if slot == 0:
            _, (*kept, first_share) = kernel_call(lambda *_: None, meta, [], [], kept=(*kept, first_share))
            down, low_bias = join(1, first_share, swap(first_share, 1), borrowed)
        if slot == 1:
            *kept, later_share = kept
            later_share = hop(later_share, (last - 1, last))
        if slot == last + 1:
            *kept, later_share = kept
            later_half = swap(later_share, 1)
        if slot == last + 2:
            *kept, down, low_bias = kept
            down, low_bias = join(last, later_share, later_half, (down, low_bias))
        sent[slot] = res[0]
        if slot == slots - segments - 1:
            early_shapes = [((2, width // 2 + extra_rows, hidden), F32) for extra_rows in (16, 0)]
            (early_main, early_side), kept = kernel_call(
                early_sums(True, FEED_EARLY), meta, [lengths_v], early_shapes, weight_scratch, kept, where=feeds
            )
        if slot == slots - 2:
            side, main = list(res[-4:-2]), list(res[-2:])

            def early_attend(meta, ins, outs, kept, scratch):
                early_sums(False, ATTEND_EARLY)(meta, ins, kept[-1:], kept, scratch)

            _, (*kept, early_main) = kernel_call(
                early_attend, meta, [lengths_v], [], weight_scratch, (*kept, early_main), where=(0,)
            )
        if "both" in uses:
            finals.append(res[1])
        pairs = hops_after(slot)
        if slot in homeward:
            pairs.append((last, homeward[slot]))
        if pairs and slot != slots - 2:
            waves[slot] = hop(res[0], *pairs)
    def weigh(own, after):
        def body(meta, ins, outs, kept, scratch):
            main_half(bool(own), False, ATTEND_EARLY, ins[-1])(meta, ins[:-1], kept[0], scratch)

        _, (main[own],) = kernel_call(
            body, meta, [*weight_refs(lengths_v, kept), early_main], [], weight_scratch,
            (main[own],), where=(0,), after=after,
        )

    def add_cores(keep, got, segs, after=()):
        blocks, _ = kernel_call(
            core_add(chip_masks), meta, [keep, got], [((block, keep.shape[1]), BF16)] * n_chip,
            where=segs, after=after,
        )
        return [blocks[0]] + [swap(blocks[i], chip_masks[i]) for i in range(n_chip - 1, 0, -1)]

    def add_in_steps(keep, got, segs, after=()):
        rows_of = (keep.shape[0] // 4, keep.shape[1])
        (up, up_go, down, down_go), _ = kernel_call(
            first_cut, meta, [keep, got], [(rows_of, BF16)] * 4, where=segs, after=after
        )
        rows_of = (rows_of[0] // 2, rows_of[1])
        (up, up_go, down, down_go), _ = kernel_call(
            second_cut, meta, [up, swap(up_go, 2), down, swap(down_go, 4)],
            [(rows_of, BF16)] * 4, where=segs,
        )
        return [up, swap(up_go, 4), down, swap(down_go, 2)]

    reduce, last_sum = (add_in_steps, cut_sum) if n_chip == 4 else (add_cores, chip_sum)
    side_got = swap(side[0], 1)
    weigh(0, [side_got])
    main_got = swap(main[0], 1)
    side_blocks = reduce(side[1], side_got, feeds, [main[0]])
    weigh(1, [side_blocks[0]] if n_chip != 4 else [])
    main_blocks = reduce(main[1], main_got, None)
    (low_own, high_own), _ = kernel_call(
        last_sum, meta, side_blocks, [((block, low_ext), BF16), ((block, half_width), BF16)], where=feeds,
        after=main_blocks[:1],
    )
    (total,), _ = kernel_call(last_sum, meta, main_blocks, [((block, ext), BF16)])
    (message,), _ = kernel_call(cross_message, meta, [low_own, sent[slots - 2]], [narrow])
    waves[slots - 2] = hop(message, *[(s, s - 1) for s in feeds], (0, turns[-2]))
    first_home = hop(finals[turns.index(0)], (last, 0))
    outputs_at = [first_home] + [
        waves[next(k for k, v in homeward.items() if v == s)] for s in range(1, last)
    ]
    outputs_at.append(finals[turns.index(last)])
    start = slots - segments
    grads_at = [sent[slots - 1]] + [waves[start + turns.index(s)] for s in range(1, segments)]

    def gather(share):
        blocks = [share] + [swap(share, m) for m in reversed(chip_masks[1:])]
        blocks = [blocks[0], *reversed(blocks[1:])]
        return blocks + [swap(b, 1) for b in blocks]

    main_all = gather(total)
    (side_mine,), _ = kernel_call(
        side_share, meta, [high_own, waves[slots - 2]], [((block, low_ext), BF16)],
        after=[main_all[2]],
    )
    (out_y, out_g, main_grad, out_bias_grad, gain_grad, shift_grad, stats, small), _ = kernel_call(
        widen_main(masks, segments), meta, [*main_all, *outputs_at, *grads_at],
        [narrow, narrow, ((1, width, hidden), F32)]
        + [((1, width), F32)] * 3
        + [((1, LANES), F32), ((SMALLS, width), F32)],
        [((shards, block, hidden), F32), ((width, LANES), BF16), ((1, LANES), F32)],
        copies=shards + 6, hbm_outs=tuple(range(7)),
    )
    (side_grad, in_bias_grad), _ = kernel_call(
        widen_side(masks), meta, [*gather(side_mine), small],
        [((1, width, half_width), F32), ((1, 3 * width), F32)],
        [((shards, block, half_width), F32), ((width, LANES), BF16), ((8, 3 * width), F32)],
        copies=shards + 1, hbm_outs=(0, 1),
    )
    return (
        out_y, out_g, main_grad, side_grad, in_bias_grad, out_bias_grad, gain_grad, shift_grad, stats[:, :2]
    )


def solution(mesh):
    over = P(("segment", "dp"), None)
    by_segment = [P("segment", None, None)] * 2 + [P("segment", None)] * 4
    in_specs = (over, P(None, "dp"), over, *by_segment)
    out_specs = (over, over, *by_segment, P("segment", None))
    return jax.shard_map(
        on_device, mesh=mesh, in_specs=in_specs, out_specs=out_specs, check_vma=False
    )
```
